256 devices in a mesh: ctx: 32 (over z_hi, y, x), head: 8 (over z_lo, core).
Axes of the slice: x: 4, y: 4, z: 8 (z_hi: 2, z_lo: 4; z = z_hi * 4 + z_lo), core: 2. Of those that a mesh axis runs over, the one named last changes fastest.
Arguments:
- queries: bfloat16 [1024, 8192], P('ctx', 'head'), may hold values from -48 to 48
- cache_keys: bfloat16 [65536, 1024], P('ctx', 'head'), may hold values from -6 to 6
- cache_values: bfloat16 [65536, 1024], P('ctx', 'head'), may hold values from -6 to 6
- span_keys: bfloat16 [1024, 1024], P('ctx', 'head'), may hold values from -6 to 6
- span_values: bfloat16 [1024, 1024], P('ctx', 'head'), may hold values from -6 to 6
- prefix_len: int32 [32], P('ctx'), may hold values from 1 to 2048, 40960 in all
- positions: int32 [1024], P('ctx'), may hold values from 0 to 1023, each once
- out_weight: bfloat16 [8192, 8192], P('head', 'ctx'), may hold values from -0.0625 to 0.0625
Outputs:
- projected: bfloat16 [1024, 8192], P('head', 'ctx')
The draws below stay inside these ranges and needn't reach their ends.
Inputs may be any that keep to these rules, and one draw needn't show every extreme that they name: Each shard's prefix occupies the first prefix_len of its 2048 slots; some shard is full. `positions`: a permutation of 0 to 1023.
All inputs are finite; a program needn't handle non-finite values.
Results may differ from the reference program's by a relative error of at most 0.02.
Values may be sent and summed in bfloat16 or wider, within the bound.
No kernel may reach another device: no remote copies, remote signals or barrier semaphores. Data moves between devices by JAX's collectives and lax.ppermute only.
A program may use at most 320 MiB of HBM per device.

```python
import math
import jax
import jax.numpy as jnp
import numpy as np
from jax import lax

D = 8192
HD = 128
GROUP = 8
SPAN = 1024
CACHE_DEV = 2048
KVH = 8
HQ = 64
CACHE_TOTAL = 65536
N_CTX = 32


def shared_keys(key, blend):
    first = jax.random.fold_in(key, 0)
    third = jax.random.fold_in(key, 2)
    shape = (CACHE_TOTAL, KVH * HD)
    normal_part = jnp.clip(jax.random.normal(first, shape, jnp.float32), -6.0, 6.0)
    field = normal_part
    nudge = jax.random.normal(third, shape, jnp.float32) * 0.15
    slot_rows = jnp.arange(CACHE_TOTAL, dtype=jnp.int32)
    paired = (slot_rows % (CACHE_TOTAL // 16) == 1)[:, None] & (blend > 0.5)
    shifted = jnp.clip(jnp.roll(field, 1, axis=0) + nudge, -6.0, 6.0)
    return jnp.where(paired, shifted, field)


def draw_cache_keys(key, part):
    field = shared_keys(key, 0.0)
    return field.astype(jnp.bfloat16)


def draw_queries(key, part):
    key = jax.random.fold_in(key, 11)
    base = jnp.clip(jax.random.normal(key, (SPAN, HQ * HD), jnp.float32), -4.0, 4.0) * 3.0
    return base.astype(jnp.bfloat16)


def levels(own_key, dims, shards, least, top_value):
    def one(dim, blocks):
        steps = jax.random.uniform(jax.random.fold_in(jax.random.fold_in(own_key, 6), dim), (blocks,), jnp.float32, least / len(shards), top_value / len(shards))
        return jnp.repeat(jnp.exp(steps), dims[dim] // blocks).reshape((-1,) + (1,) * (len(dims) - dim - 1))

    factor_of = one(*shards[0])
    for cut in shards[1:]:
        factor_of = factor_of * one(*cut)
    return factor_of


def split_up(amount, total, bound, lean):
    loads = [(1 << 20) // math.isqrt(grade ** lean) + 1 for grade in range(2, amount + 1)]
    spare, given = total - bound - (amount - 1), [1] * (amount - 1)
    while spare > 0:
        candidates = [i for i in range(amount - 1) if given[i] < bound]
        mass, remaining = sum([loads[i] for i in candidates]), spare
        for i in candidates:
            extra = min(bound - given[i], max(1, remaining * loads[i] // mass), spare)
            given[i] = given[i] + extra
            spare = spare - extra
    return np.array([bound] + given)


def uneven_parts(rng, count, total, limit, slope):
    if count == 2:
        one = jax.random.randint(rng, (), max(1, total - limit), min(limit, total - 1) + 1)
        return jnp.stack([one, total - one])
    sizes = jnp.asarray(split_up(count, total, limit, slope), jnp.int32)
    twos = (count - 1) // 2
    source_of, sink = sizes[1:1 + 2 * twos:2], sizes[2:2 + 2 * twos:2]
    margin = jnp.minimum(source_of - 1, limit - sink)
    moved = jax.random.randint(jax.random.fold_in(rng, 1), (twos,), 0, 1 << 20) % (margin + 1)
    sizes = sizes.at[1:1 + 2 * twos:2].set(source_of - moved).at[2:2 + 2 * twos:2].set(sink + moved)
    return sizes[jax.random.permutation(jax.random.fold_in(rng, 2), count)]


def centred(key, dims, scale, bound, cuts=(), held_as=jnp.bfloat16):
    array = scale * jax.random.normal(key, dims, jnp.float32)
    if cuts:
        array = array * levels(key, dims, cuts, -0.22, 0.18)
    return jnp.clip(array, -bound, bound).astype(held_as)


def setup_inputs(seed: int = 0) -> dict:
    keys = jax.random.split(jax.random.key(seed), 9)
    return {
        "queries": draw_queries(jax.random.fold_in(keys[8], 71), 0),
        "cache_keys": draw_cache_keys(jax.random.fold_in(keys[8], 71), 0),
        "cache_values": centred(keys[2], (CACHE_TOTAL, KVH * HD), 1.0, 6.0, ((0, 32), (1, 8))),
        "span_keys": centred(keys[3], (SPAN, KVH * HD), 1.0, 6.0, ((0, 32), (1, 8))),
        "span_values": centred(keys[4], (SPAN, KVH * HD), 1.0, 6.0, ((0, 32), (1, 8))),
        "prefix_len": uneven_parts(keys[5], N_CTX, CACHE_TOTAL * 5 // 8, CACHE_DEV, 2).astype(jnp.int32),
        "positions": jax.random.permutation(keys[6], SPAN).astype(jnp.int32),
        "out_weight": centred(keys[7], (HQ * HD, D), (HQ * HD) ** -0.5, 0.0625, ((0, 8), (1, 32))),
    }


def reference(queries, cache_keys, cache_values, span_keys, span_values, prefix_len, positions, out_weight):
    slot_rows = jnp.arange(CACHE_TOTAL, dtype=jnp.int32)
    cache_open = (slot_rows % CACHE_DEV) < prefix_len[slot_rows // CACHE_DEV]
    span_open = positions[None, :] <= positions[:, None]
    visible = jnp.concatenate([jnp.broadcast_to(cache_open[None, :], (SPAN, CACHE_TOTAL)), span_open], axis=1)
    all_keys = jnp.concatenate([cache_keys, span_keys], axis=0)
    all_values = jnp.concatenate([cache_values, span_values], axis=0)
    score_scale = 1.0 / (HD ** 0.5)

    def single_head(head_index):
        group_index = head_index // GROUP
        query_head = lax.dynamic_slice_in_dim(queries, head_index * HD, HD, 1).astype(jnp.float32)
        key_head = lax.dynamic_slice_in_dim(all_keys, group_index * HD, HD, 1).astype(jnp.float32)
        value_head = lax.dynamic_slice_in_dim(all_values, group_index * HD, HD, 1).astype(jnp.float32)
        scores = jnp.dot(query_head, key_head.T, precision=lax.Precision.HIGHEST) * score_scale
        peak = jnp.max(jnp.where(visible, scores, -1e30), axis=1)
        weights = jnp.where(visible, jnp.exp(scores - peak[:, None]), 0.0)
        norm = jnp.sum(weights, axis=1)
        rounded_length = weights.astype(jnp.bfloat16).astype(jnp.float32)
        summed = jnp.dot(rounded_length, value_head, precision=lax.Precision.HIGHEST)
        return summed / norm[:, None]

    per_head = lax.map(single_head, jnp.arange(HQ, dtype=jnp.int32))
    attended = jnp.transpose(per_head, (1, 0, 2)).reshape(SPAN, HQ * HD).astype(jnp.bfloat16)
    return jnp.dot(attended, out_weight, preferred_element_type=jnp.float32).astype(jnp.bfloat16)
```

```python
import functools
import math

import jax
import jax.numpy as jnp
from jax import lax
from jax.experimental import pallas as pl
from jax.experimental.pallas import tpu as pltpu
from jax.sharding import PartitionSpec as P

BF = jnp.bfloat16
F32 = jnp.float32
HD = 128
GROUP = 8
HALF = 1024
META = 80
QW = GROUP * HD + 128
LOG2_SCALE = math.log2(math.e) / math.sqrt(HD)
NEG = -1e30


def call(body, out_shape, args, scratch=(), smem=(), flops=0, nbytes=0, vmem=56 << 20):
    specs = [pl.BlockSpec(memory_space=pltpu.SMEM if i in smem else pltpu.VMEM) for i in range(len(args))]
    return pl.pallas_call(
        body,
        out_shape=out_shape,
        in_specs=specs,
        out_specs=jax.tree.map(lambda _: pl.BlockSpec(memory_space=pltpu.VMEM), out_shape),
        scratch_shapes=list(scratch),
        cost_estimate=pl.CostEstimate(flops=flops, bytes_accessed=nbytes, transcendentals=0),
        compiler_params=pltpu.CompilerParams(vmem_limit_bytes=vmem),
    )(*args)


def sds(*shape, dtype=BF):
    return jax.ShapeDtypeStruct(shape, dtype)


def pack_query(q_ref, pos_ref, out_ref):
    pos = jnp.broadcast_to(pos_ref[...], (32, 32))
    row = lax.broadcasted_iota(jnp.int32, (32, 32), 0)
    col = lax.broadcasted_iota(jnp.int32, (32, 32), 1)
    column = jnp.sum(jnp.where(row == col, pos, 0), axis=1, keepdims=True)
    lane = lax.broadcasted_iota(jnp.int32, (32, 128), 1)
    high, low = column // 32, column % 32
    numbers = jnp.where(lane == 0, high, jnp.where(lane == 1, low, 0))
    out_ref[:, : GROUP * HD] = q_ref[...]
    out_ref[:, GROUP * HD :] = numbers.astype(F32).astype(BF)


def pack_cache(len_ref, k_ref, v_ref, sk_ref, sv_ref, pos_ref, out_ref):
    used = len_ref[0]
    first = k_ref[0:1, :]
    for half in range(2):
        base = half * (2 * HALF + META)
        for block in range(HALF // HD):
            start = half * HALF + block * HD
            row = lax.broadcasted_iota(jnp.int32, (HD, HD), 0) + start
            seen = row < used
            keys = jnp.where(seen, k_ref[start : start + HD, :].astype(F32), first.astype(F32))
            out_ref[base + block * HD : base + (block + 1) * HD, :] = keys.T.astype(BF)
            values = jnp.where(seen, v_ref[start : start + HD, :].astype(F32), 0.0)
            out_ref[base + HALF + block * HD : base + HALF + (block + 1) * HD, :] = values.astype(BF)
    meta = 2 * HALF
    out_ref[meta : meta + 32, :] = sk_ref[...]
    out_ref[meta + 32 : meta + 64, :] = sv_ref[...]
    pos = jnp.concatenate([pos_ref[...], jnp.zeros((1, 96), jnp.int32)], axis=1)
    pos = jnp.broadcast_to(pos, (16, HD))
    row = lax.broadcasted_iota(jnp.int32, (16, HD), 0)
    lane = lax.broadcasted_iota(jnp.int32, (16, HD), 1)
    extent = jnp.where(lane == 0, used // 32, jnp.where(lane == 1, used % 32, 0))
    numbers = jnp.where(row == 0, pos // 32, jnp.where(row == 1, pos % 32, jnp.where(row == 2, extent, 0)))
    out_ref[meta + 64 : meta + 80, :] = numbers.astype(F32).astype(BF)


def attend(n_tiles, layout, span, first, last, *refs):
    refs = list(refs)
    tiles = [refs.pop(0) for _ in range(n_tiles)]
    kvs = [refs.pop(0) for _ in layout]
    metas = [refs.pop(0) for _ in layout]
    spans = [refs.pop(0) for _ in range(4)] if span else []
    if not first:
        acc_in, st_in = refs.pop(0), refs.pop(0)
    if last:
        outs = [refs.pop(0) for _ in range(n_tiles // 2)]
    else:
        acc_out, st_out = refs.pop(0), refs.pop(0)
    kt, v2, score_a, score_b = refs
    rows = 32 * n_tiles
    at = 0
    for kv, meta, pieces in zip(kvs, metas, layout):
        numbers = meta[...].astype(F32)
        used = numbers[2:3, 0:1] * 32.0 + numbers[2:3, 1:2]
        for start, cache_row in pieces:
            for block in range(HALF // HD):
                piece = kv[start + block * HD : start + (block + 1) * HD, :]
                kt[:HD, at + block * HD : at + (block + 1) * HD] = piece
                kt[HD:, at + block * HD : at + (block + 1) * HD] = piece
            v2[at : at + HALF, :HD] = kv[start + HALF : start + 2 * HALF, :]
            index = lax.broadcasted_iota(jnp.int32, (HALF, HD), 0) + cache_row
            v2[at : at + HALF, HD:] = jnp.where(index.astype(F32) < used, 1.0, 0.0).astype(BF)
            at += HALF
    blocks = [(c, 512) for c in range(0, at, 512)]
    if span:
        span_keys = jnp.concatenate([s[0:32, :] for s in spans], axis=0)
        transposed = span_keys.astype(F32).T.astype(BF)
        kt[:HD, at : at + HD] = transposed
        kt[HD:, at : at + HD] = transposed
        for i, s in enumerate(spans):
            v2[at + 32 * i : at + 32 * (i + 1), :HD] = s[32:64, :]
        v2[at : at + HD, HD:] = jnp.ones((HD, HD), BF)
        key_pos = jnp.concatenate(
            [s[64:65, 0:32].astype(F32) * 32.0 + s[65:66, 0:32].astype(F32) for s in spans], axis=1
        )
        numbers = jnp.concatenate([t[:, GROUP * HD :] for t in tiles], axis=0).astype(F32)
        query_pos = numbers[:, 0:1] * 32.0 + numbers[:, 1:2]
        seen = key_pos <= query_pos
        blocks.append((at, HD))
    lane = lax.broadcasted_iota(jnp.int32, (rows, HD), 1)
    st = jnp.zeros((rows, HD), F32) if first else st_in[...]
    new_st = jnp.zeros((rows, HD), F32)
    peak = None
    for head in range(GROUP + 1):
        mine, previous = (score_a, score_b) if head % 2 == 0 else (score_b, score_a)
        cols = slice(head * HD, (head + 1) * HD)
        if head < GROUP:
            query = jnp.concatenate([t[:, cols] for t in tiles], axis=0).astype(F32) * LOG2_SCALE
            high = query.astype(BF)
            low = (query - high.astype(F32)).astype(BF)
            query = jnp.concatenate([high, low], axis=1)
        top = None
        acc = None
        for c, width in blocks:
            if head < GROUP:
                s = jnp.dot(query, kt[:, c : c + width], preferred_element_type=F32)
                if width == HD:
                    s = jnp.where(seen, s, NEG)
                mine[:, c : c + width] = s
                for i in range(0, width, HD):
                    top = s[:, i : i + HD] if top is None else jnp.maximum(top, s[:, i : i + HD])
            if head > 0:
                p = jnp.exp2(previous[:, c : c + width] - peak).astype(BF)
                term = jnp.dot(p, v2[c : c + width, :], preferred_element_type=F32)
                acc = term if acc is None else acc + term
        if head > 0:
            h = head - 1
            cols = slice(h * HD, (h + 1) * HD)
            total, weight = acc[:, :HD], acc[:, HD:]
            if not first:
                rescale = jnp.exp2(st[:, h : h + 1] - peak)
                total = total + acc_in[:, cols] * rescale
                weight = weight + st[:, GROUP + h : GROUP + h + 1] * rescale
            peak_all = jnp.broadcast_to(peak, (rows, HD))
            new_st = jnp.where(lane == h, peak_all, new_st)
            new_st = jnp.where(lane == GROUP + h, weight, new_st)
            if last:
                for i, out in enumerate(outs):
                    out[:, cols] = total[64 * i : 64 * (i + 1), :].astype(BF)
            else:
                acc_out[:, cols] = total
        if head < GROUP:
            peak = jnp.max(top, axis=1, keepdims=True).astype(BF).astype(F32)
            if not first:
                peak = jnp.maximum(peak, st[:, head : head + 1])
    if last:
        high = new_st.astype(BF).astype(F32)
        low = pltpu.roll(new_st - high, GROUP, 1)
        packed = jnp.where(lane < 2 * GROUP, high, jnp.where(lane < 3 * GROUP, low, 0.0)).astype(BF)
        for i, out in enumerate(outs):
            out[:, GROUP * HD :] = packed[64 * i : 64 * (i + 1), :]
    else:
        st_out[...] = new_st


def attend_call(tiles, kvs, metas, layout, spans, carry, last):
    n_keys = HALF * sum(len(p) for p in layout) + (HD if spans else 0)
    rows = 32 * len(tiles)
    first = carry is None
    args = list(tiles) + list(kvs) + list(metas) + list(spans) + ([] if first else list(carry))
    if last:
        out = [sds(64, QW) for _ in range(len(tiles) // 2)]
    else:
        out = [sds(rows, GROUP * HD, dtype=F32), sds(rows, HD, dtype=F32)]
    return call(
        functools.partial(attend, len(tiles), layout, bool(spans), first, last),
        out,
        args,
        scratch=[
            pltpu.VMEM((2 * HD, n_keys), BF),
            pltpu.VMEM((n_keys, 2 * HD), BF),
            pltpu.VMEM((rows, n_keys), F32),
            pltpu.VMEM((rows, n_keys), F32),
        ],
        flops=rows * GROUP * n_keys * HD * 8,
        nbytes=4 << 20,
    )


def join(messages, final):
    stats = [m[:, GROUP * HD :].astype(F32) for m in messages]
    sums, peaks, weights = [], [], []
    for h in range(GROUP):
        each = [s[:, h : h + 1] for s in stats]
        peak = functools.reduce(jnp.maximum, each)
        scales = [jnp.exp2(p - peak) for p in each]
        weight = sum(
            (s[:, GROUP + h : GROUP + h + 1] + s[:, 2 * GROUP + h : 2 * GROUP + h + 1]) * c
            for s, c in zip(stats, scales)
        )
        total = sum(m[:, h * HD : (h + 1) * HD].astype(F32) * c for m, c in zip(messages, scales))
        sums.append(total / weight if final else total)
        peaks.append(peak)
        weights.append(weight)
    return sums, peaks, weights


def join_x(a_ref, b_ref, c_ref, d_ref, out_ref):
    messages = [r[...] for r in (a_ref, b_ref, c_ref, d_ref)]
    sums, peaks, weights = join(messages, False)
    lane = lax.broadcasted_iota(jnp.int32, (64, HD), 1)
    numbers = jnp.zeros((64, HD), F32)
    for h in range(GROUP):
        out_ref[:, h * HD : (h + 1) * HD] = sums[h].astype(BF)
        high = weights[h].astype(BF).astype(F32)
        numbers = jnp.where(lane == h, peaks[h], numbers)
        numbers = jnp.where(lane == GROUP + h, high, numbers)
        numbers = jnp.where(lane == 2 * GROUP + h, weights[h] - high, numbers)
    out_ref[:, GROUP * HD :] = numbers.astype(BF)


def join_z(own_ref, other_ref, out_ref):
    other = jnp.concatenate([other_ref[32:64, :], other_ref[0:32, :]], axis=0)
    sums, _, _ = join([own_ref[...], other], True)
    for h in range(GROUP):
        out_ref[:, h * HD : (h + 1) * HD] = sums[h].astype(BF)


def project(where_ref, a0, a1, a2, a3, w0, w1, w2, w3, keep_ref, send_ref):
    z, y, core = where_ref[0], where_ref[1], where_ref[2]
    rows = jnp.concatenate([a0[...], a1[...], a2[...], a3[...]], axis=0)
    for i, w in enumerate((w0, w1, w2, w3)):
        out = jnp.dot(rows, w[...], preferred_element_type=F32).astype(BF)
        for j, dy in enumerate((0, 1, 3, 2)):
            there = lax.rem(y + dy, 4)
            for part in range(2):
                z_there = z if part == 0 else 1 - z
                slot = pl.multiple_of((z_there * 2 + there // 2) * 32, 32)
                piece = out[64 * j + 32 * part : 64 * j + 32 * (part + 1), :]

                @pl.when(lax.rem(there, 2) == core)
                def _():
                    keep_ref[pl.ds(slot, 32), i * 256 : (i + 1) * 256] = piece

                @pl.when(lax.rem(there, 2) != core)
                def _():
                    send_ref[pl.ds(slot, 32), i * 256 : (i + 1) * 256] = piece


def add_cores(where_ref, keep_ref, got_ref, own_ref, o1, o2, o3):
    z_lo = where_ref[3]
    for k, out in enumerate((own_ref, o1, o2, o3)):
        slot = pl.multiple_of((z_lo ^ k) * 32, 32)
        out[...] = (keep_ref[pl.ds(slot, 32), :].astype(F32) + got_ref[pl.ds(slot, 32), :].astype(F32)).astype(BF)


def add_z(a_ref, b_ref, c_ref, d_ref, o0, o1, o2, o3):
    total = sum(r[...].astype(F32) for r in (a_ref, b_ref, c_ref, d_ref)).astype(BF)
    for i, out in enumerate((o0, o1, o2, o3)):
        out[...] = total[:, i * 256 : (i + 1) * 256]


def place(where_ref, a_ref, b_ref, c_ref, d_ref, out_ref):
    x = where_ref[4]
    for dx, r in zip((0, 1, 3, 2), (a_ref, b_ref, c_ref, d_ref)):
        slot = pl.multiple_of(lax.rem(x + dx, 4) * 32, 32)
        out_ref[pl.ds(slot, 32), :] = r[...]


def ctx_shift(dz, dy, dx):
    pairs = []
    for c in range(32):
        z, y, x = c // 16, (c // 4) % 4, c % 4
        pairs.append((c, ((z + dz) % 2) * 16 + ((y + dy) % 4) * 4 + (x + dx) % 4))
    return pairs


def fetch(value, dz=0, dy=0, dx=0):
    return lax.ppermute(value, "ctx", ctx_shift(-dz, -dy, -dx))


def shards(queries, cache_keys, cache_values, span_keys, span_values, prefix_len, positions, out_weight):
    index = lax.axis_index("ctx")
    head = lax.axis_index("head")
    where = jnp.stack([index // 16, (index // 4) % 4, head % 2, head // 2, index % 4]).astype(jnp.int32)
    pos_row = positions.reshape(1, 32)
    tile = call(pack_query, sds(32, QW), [queries, pos_row])
    tile_z = fetch(tile, dz=1)
    own_tiles = [tile] + [fetch(tile, dx=d) for d in (1, -1, 2)]
    kv = call(
        pack_cache,
        sds(4 * HALF + META, HD),
        [prefix_len, cache_keys, cache_values, span_keys, span_values, pos_row],
        smem=(0,),
    )
    kv_up = fetch(kv, dy=1)
    kv_down = fetch(kv, dy=-1)
    z_tiles = [tile_z] + [fetch(tile_z, dx=d) for d in (1, -1, 2)]
    tiles = [t for pair in zip(own_tiles, z_tiles) for t in pair]

    cut = 2 * HALF + META
    numbers = 2 * HALF + 64
    meta = lambda m: m[numbers : numbers + 16]
    whole = [(0, 0), (cut, HALF)]
    carry = attend_call(tiles, [kv], [meta(kv)], [whole], [], None, False)
    far_a = fetch(kv_up[:cut], dy=1)
    far_b = fetch(kv_down[cut:], dy=-1)
    carry = attend_call(tiles, [kv_up, kv_down], [meta(kv_up), meta(kv_down)], [whole, whole], [], carry, False)
    spans = [m[2 * HALF : 2 * HALF + META] for m in (kv, kv_up, kv_down, far_a)]
    parts = attend_call(
        tiles, [far_a, far_b], [meta(far_a), meta(far_a)], [[(0, 0)], [(0, HALF)]], spans, carry, True
    )
    weights = [out_weight] + [fetch(out_weight, dx=d) for d in (1, -1, 2)]

    joined = call(join_x, sds(64, QW), [parts[0]] + [fetch(parts[i], dx=-d) for i, d in ((1, 1), (2, -1), (3, 2))])
    attended = call(join_z, sds(64, GROUP * HD), [joined, fetch(joined, dz=1)])
    rows = [attended] + [fetch(attended, dy=d) for d in (1, -1, 2)]
    keep, send = call(
        project,
        [sds(128, 1024), sds(128, 1024)],
        [where] + rows + weights,
        smem=(0,),
        flops=2 * 256 * 1024 * 1024,
        nbytes=4 << 20,
    )
    got = lax.ppermute(send, "head", [(h, h ^ 1) for h in range(8)])
    own, *others = call(add_cores, [sds(32, 1024)] * 4, [where, keep, got], smem=(0,))
    others = [lax.ppermute(o, "head", [(h, h ^ (2 * k)) for h in range(8)]) for k, o in zip((1, 2, 3), others)]
    pieces = call(add_z, [sds(32, 256)] * 4, [own] + others)
    pieces = [pieces[0]] + [fetch(pieces[i], dx=-d) for i, d in ((1, 1), (2, -1), (3, 2))]
    pieces = [pieces[0], pieces[2], pieces[1], pieces[3]]
    return call(place, sds(128, 256), [where] + pieces, smem=(0,))


def solution(mesh):
    return jax.shard_map(
        shards,
        mesh=mesh,
        in_specs=(
            P("ctx", "head"),
            P("ctx", "head"),
            P("ctx", "head"),
            P("ctx", "head"),
            P("ctx", "head"),
            P("ctx"),
            P("ctx"),
            P("head", "ctx"),
        ),
        out_specs=P("head", "ctx"),
        check_vma=False,
    )
```

```python
import functools
import math

import jax
import jax.numpy as jnp
from jax import lax
from jax.experimental import pallas as pl
from jax.experimental.pallas import tpu as pltpu
from jax.sharding import PartitionSpec as P

BF = jnp.bfloat16
F32 = jnp.float32
HD = 128
GROUP = 8
HALF = 1024
META = 128
QW = GROUP * HD + 128
LOG2_SCALE = math.log2(math.e) / math.sqrt(HD)
NEG = -1e30


def call(body, out_shape, args, scratch=(), smem=(), idle=(), flops=0, nbytes=0, vmem=8 << 20):
    specs = []
    for i in range(len(args)):
        if i in smem:
            specs.append(pl.BlockSpec(memory_space=pltpu.SMEM))
        elif i in idle:
            specs.append(pl.BlockSpec(memory_space=pl.ANY))
        else:
            specs.append(pl.BlockSpec(memory_space=pltpu.VMEM))
    return pl.pallas_call(
        body,
        out_shape=out_shape,
        in_specs=specs,
        out_specs=jax.tree.map(lambda _: pl.BlockSpec(memory_space=pltpu.VMEM), out_shape),
        scratch_shapes=list(scratch),
        cost_estimate=pl.CostEstimate(flops=flops, bytes_accessed=nbytes, transcendentals=0),
        compiler_params=pltpu.CompilerParams(vmem_limit_bytes=vmem),
    )(*args)


def sds(*shape, dtype=BF):
    return jax.ShapeDtypeStruct(shape, dtype)


def pack_query(q_ref, pos_ref, out_ref):
    pos = jnp.broadcast_to(pos_ref[...], (32, 32))
    row = lax.broadcasted_iota(jnp.int32, (32, 32), 0)
    col = lax.broadcasted_iota(jnp.int32, (32, 32), 1)
    column = jnp.sum(jnp.where(row == col, pos, 0), axis=1, keepdims=True)
    lane = lax.broadcasted_iota(jnp.int32, (32, 128), 1)
    high, low = column // 32, column % 32
    numbers = jnp.where(lane == 0, high, jnp.where(lane == 1, low, 0))
    out_ref[:, : GROUP * HD] = q_ref[...]
    out_ref[:, GROUP * HD :] = numbers.astype(F32).astype(BF)


def pack_cache(len_ref, k_ref, v_ref, sk_ref, sv_ref, pos_ref, out_ref):
    used = len_ref[0]
    first = jnp.broadcast_to(k_ref[0:1, :].astype(F32), (HD, HD))
    for half in range(2):
        base = half * (2 * HALF + META)
        for block in range(HALF // HD):
            start = half * HALF + block * HD
            seen = lax.broadcasted_iota(jnp.int32, (HD, HD), 0) + start < used
            keys = jnp.where(seen, k_ref[start : start + HD, :].astype(F32), first)
            out_ref[base + block * HD : base + (block + 1) * HD, :] = keys.astype(BF)
            values = jnp.where(seen, v_ref[start : start + HD, :].astype(F32), 0.0)
            out_ref[base + HALF + block * HD : base + HALF + (block + 1) * HD, :] = values.astype(BF)
    meta = 2 * HALF
    out_ref[meta : meta + 32, :] = sk_ref[...]
    out_ref[meta + 32 : meta + 64, :] = sv_ref[...]
    pos = jnp.concatenate([pos_ref[...], jnp.zeros((1, 96), jnp.int32)], axis=1)
    pos = jnp.broadcast_to(pos, (64, HD))
    row = lax.broadcasted_iota(jnp.int32, (64, HD), 0)
    lane = lax.broadcasted_iota(jnp.int32, (64, HD), 1)
    extent = jnp.where(lane == 0, used // 32, jnp.where(lane == 1, used % 32, 0))
    numbers = jnp.where(row == 0, pos // 32, jnp.where(row == 1, pos % 32, jnp.where(row == 2, extent, 0)))
    out_ref[meta + 64 : meta + 128, :] = numbers.astype(F32).astype(BF)


def attend(n_tiles, layout, span, first, last, n_idle, *refs):
    refs = list(refs)
    tiles = [refs.pop(0) for _ in range(n_tiles)]
    kvs = [refs.pop(0) for _ in layout]
    spans = [refs.pop(0) for _ in range(3)] if span else []
    if not first:
        acc_in, st_in = refs.pop(0), refs.pop(0)
    if first:
        w_in = refs.pop(0)
    del refs[:n_idle]
    if last:
        outs = [refs.pop(0) for _ in range(n_tiles // 2)]
    else:
        acc_out, st_out = refs.pop(0), refs.pop(0)
        for kv in kvs:
            refs.pop(0)[...] = kv[2 * HALF : 2 * HALF + META, :]
    if first:
        refs.pop(0)[...] = w_in[...]
    v2, score_a, score_b = refs
    rows = 32 * n_tiles
    blocks = []
    at = 0
    for i, (holder, pieces) in enumerate(layout):
        numbers = kvs[holder][2 * HALF + 64 : 2 * HALF + 80, :].astype(F32)
        used = numbers[2:3, 0:1] * 32.0 + numbers[2:3, 1:2]
        for start, cache_row in pieces:
            v2[at : at + HALF, :HD] = kvs[i][start + HALF : start + 2 * HALF, :]
            index = lax.broadcasted_iota(jnp.int32, (HALF, HD), 0) + cache_row
            v2[at : at + HALF, HD:] = jnp.where(index.astype(F32) < used, 1.0, 0.0).astype(BF)
            blocks += [(at + c, 256, kvs[i], start + c) for c in range(0, HALF, 256)]
            at += HALF
    if span:
        near = [s[...] for s in spans] + [kvs[0][2 * HALF : 2 * HALF + META, :]]
        span_keys = jnp.concatenate([s[0:32, :] for s in near], axis=0)
        for i, s in enumerate(near):
            v2[at + 32 * i : at + 32 * (i + 1), :HD] = s[32:64, :]
        v2[at : at + HD, HD:] = jnp.ones((HD, HD), BF)
        near = [s[64:80, :].astype(F32) for s in near]
        key_pos = jnp.concatenate([s[0:1, 0:32] * 32.0 + s[1:2, 0:32] for s in near], axis=1)
        numbers = jnp.concatenate([t[:, GROUP * HD :] for t in tiles], axis=0).astype(F32)
        query_pos = numbers[:, 0:1] * 32.0 + numbers[:, 1:2]
        seen = key_pos <= query_pos
        blocks.append((at, HD, None, 0))
    lane = lax.broadcasted_iota(jnp.int32, (rows, HD), 1)
    st = jnp.zeros((rows, HD), F32) if first else st_in[...]
    new_st = jnp.zeros((rows, HD), F32)
    peak = None
    for head in range(GROUP + 1):
        mine, previous = (score_a, score_b) if head % 2 == 0 else (score_b, score_a)
        cols = slice(head * HD, (head + 1) * HD)
        if head < GROUP:
            query = jnp.concatenate([t[:, cols] for t in tiles], axis=0)
        top = None
        acc = None
        for c, width, kv, row in blocks:
            if head < GROUP:
                keys = span_keys if kv is None else kv[row : row + width, :]
                s = lax.dot_general(query, keys, (((1,), (1,)), ((), ())), preferred_element_type=F32)
                s = s * LOG2_SCALE
                if kv is None:
                    s = jnp.where(seen, s, NEG)
                mine[:, c : c + width] = s
                for i in range(0, width, HD):
                    top = s[:, i : i + HD] if top is None else jnp.maximum(top, s[:, i : i + HD])
            if head > 0:
                p = jnp.exp2(previous[:, c : c + width] - peak).astype(BF)
                term = jnp.dot(p, v2[c : c + width, :], preferred_element_type=F32)
                acc = term if acc is None else acc + term
        if head > 0:
            h = head - 1
            cols = slice(h * HD, (h + 1) * HD)
            total, weight = acc[:, :HD], acc[:, HD:]
            if not first:
                rescale = jnp.exp2(st[:, h : h + 1] - peak)
                total = total + acc_in[:, cols] * rescale
                weight = weight + st[:, GROUP + h : GROUP + h + 1] * rescale
            new_st = jnp.where(lane == h, jnp.broadcast_to(peak, (rows, HD)), new_st)
            new_st = jnp.where(lane == GROUP + h, weight, new_st)
            if last:
                for i, out in enumerate(outs):
                    out[:, cols] = total[64 * i : 64 * (i + 1), :].astype(BF)
            else:
                acc_out[:, cols] = total
        if head < GROUP:
            peak = jnp.max(top, axis=1, keepdims=True).astype(BF).astype(F32)
            if not first:
                peak = jnp.maximum(peak, st[:, head : head + 1])
    if last:
        high = new_st.astype(BF).astype(F32)
        low = pltpu.roll(new_st - high, GROUP, 1)
        packed = jnp.where(lane < 2 * GROUP, high, jnp.where(lane < 3 * GROUP, low, 0.0)).astype(BF)
        for i, out in enumerate(outs):
            out[:, GROUP * HD :] = packed[64 * i : 64 * (i + 1), :]
    else:
        st_out[...] = new_st


def attend_call(tiles, kvs, layout, spans=(), carry=None, weight=None, idle=(), last=False):
    n_keys = HALF * sum(len(p) for _, p in layout) + (HD if spans else 0)
    rows = 32 * len(tiles)
    first = carry is None
    args = list(tiles) + list(kvs) + list(spans) + ([weight] if first else list(carry)) + list(idle)
    if last:
        out = [sds(64, QW) for _ in range(len(tiles) // 2)]
    else:
        out = [sds(rows, GROUP * HD, dtype=F32), sds(rows, HD, dtype=F32)]
        out += [sds(META, HD) for _ in kvs]
        out += [sds(*weight.shape)] if first else []
    return call(
        functools.partial(attend, len(tiles), layout, bool(spans), first, last, len(idle)),
        out,
        args,
        scratch=[
            pltpu.VMEM((n_keys, 2 * HD), BF),
            pltpu.VMEM((rows, n_keys), F32),
            pltpu.VMEM((rows, n_keys), F32),
        ],
        idle=range(len(args) - len(idle), len(args)),
        flops=rows * GROUP * n_keys * HD * 8,
        nbytes=4 << 20,
        vmem=24 << 20,
    )


def join(messages, final):
    stats = [m[:, GROUP * HD :].astype(F32) for m in messages]
    sums, peaks, weights = [], [], []
    for h in range(GROUP):
        each = [s[:, h : h + 1] for s in stats]
        peak = functools.reduce(jnp.maximum, each)
        scales = [jnp.exp2(p - peak) for p in each]
        weight = sum(
            (s[:, GROUP + h : GROUP + h + 1] + s[:, 2 * GROUP + h : 2 * GROUP + h + 1]) * c
            for s, c in zip(stats, scales)
        )
        total = sum(m[:, h * HD : (h + 1) * HD].astype(F32) * c for m, c in zip(messages, scales))
        sums.append(total / weight if final else total)
        peaks.append(peak)
        weights.append(weight)
    return sums, peaks, weights


def join_x(a_ref, b_ref, c_ref, d_ref, out_ref):
    messages = [r[...] for r in (a_ref, b_ref, c_ref, d_ref)]
    sums, peaks, weights = join(messages, False)
    lane = lax.broadcasted_iota(jnp.int32, (64, HD), 1)
    numbers = jnp.zeros((64, HD), F32)
    for h in range(GROUP):
        out_ref[:, h * HD : (h + 1) * HD] = sums[h].astype(BF)
        high = weights[h].astype(BF).astype(F32)
        numbers = jnp.where(lane == h, peaks[h], numbers)
        numbers = jnp.where(lane == GROUP + h, high, numbers)
        numbers = jnp.where(lane == 2 * GROUP + h, weights[h] - high, numbers)
    out_ref[:, GROUP * HD :] = numbers.astype(BF)


def join_z(own_ref, other_ref, out_ref):
    other = jnp.concatenate([other_ref[32:64, :], other_ref[0:32, :]], axis=0)
    sums, _, _ = join([own_ref[...], other], True)
    for h in range(GROUP):
        out_ref[:, h * HD : (h + 1) * HD] = sums[h].astype(BF)


def project(where_ref, a0, a1, a2, a3, w0, w1, w2, w3, keep_ref, send_ref, rows_ref):
    z, y, core = where_ref[0], where_ref[1], where_ref[2]
    for a, dy in zip((a0, a1, a2, a3), (0, 1, 3, 2)):
        there = lax.rem(y + dy, 4)
        other = lax.rem(there + core, 2)
        for part in range(2):
            z_there = z if part == 0 else 1 - z
            slot = pl.multiple_of((other * 4 + z_there * 2 + there // 2) * 32, 32)
            rows_ref[pl.ds(slot, 32), :] = a[32 * part : 32 * (part + 1), :]
    for i, w in enumerate((w0, w1, w2, w3)):
        out = jnp.dot(rows_ref[...], w[...], preferred_element_type=F32).astype(BF)
        keep_ref[:, i * 256 : (i + 1) * 256] = out[:128, :]
        send_ref[:, i * 256 : (i + 1) * 256] = out[128:, :]


def add_cores(where_ref, keep_ref, got_ref, own_ref, o1, o2, o3):
    z_lo = where_ref[3]
    for k, out in enumerate((own_ref, o1, o2, o3)):
        slot = pl.multiple_of((z_lo ^ k) * 32, 32)
        out[...] = (keep_ref[pl.ds(slot, 32), :].astype(F32) + got_ref[pl.ds(slot, 32), :].astype(F32)).astype(BF)


def add_z(a_ref, b_ref, c_ref, d_ref, o0, o1, o2, o3):
    total = sum(r[...].astype(F32) for r in (a_ref, b_ref, c_ref, d_ref)).astype(BF)
    for i, out in enumerate((o0, o1, o2, o3)):
        out[...] = total[:, i * 256 : (i + 1) * 256]


def place(where_ref, a_ref, b_ref, c_ref, d_ref, out_ref):
    x = where_ref[4]
    for dx, r in zip((0, 1, 3, 2), (a_ref, b_ref, c_ref, d_ref)):
        slot = pl.multiple_of(lax.rem(x + dx, 4) * 32, 32)
        out_ref[pl.ds(slot, 32), :] = r[...]


def ctx_shift(dz, dy, dx):
    pairs = []
    for c in range(32):
        z, y, x = c // 16, (c // 4) % 4, c % 4
        pairs.append((c, ((z + dz) % 2) * 16 + ((y + dy) % 4) * 4 + (x + dx) % 4))
    return pairs


def fetch(value, dz=0, dy=0, dx=0):
    return lax.ppermute(value, "ctx", ctx_shift(-dz, -dy, -dx))


def shards(queries, cache_keys, cache_values, span_keys, span_values, prefix_len, positions, out_weight):
    index = lax.axis_index("ctx")
    head = lax.axis_index("head")
    where = jnp.stack([index // 16, (index // 4) % 4, head % 2, head // 2, index % 4]).astype(jnp.int32)
    pos_row = positions.reshape(1, 32)
    tile = call(pack_query, sds(32, QW), [queries, pos_row])
    tile_z = fetch(tile, dz=1)
    own_tiles = [tile] + [fetch(tile, dx=d) for d in (1, -1, 2)]
    kv = call(
        pack_cache,
        sds(4 * HALF + META, HD),
        [prefix_len, cache_keys, cache_values, span_keys, span_values, pos_row],
        smem=(0,),
    )
    kv_up = fetch(kv, dy=1)
    kv_down = fetch(kv, dy=-1)
    z_tiles = [tile_z] + [fetch(tile_z, dx=d) for d in (1, -1, 2)]
    tiles = [t for pair in zip(own_tiles, z_tiles) for t in pair]

    cut = 2 * HALF + META
    whole = [(0, 0), (cut, HALF)]
    acc, st, span, weight = attend_call(tiles, [kv], [(0, whole)], weight=out_weight)
    weights = [out_weight] + [fetch(weight, dx=d) for d in (2, 1, -1)]
    weights = [weights[0], weights[2], weights[3], weights[1]]
    far_a = fetch(kv_up[:cut], dy=1)
    far_b = fetch(kv_down[cut:], dy=-1)
    acc, st, *spans = attend_call(tiles, [kv_up, kv_down], [(0, whole), (1, whole)], carry=(acc, st))
    parts = attend_call(
        tiles,
        [far_a, far_b],
        [(0, [(0, 0)]), (0, [(0, HALF)])],
        spans=[span] + spans,
        carry=(acc, st),
        idle=weights[1:],
        last=True,
    )

    joined = call(join_x, sds(64, QW), [parts[0]] + [fetch(parts[i], dx=-d) for i, d in ((1, 1), (2, -1), (3, 2))])
    attended = call(join_z, sds(64, GROUP * HD), [joined, fetch(joined, dz=1)])
    rows = [attended] + [fetch(attended, dy=d) for d in (1, -1, 2)]
    keep, send = call(
        project,
        [sds(128, 1024), sds(128, 1024)],
        [where] + rows + weights,
        scratch=[pltpu.VMEM((256, 1024), BF)],
        smem=(0,),
        flops=2 * 256 * 1024 * 1024,
        nbytes=4 << 20,
    )
    got = lax.ppermute(send, "head", [(h, h ^ 1) for h in range(8)])
    own, *others = call(add_cores, [sds(32, 1024)] * 4, [where, keep, got], smem=(0,))
    others = [lax.ppermute(o, "head", [(h, h ^ (2 * k)) for h in range(8)]) for k, o in zip((1, 2, 3), others)]
    pieces = call(add_z, [sds(32, 256)] * 4, [own] + others)
    pieces = [pieces[0]] + [fetch(pieces[i], dx=-d) for i, d in ((1, 1), (2, -1), (3, 2))]
    pieces = [pieces[0], pieces[2], pieces[1], pieces[3]]
    return call(place, sds(128, 256), [where] + pieces, smem=(0,))


def solution(mesh):
    return jax.shard_map(
        shards,
        mesh=mesh,
        in_specs=(
            P("ctx", "head"),
            P("ctx", "head"),
            P("ctx", "head"),
            P("ctx", "head"),
            P("ctx", "head"),
            P("ctx"),
            P("ctx"),
            P("head", "ctx"),
        ),
        out_specs=P("head", "ctx"),
        check_vma=False,
    )
```

```python
import functools
import math

import jax
import jax.numpy as jnp
from jax import lax
from jax.experimental import pallas as pl
from jax.experimental.pallas import tpu as pltpu
from jax.sharding import PartitionSpec as P

BF = jnp.bfloat16
F32 = jnp.float32
HD = 128
GROUP = 8
HALF = 1024
META = 128
QW = GROUP * HD + 128
LOG2_SCALE = math.log2(math.e) / math.sqrt(HD)
NEG = -1e30


def call(body, out_shape, args, scratch=(), smem=(), idle=(), raw=(), flops=0, nbytes=0, vmem=8 << 20):
    specs = []
    for i in range(len(args)):
        if i in smem:
            specs.append(pl.BlockSpec(memory_space=pltpu.SMEM))
        elif i in raw:
            specs.append(pl.BlockSpec(memory_space=pltpu.HBM))
        elif i in idle:
            specs.append(pl.BlockSpec(memory_space=pl.ANY))
        else:
            specs.append(pl.BlockSpec(memory_space=pltpu.VMEM))
    return pl.pallas_call(
        body,
        out_shape=out_shape,
        in_specs=specs,
        out_specs=jax.tree.map(lambda _: pl.BlockSpec(memory_space=pltpu.VMEM), out_shape),
        scratch_shapes=list(scratch),
        cost_estimate=pl.CostEstimate(flops=flops, bytes_accessed=nbytes, transcendentals=0),
        compiler_params=pltpu.CompilerParams(vmem_limit_bytes=vmem),
    )(*args)


def sds(*shape, dtype=BF):
    return jax.ShapeDtypeStruct(shape, dtype)


def pack_query(q_ref, pos_ref, out_ref, sem):
    copy = pltpu.make_async_copy(q_ref, out_ref.at[:, : GROUP * HD], sem)
    copy.start()
    pos = jnp.broadcast_to(pos_ref[...], (32, 32))
    row = lax.broadcasted_iota(jnp.int32, (32, 32), 0)
    col = lax.broadcasted_iota(jnp.int32, (32, 32), 1)
    column = jnp.sum(jnp.where(row == col, pos, 0), axis=1, keepdims=True)
    lane = lax.broadcasted_iota(jnp.int32, (32, 128), 1)
    high, low = column // 32, column % 32
    numbers = jnp.where(lane == 0, high, jnp.where(lane == 1, low, 0))
    out_ref[:, GROUP * HD :] = numbers.astype(F32).astype(BF)
    copy.wait()


def pack_cache(len_ref, k_hbm, v_hbm, sk_ref, sv_ref, pos_ref, _, out_ref, k_ref, v_ref, sems):
    meta = 2 * HALF
    copies = [
        pltpu.make_async_copy(k_hbm, k_ref, sems.at[0]),
        pltpu.make_async_copy(v_hbm, v_ref, sems.at[1]),
        pltpu.make_async_copy(sk_ref, out_ref.at[meta : meta + 32], sems.at[2]),
        pltpu.make_async_copy(sv_ref, out_ref.at[meta + 32 : meta + 64], sems.at[3]),
    ]
    for copy in copies:
        copy.start()
    for copy in copies:
        copy.wait()
    used = len_ref[0]
    first = jnp.broadcast_to(k_ref[0:1, :].astype(F32), (HD, HD))
    for half in range(2):
        base = half * (2 * HALF + META)
        for block in range(HALF // HD):
            start = half * HALF + block * HD
            seen = lax.broadcasted_iota(jnp.int32, (HD, HD), 0) + start < used
            keys = jnp.where(seen, k_ref[start : start + HD, :].astype(F32), first)
            out_ref[base + block * HD : base + (block + 1) * HD, :] = keys.astype(BF)
            values = jnp.where(seen, v_ref[start : start + HD, :].astype(F32), 0.0)
            out_ref[base + HALF + block * HD : base + HALF + (block + 1) * HD, :] = values.astype(BF)
    pos = jnp.concatenate([pos_ref[...], jnp.zeros((1, 96), jnp.int32)], axis=1)
    pos = jnp.broadcast_to(pos, (64, HD))
    row = lax.broadcasted_iota(jnp.int32, (64, HD), 0)
    lane = lax.broadcasted_iota(jnp.int32, (64, HD), 1)
    extent = jnp.where(lane == 0, used // 32, jnp.where(lane == 1, used % 32, 0))
    numbers = jnp.where(row == 0, pos // 32, jnp.where(row == 1, pos % 32, jnp.where(row == 2, extent, 0)))
    out_ref[meta + 64 : meta + 128, :] = numbers.astype(F32).astype(BF)


def attend(layout, span, first, picks, unit, n_tiles, n_idle, *refs):
    last = picks is not None
    refs = list(refs)
    tiles = [refs.pop(0) for _ in range(n_tiles)]
    kvs = [refs.pop(0) for _ in layout]
    spans = [refs.pop(0) for _ in range(3)] if span else []
    if not first:
        acc_in, st_in = refs.pop(0), refs.pop(0)
    if first:
        w_in = refs.pop(0)
    del refs[:n_idle]
    if last:
        outs = [refs.pop(0) for _ in picks]
    else:
        acc_out, st_out = refs.pop(0), refs.pop(0)
        for kv in kvs:
            refs.pop(0)[...] = kv[2 * HALF : 2 * HALF + META, :]
    if first:
        refs.pop(0)[...] = w_in[...]
    v2, score_a, score_b = refs
    rows = 32 * n_tiles

    def carried(ref, cols):
        if not last:
            return ref[:, cols]
        return jnp.concatenate([ref[64 * i : 64 * (i + 1), cols] for i in picks], axis=0)

    blocks = []
    at = 0
    for i, (holder, pieces) in enumerate(layout):
        numbers = kvs[holder][2 * HALF + 64 : 2 * HALF + 80, :].astype(F32)
        used = numbers[2:3, 0:1] * 32.0 + numbers[2:3, 1:2]
        for start, cache_row in pieces:
            v2[at : at + HALF, :HD] = kvs[i][start + HALF : start + 2 * HALF, :]
            index = lax.broadcasted_iota(jnp.int32, (HALF, HD), 0) + cache_row
            v2[at : at + HALF, HD:] = jnp.where(index.astype(F32) < used, 1.0, 0.0).astype(BF)
            blocks += [(at + c, 256, kvs[i], start + c) for c in range(0, HALF, 256)]
            at += HALF
    if span:
        near = [s[...] for s in spans] + [kvs[0][2 * HALF : 2 * HALF + META, :]]
        span_keys = jnp.concatenate([s[0:32, :] for s in near], axis=0)
        for i, s in enumerate(near):
            v2[at + 32 * i : at + 32 * (i + 1), :HD] = s[32:64, :]
        v2[at : at + HD, HD:] = jnp.ones((HD, HD), BF)
        near = [s[64:80, :].astype(F32) for s in near]
        key_pos = jnp.concatenate([s[0:1, 0:32] * 32.0 + s[1:2, 0:32] for s in near], axis=1)
        numbers = jnp.concatenate([t[:, GROUP * HD :] for t in tiles], axis=0).astype(F32)
        query_pos = numbers[:, 0:1] * 32.0 + numbers[:, 1:2]
        seen = key_pos <= query_pos
        blocks.append((at, HD, None, 0))
    if span:
        seen = jnp.concatenate([seen] * unit, axis=0)
    lane = lax.broadcasted_iota(jnp.int32, (rows, HD), 1)
    st = jnp.zeros((rows, HD), F32) if first else carried(st_in, slice(0, HD))
    new_st = jnp.zeros((rows, HD), F32)
    peak = None
    for step in range(GROUP // unit + 1):
        mine, previous = (score_a, score_b) if step % 2 == 0 else (score_b, score_a)
        heads = range(step * unit, (step + 1) * unit)
        if step < GROUP // unit:
            query = jnp.concatenate([t[:, h * HD : (h + 1) * HD] for h in heads for t in tiles], axis=0)
        top = None
        acc = None
        for c, width, kv, row in blocks:
            if step < GROUP // unit:
                keys = span_keys if kv is None else kv[row : row + width, :]
                s = lax.dot_general(query, keys, (((1,), (1,)), ((), ())), preferred_element_type=F32)
                s = s * LOG2_SCALE
                if kv is None:
                    s = jnp.where(seen, s, NEG)
                mine[:, c : c + width] = s
                for i in range(0, width, HD):
                    top = s[:, i : i + HD] if top is None else jnp.maximum(top, s[:, i : i + HD])
            if step > 0:
                p = jnp.exp2(previous[:, c : c + width] - peak).astype(BF)
                term = jnp.dot(p, v2[c : c + width, :], preferred_element_type=F32)
                acc = term if acc is None else acc + term
        if step > 0:
            for u in range(unit):
                h = (step - 1) * unit + u
                part = slice(u * rows, (u + 1) * rows)
                cols = slice(h * HD, (h + 1) * HD)
                total, weight, shift = acc[part, :HD], acc[part, HD:], peak[part, :]
                if not first:
                    rescale = jnp.exp2(st[:, h : h + 1] - shift)
                    total = total + carried(acc_in, cols) * rescale
                    weight = weight + st[:, GROUP + h : GROUP + h + 1] * rescale
                new_st = jnp.where(lane == h, jnp.broadcast_to(shift, (rows, HD)), new_st)
                new_st = jnp.where(lane == GROUP + h, weight, new_st)
                if last:
                    for i, out in enumerate(outs):
                        out[:, cols] = total[64 * i : 64 * (i + 1), :].astype(BF)
                else:
                    acc_out[:, cols] = total
        if step < GROUP // unit:
            peak = jnp.max(top, axis=1, keepdims=True).astype(BF).astype(F32)
            if not first:
                peak = jnp.maximum(peak, jnp.concatenate([st[:, h : h + 1] for h in heads], axis=0))
    if last:
        high = new_st.astype(BF).astype(F32)
        low = pltpu.roll(new_st - high, GROUP, 1)
        packed = jnp.where(lane < 2 * GROUP, high, jnp.where(lane < 3 * GROUP, low, 0.0)).astype(BF)
        for i, out in enumerate(outs):
            out[:, GROUP * HD :] = packed[64 * i : 64 * (i + 1), :]
    else:
        st_out[...] = new_st


def attend_call(tiles, kvs, layout, spans=(), carry=None, weight=None, idle=(), picks=None, unit=1):
    n_keys = HALF * sum(len(p) for _, p in layout) + (HD if spans else 0)
    rows = 32 * len(tiles)
    first = carry is None
    args = list(tiles) + list(kvs) + list(spans) + ([weight] if first else list(carry)) + list(idle)
    if picks is not None:
        out = [sds(64, QW) for _ in picks]
    else:
        out = [sds(rows, GROUP * HD, dtype=F32), sds(rows, HD, dtype=F32)]
        out += [sds(META, HD) for _ in kvs]
        out += [sds(*weight.shape)] if first else []
    return call(
        functools.partial(attend, layout, bool(spans), first, picks, unit, len(tiles), len(idle)),
        out,
        args,
        scratch=[
            pltpu.VMEM((n_keys, 2 * HD), BF),
            pltpu.VMEM((rows * unit, n_keys), F32),
            pltpu.VMEM((rows * unit, n_keys), F32),
        ],
        idle=range(len(args) - len(idle), len(args)),
        flops=rows * GROUP * n_keys * HD * 8,
        nbytes=4 << 20,
        vmem=24 << 20,
    )


def join(messages, final):
    stats = [m[:, GROUP * HD :].astype(F32) for m in messages]
    sums, peaks, weights = [], [], []
    for h in range(GROUP):
        each = [s[:, h : h + 1] for s in stats]
        peak = functools.reduce(jnp.maximum, each)
        scales = [jnp.exp2(p - peak) for p in each]
        weight = sum(
            (s[:, GROUP + h : GROUP + h + 1] + s[:, 2 * GROUP + h : 2 * GROUP + h + 1]) * c
            for s, c in zip(stats, scales)
        )
        total = sum(m[:, h * HD : (h + 1) * HD].astype(F32) * c for m, c in zip(messages, scales))
        sums.append(total / weight if final else total)
        peaks.append(peak)
        weights.append(weight)
    return sums, peaks, weights


def join_x(a_ref, b_ref, c_ref, d_ref, out_ref):
    messages = [r[...] for r in (a_ref, b_ref, c_ref, d_ref)]
    sums, peaks, weights = join(messages, False)
    lane = lax.broadcasted_iota(jnp.int32, (64, HD), 1)
    numbers = jnp.zeros((64, HD), F32)
    for h in range(GROUP):
        out_ref[:, h * HD : (h + 1) * HD] = sums[h].astype(BF)
        high = weights[h].astype(BF).astype(F32)
        numbers = jnp.where(lane == h, peaks[h], numbers)
        numbers = jnp.where(lane == GROUP + h, high, numbers)
        numbers = jnp.where(lane == 2 * GROUP + h, weights[h] - high, numbers)
    out_ref[:, GROUP * HD :] = numbers.astype(BF)


def join_z(own_ref, other_ref, out_ref):
    other = jnp.concatenate([other_ref[32:64, :], other_ref[0:32, :]], axis=0)
    sums, _, _ = join([own_ref[...], other], True)
    for h in range(GROUP):
        out_ref[:, h * HD : (h + 1) * HD] = sums[h].astype(BF)


def halve(a_ref, b_ref, _, top_ref, bottom_ref):
    top_ref[...] = a_ref[:512, :]
    bottom_ref[...] = b_ref[512:, :]


def project(where_ref, a0, a1, a2, a3, w0, w1, w2, w3a, w3b, keep_ref, send_ref, rows_ref):
    z, y, core = where_ref[0], where_ref[1], where_ref[2]
    for a, dy in zip((a0, a1, a2, a3), (0, 1, 3, 2)):
        there = lax.rem(y + dy, 4)
        other = lax.rem(there + core, 2)
        for part in range(2):
            z_there = z if part == 0 else 1 - z
            slot = pl.multiple_of((other * 4 + z_there * 2 + there // 2) * 32, 32)
            rows_ref[pl.ds(slot, 32), :] = a[32 * part : 32 * (part + 1), :]
    for i, w in enumerate((w0, w1, w2, (w3a, w3b))):
        if i < 3:
            out = jnp.dot(rows_ref[...], w[...], preferred_element_type=F32)
        else:
            depth = w3a.shape[0]
            out = jnp.dot(rows_ref[:, :depth], w3a[...], preferred_element_type=F32)
            out += jnp.dot(rows_ref[:, depth:], w3b[...], preferred_element_type=F32)
        out = out.astype(BF)
        keep_ref[:, i * 256 : (i + 1) * 256] = out[:128, :]
        send_ref[:, i * 256 : (i + 1) * 256] = out[128:, :]


def add_cores(where_ref, keep_ref, got_ref, own_ref, o1, o2, o3):
    z_lo = where_ref[3]
    for k, out in enumerate((own_ref, o1, o2, o3)):
        slot = pl.multiple_of((z_lo ^ k) * 32, 32)
        out[...] = (keep_ref[pl.ds(slot, 32), :].astype(F32) + got_ref[pl.ds(slot, 32), :].astype(F32)).astype(BF)


def add_z(a_ref, b_ref, c_ref, d_ref, o0, o1, o2, o3):
    total = sum(r[...].astype(F32) for r in (a_ref, b_ref, c_ref, d_ref)).astype(BF)
    for i, out in enumerate((o0, o1, o2, o3)):
        out[...] = total[:, i * 256 : (i + 1) * 256]


def place(where_ref, a_ref, b_ref, c_ref, d_ref, out_ref):
    x = where_ref[4]
    for dx, r in zip((0, 1, 3, 2), (a_ref, b_ref, c_ref, d_ref)):
        slot = pl.multiple_of(lax.rem(x + dx, 4) * 32, 32)
        out_ref[pl.ds(slot, 32), :] = r[...]


def ctx_shift(dz, dy, dx):
    pairs = []
    for c in range(32):
        z, y, x = c // 16, (c // 4) % 4, c % 4
        pairs.append((c, ((z + dz) % 2) * 16 + ((y + dy) % 4) * 4 + (x + dx) % 4))
    return pairs


def fetch(value, dz=0, dy=0, dx=0):
    return lax.ppermute(value, "ctx", ctx_shift(-dz, -dy, -dx))


def shards(queries, cache_keys, cache_values, span_keys, span_values, prefix_len, positions, out_weight):
    index = lax.axis_index("ctx")
    head = lax.axis_index("head")
    where = jnp.stack([index // 16, (index // 4) % 4, head % 2, head // 2, index % 4]).astype(jnp.int32)
    pos_row = positions.reshape(1, 32)
    tile = call(pack_query, sds(32, QW), [queries, pos_row], scratch=[pltpu.SemaphoreType.DMA], raw=(0,))
    tile_z = fetch(tile, dz=1)
    own_tiles = [tile] + [fetch(tile, dx=d) for d in (1, -1, 2)]
    kv = call(
        pack_cache,
        sds(4 * HALF + META, HD),
        [prefix_len, cache_keys, cache_values, span_keys, span_values, pos_row, tile],
        scratch=[
            pltpu.VMEM((2 * HALF, HD), BF),
            pltpu.VMEM((2 * HALF, HD), BF),
            pltpu.SemaphoreType.DMA((4,)),
        ],
        smem=(0,),
        raw=(1, 2, 3, 4),
        idle=(6,),
        vmem=58 << 20,
    )
    kv_up = fetch(kv, dy=1)
    kv_down = fetch(kv, dy=-1)
    z_tiles = [tile_z] + [fetch(tile_z, dx=d) for d in (1, -1, 2)]
    tiles = [t for pair in zip(own_tiles, z_tiles) for t in pair]

    cut = 2 * HALF + META
    whole = [(0, 0), (cut, HALF)]
    acc, st, span, weight = attend_call(tiles, [kv], [(0, whole)], weight=out_weight)
    far_a = fetch(kv_up[:cut], dy=1)
    far_b = fetch(kv_down[cut:], dy=-1)
    w_up, w_down = fetch(weight, dx=1), fetch(weight, dx=-1)
    acc, st, *spans = attend_call(tiles, [kv_up, kv_down], [(0, whole), (1, whole)], carry=(acc, st))
    halves = call(halve, [sds(512, 256)] * 2, [w_up, w_down, st], idle=(2,))
    w_far = [fetch(halves[0], dx=1), fetch(halves[1], dx=-1)]
    weights = [out_weight, w_up, w_down] + w_far

    def finish(picks, idle):
        mine = [t for i in picks for t in tiles[2 * i : 2 * i + 2]]
        far = [(0, [(0, 0)]), (0, [(0, HALF)])]
        return attend_call(
            mine, [far_a, far_b], far, spans=[span] + spans, carry=(acc, st), idle=idle, picks=picks, unit=2
        )

    part_3, part_1 = finish((3, 1), [w_up, w_down])
    got_3, got_1 = fetch(part_3, dx=-2), fetch(part_1, dx=-1)
    part_2, part_0 = finish((2, 0), w_far)
    got_2 = fetch(part_2, dx=1)
    joined = call(join_x, sds(64, QW), [part_0, got_1, got_2, got_3])
    attended = call(join_z, sds(64, GROUP * HD), [joined, fetch(joined, dz=1)])
    rows = [attended] + [fetch(attended, dy=d) for d in (1, -1, 2)]
    keep, send = call(
        project,
        [sds(128, 1024), sds(128, 1024)],
        [where] + rows + weights,
        scratch=[pltpu.VMEM((256, 1024), BF)],
        smem=(0,),
        flops=2 * 256 * 1024 * 1024,
        nbytes=4 << 20,
    )
    got = lax.ppermute(send, "head", [(h, h ^ 1) for h in range(8)])
    own, *others = call(add_cores, [sds(32, 1024)] * 4, [where, keep, got], smem=(0,))
    others = [lax.ppermute(o, "head", [(h, h ^ (2 * k)) for h in range(8)]) for k, o in zip((1, 2, 3), others)]
    pieces = call(add_z, [sds(32, 256)] * 4, [own] + others)
    pieces = [pieces[0]] + [fetch(pieces[i], dx=-d) for i, d in ((1, 1), (2, -1), (3, 2))]
    pieces = [pieces[0], pieces[2], pieces[1], pieces[3]]
    return call(place, sds(128, 256), [where] + pieces, smem=(0,))


def solution(mesh):
    return jax.shard_map(
        shards,
        mesh=mesh,
        in_specs=(
            P("ctx", "head"),
            P("ctx", "head"),
            P("ctx", "head"),
            P("ctx", "head"),
            P("ctx", "head"),
            P("ctx"),
            P("ctx"),
            P("head", "ctx"),
        ),
        out_specs=P("head", "ctx"),
        check_vma=False,
    )
```

```python
import functools
import math

import jax
import jax.numpy as jnp
from jax import lax
from jax.experimental import pallas as pl
from jax.experimental.pallas import tpu as pltpu
from jax.sharding import PartitionSpec as P

BF = jnp.bfloat16
F32 = jnp.float32
HD = 128
GROUP = 8
HALF = 1024
META = 128
QW = GROUP * HD + 128
LOG2_SCALE = math.log2(math.e) / math.sqrt(HD)
NEG = -1e30


def call(body, out_shape, args, scratch=(), smem=(), idle=(), raw=(), flops=0, nbytes=0, vmem=8 << 20):
    args, specs = list(args), []
    for i in range(len(args)):
        if i in smem:
            specs.append(pl.BlockSpec(memory_space=pltpu.SMEM))
        elif i in raw:
            specs.append(pl.BlockSpec(memory_space=pltpu.HBM))
            args[i] = pltpu.with_memory_space_constraint(args[i], pltpu.HBM)
        elif i in idle:
            specs.append(pl.BlockSpec(memory_space=pl.ANY))
        else:
            specs.append(pl.BlockSpec(memory_space=pltpu.VMEM))
    return pl.pallas_call(
        body,
        out_shape=out_shape,
        in_specs=specs,
        out_specs=jax.tree.map(lambda _: pl.BlockSpec(memory_space=pltpu.VMEM), out_shape),
        scratch_shapes=list(scratch),
        cost_estimate=pl.CostEstimate(flops=flops, bytes_accessed=nbytes, transcendentals=0),
        compiler_params=pltpu.CompilerParams(vmem_limit_bytes=vmem),
    )(*args)


def near(*shape, dtype=BF):
    return pltpu.VMEM(shape, dtype)


def sds(*shape, dtype=BF):
    return jax.ShapeDtypeStruct(shape, dtype)


def pack(len_ref, q_hbm, k_hbm, v_hbm, sk_hbm, sv_hbm, pos_ref, tile_ref, out_ref, k_ref, v_ref, sems):
    meta = 2 * HALF
    copies = [
        pltpu.make_async_copy(k_hbm, k_ref, sems.at[0]),
        pltpu.make_async_copy(v_hbm, v_ref, sems.at[1]),
        pltpu.make_async_copy(sk_hbm, out_ref.at[meta : meta + 32], sems.at[2]),
        pltpu.make_async_copy(sv_hbm, out_ref.at[meta + 32 : meta + 64], sems.at[3]),
        pltpu.make_async_copy(q_hbm, tile_ref.at[:, : GROUP * HD], sems.at[4]),
    ]
    for copy in copies:
        copy.start()
    pos = jnp.broadcast_to(pos_ref[...], (32, 32))
    row = lax.broadcasted_iota(jnp.int32, (32, 32), 0)
    col = lax.broadcasted_iota(jnp.int32, (32, 32), 1)
    column = jnp.sum(jnp.where(row == col, pos, 0), axis=1, keepdims=True)
    lane = lax.broadcasted_iota(jnp.int32, (32, 128), 1)
    numbers = jnp.where(lane == 0, column // 32, jnp.where(lane == 1, column % 32, 0))
    tile_ref[:, GROUP * HD :] = numbers.astype(F32).astype(BF)
    for copy in copies:
        copy.wait()
    used = len_ref[0]
    first = jnp.broadcast_to(k_ref[0:1, :].astype(F32), (HD, HD))
    for half in range(2):
        base = half * (2 * HALF + META)
        for block in range(HALF // HD):
            start = half * HALF + block * HD
            seen = lax.broadcasted_iota(jnp.int32, (HD, HD), 0) + start < used
            keys = jnp.where(seen, k_ref[start : start + HD, :].astype(F32), first)
            out_ref[base + block * HD : base + (block + 1) * HD, :] = keys.astype(BF)
            values = jnp.where(seen, v_ref[start : start + HD, :].astype(F32), 0.0)
            out_ref[base + HALF + block * HD : base + HALF + (block + 1) * HD, :] = values.astype(BF)
    pos = jnp.concatenate([pos_ref[...], jnp.zeros((1, 96), jnp.int32)], axis=1)
    pos = jnp.broadcast_to(pos, (64, HD))
    row = lax.broadcasted_iota(jnp.int32, (64, HD), 0)
    lane = lax.broadcasted_iota(jnp.int32, (64, HD), 1)
    extent = jnp.where(lane == 0, used // 32, jnp.where(lane == 1, used % 32, 0))
    numbers = jnp.where(row == 0, pos // 32, jnp.where(row == 1, pos % 32, jnp.where(row == 2, extent, 0)))
    out_ref[meta + 64 : meta + 128, :] = numbers.astype(F32).astype(BF)


def pair(a_ref, b_ref, out_ref):
    out_ref[0:32, :] = a_ref[...]
    out_ref[32:64, :] = b_ref[...]


def attend(layout, span, first, picks, unit, n_tiles, n_idle, *refs):
    last = picks is not None
    refs = list(refs)
    tiles = [refs.pop(0) for _ in range(n_tiles)]
    kvs = [refs.pop(0) for _ in layout]
    spans = [refs.pop(0) for _ in range(3)] if span else []
    if not first:
        acc_in, st_in = refs.pop(0), refs.pop(0)
    if first:
        w_in = refs.pop(0)
    del refs[:n_idle]
    if last:
        outs = [refs.pop(0) for _ in picks]
    else:
        acc_out, st_out = refs.pop(0), refs.pop(0)
        for kv in kvs:
            refs.pop(0)[...] = kv[2 * HALF : 2 * HALF + META, :]
    if first:
        refs.pop(0)[...] = w_in[...]
    v2, score_a, score_b = refs
    rows = 64 * n_tiles

    def carried(ref, cols):
        if not last:
            return ref[:, cols]
        return jnp.concatenate([ref[64 * i : 64 * (i + 1), cols] for i in picks], axis=0)

    blocks = []
    at = 0
    for i, (holder, pieces) in enumerate(layout):
        numbers = kvs[holder][2 * HALF + 64 : 2 * HALF + 80, :].astype(F32)
        used = numbers[2:3, 0:1] * 32.0 + numbers[2:3, 1:2]
        for start, cache_row in pieces:
            v2[at : at + HALF, :HD] = kvs[i][start + HALF : start + 2 * HALF, :]
            index = lax.broadcasted_iota(jnp.int32, (HALF, HD), 0) + cache_row
            v2[at : at + HALF, HD:] = jnp.where(index.astype(F32) < used, 1.0, 0.0).astype(BF)
            blocks += [(at + c, 256, kvs[i], start + c) for c in range(0, HALF, 256)]
            at += HALF
    if span:
        near = [s[...] for s in spans] + [kvs[0][2 * HALF : 2 * HALF + META, :]]
        span_keys = jnp.concatenate([s[0:32, :] for s in near], axis=0)
        for i, s in enumerate(near):
            v2[at + 32 * i : at + 32 * (i + 1), :HD] = s[32:64, :]
        v2[at : at + HD, HD:] = jnp.ones((HD, HD), BF)
        near = [s[64:80, :].astype(F32) for s in near]
        key_pos = jnp.concatenate([s[0:1, 0:32] * 32.0 + s[1:2, 0:32] for s in near], axis=1)
        numbers = jnp.concatenate([t[:, GROUP * HD :] for t in tiles], axis=0).astype(F32)
        query_pos = numbers[:, 0:1] * 32.0 + numbers[:, 1:2]
        seen = key_pos <= query_pos
        blocks.append((at, HD, None, 0))
    if span:
        seen = jnp.concatenate([seen] * unit, axis=0)
    lane = lax.broadcasted_iota(jnp.int32, (rows, HD), 1)
    st = jnp.zeros((rows, HD), F32) if first else carried(st_in, slice(0, HD))
    new_st = jnp.zeros((rows, HD), F32)
    peak = None
    for step in range(GROUP // unit + 1):
        mine, previous = (score_a, score_b) if step % 2 == 0 else (score_b, score_a)
        heads = range(step * unit, (step + 1) * unit)
        if step < GROUP // unit:
            query = jnp.concatenate([t[:, h * HD : (h + 1) * HD] for h in heads for t in tiles], axis=0)
        top = None
        acc = None
        for c, width, kv, row in blocks:
            if step < GROUP // unit:
                keys = span_keys if kv is None else kv[row : row + width, :]
                s = lax.dot_general(query, keys, (((1,), (1,)), ((), ())), preferred_element_type=F32)
                s = s * LOG2_SCALE
                if kv is None:
                    s = jnp.where(seen, s, NEG)
                mine[:, c : c + width] = s
                for i in range(0, width, HD):
                    top = s[:, i : i + HD] if top is None else jnp.maximum(top, s[:, i : i + HD])
            if step > 0:
                p = jnp.exp2(previous[:, c : c + width] - peak).astype(BF)
                term = jnp.dot(p, v2[c : c + width, :], preferred_element_type=F32)
                acc = term if acc is None else acc + term
        if step > 0:
            for u in range(unit):
                h = (step - 1) * unit + u
                part = slice(u * rows, (u + 1) * rows)
                cols = slice(h * HD, (h + 1) * HD)
                total, weight, shift = acc[part, :HD], acc[part, HD:], peak[part, :]
                if not first:
                    rescale = jnp.exp2(st[:, h : h + 1] - shift)
                    total = total + carried(acc_in, cols) * rescale
                    weight = weight + st[:, GROUP + h : GROUP + h + 1] * rescale
                new_st = jnp.where(lane == h, jnp.broadcast_to(shift, (rows, HD)), new_st)
                new_st = jnp.where(lane == GROUP + h, weight, new_st)
                if last:
                    for i, out in enumerate(outs):
                        out[:, cols] = total[64 * i : 64 * (i + 1), :].astype(BF)
                else:
                    acc_out[:, cols] = total
        if step < GROUP // unit:
            peak = jnp.max(top, axis=1, keepdims=True).astype(BF).astype(F32)
            if not first:
                peak = jnp.maximum(peak, jnp.concatenate([st[:, h : h + 1] for h in heads], axis=0))
    if last:
        high = new_st.astype(BF).astype(F32)
        low = pltpu.roll(new_st - high, GROUP, 1)
        packed = jnp.where(lane < 2 * GROUP, high, jnp.where(lane < 3 * GROUP, low, 0.0)).astype(BF)
        for i, out in enumerate(outs):
            out[:, GROUP * HD :] = packed[64 * i : 64 * (i + 1), :]
    else:
        st_out[...] = new_st


def attend_call(tiles, kvs, layout, spans=(), carry=None, weight=None, idle=(), picks=None, unit=1):
    n_keys = HALF * sum(len(p) for _, p in layout) + (HD if spans else 0)
    rows = 64 * len(tiles)
    first = carry is None
    args = list(tiles) + list(kvs) + list(spans) + ([weight] if first else list(carry)) + list(idle)
    if picks is not None:
        out = [sds(64, QW) for _ in picks]
    else:
        out = [sds(rows, GROUP * HD, dtype=F32), sds(rows, HD, dtype=F32)]
        out += [sds(META, HD) for _ in kvs]
        out += [sds(*weight.shape)] if first else []
    return call(
        functools.partial(attend, layout, bool(spans), first, picks, unit, len(tiles), len(idle)),
        out,
        args,
        scratch=[
            pltpu.VMEM((n_keys, 2 * HD), BF),
            pltpu.VMEM((rows * unit, n_keys), F32),
            pltpu.VMEM((rows * unit, n_keys), F32),
        ],
        idle=range(len(args) - len(idle), len(args)),
        flops=rows * GROUP * n_keys * HD * 8,
        nbytes=4 << 20,
        vmem=24 << 20,
    )


def join(messages, final):
    stats = [m[:, GROUP * HD :].astype(F32) for m in messages]
    sums, peaks, weights = [], [], []
    for h in range(GROUP):
        each = [s[:, h : h + 1] for s in stats]
        peak = functools.reduce(jnp.maximum, each)
        scales = [jnp.exp2(p - peak) for p in each]
        weight = sum(
            (s[:, GROUP + h : GROUP + h + 1] + s[:, 2 * GROUP + h : 2 * GROUP + h + 1]) * c
            for s, c in zip(stats, scales)
        )
        total = sum(m[:, h * HD : (h + 1) * HD].astype(F32) * c for m, c in zip(messages, scales))
        sums.append(total / weight if final else total)
        peaks.append(peak)
        weights.append(weight)
    return sums, peaks, weights


def join_x(a_ref, b_ref, c_ref, d_ref, w_ref, out_ref, w_out):
    w_out[...] = w_ref[...]
    messages = [r[...] for r in (a_ref, b_ref, c_ref, d_ref)]
    sums, peaks, weights = join(messages, False)
    lane = lax.broadcasted_iota(jnp.int32, (64, HD), 1)
    numbers = jnp.zeros((64, HD), F32)
    for h in range(GROUP):
        out_ref[:, h * HD : (h + 1) * HD] = sums[h].astype(BF)
        high = weights[h].astype(BF).astype(F32)
        numbers = jnp.where(lane == h, peaks[h], numbers)
        numbers = jnp.where(lane == GROUP + h, high, numbers)
        numbers = jnp.where(lane == 2 * GROUP + h, weights[h] - high, numbers)
    out_ref[:, GROUP * HD :] = numbers.astype(BF)


def join_z(own_ref, other_ref, out_ref):
    other = jnp.concatenate([other_ref[32:64, :], other_ref[0:32, :]], axis=0)
    sums, _, _ = join([own_ref[...], other], True)
    for h in range(GROUP):
        out_ref[:, h * HD : (h + 1) * HD] = sums[h].astype(BF)


def project(where_ref, a0, a1, a2, a3, w0, w1, w2, w3, keep_ref, send_ref, rows_ref):
    z, y, core = where_ref[0], where_ref[1], where_ref[2]
    for a, dy in zip((a0, a1, a2, a3), (0, 1, 3, 2)):
        there = lax.rem(y + dy, 4)
        other = lax.rem(there + core, 2)
        for part in range(2):
            z_there = z if part == 0 else 1 - z
            slot = pl.multiple_of((other * 4 + z_there * 2 + there // 2) * 32, 32)
            rows_ref[pl.ds(slot, 32), :] = a[32 * part : 32 * (part + 1), :]
    for i, w in enumerate((w0, w1, w2, w3)):
        out = jnp.dot(rows_ref[...], w[...], preferred_element_type=F32).astype(BF)
        keep_ref[:, i * 256 : (i + 1) * 256] = out[:128, :]
        send_ref[:, i * 256 : (i + 1) * 256] = out[128:, :]


def add_cores(where_ref, keep_ref, got_ref, own_ref, o1, o2, o3):
    z_lo = where_ref[3]
    for k, out in enumerate((own_ref, o1, o2, o3)):
        slot = pl.multiple_of((z_lo ^ k) * 32, 32)
        out[...] = (keep_ref[pl.ds(slot, 32), :].astype(F32) + got_ref[pl.ds(slot, 32), :].astype(F32)).astype(BF)


def add_z(a_ref, b_ref, c_ref, d_ref, o0, o1, o2, o3):
    total = sum(r[...].astype(F32) for r in (a_ref, b_ref, c_ref, d_ref)).astype(BF)
    for i, out in enumerate((o0, o1, o2, o3)):
        out[...] = total[:, i * 256 : (i + 1) * 256]


def place(where_ref, a_ref, b_ref, c_ref, d_ref, out_ref):
    x = where_ref[4]
    for dx, r in zip((0, 1, 3, 2), (a_ref, b_ref, c_ref, d_ref)):
        slot = pl.multiple_of(lax.rem(x + dx, 4) * 32, 32)
        out_ref[pl.ds(slot, 32), :] = r[...]


def ctx_shift(dz, dy, dx):
    pairs = []
    for c in range(32):
        z, y, x = c // 16, (c // 4) % 4, c % 4
        pairs.append((c, ((z + dz) % 2) * 16 + ((y + dy) % 4) * 4 + (x + dx) % 4))
    return pairs


def fetch(value, dz=0, dy=0, dx=0):
    return lax.ppermute(value, "ctx", ctx_shift(-dz, -dy, -dx))


def shards(queries, cache_keys, cache_values, span_keys, span_values, prefix_len, positions, out_weight):
    index = lax.axis_index("ctx")
    head = lax.axis_index("head")
    where = jnp.stack([index // 16, (index // 4) % 4, head % 2, head // 2, index % 4]).astype(jnp.int32)
    pos_row = positions.reshape(1, 32)
    tile, kv = call(
        pack,
        [near(32, QW), near(4 * HALF + META, HD)],
        [prefix_len, queries, cache_keys, cache_values, span_keys, span_values, pos_row],
        scratch=[
            pltpu.VMEM((2 * HALF, HD), BF),
            pltpu.VMEM((2 * HALF, HD), BF),
            pltpu.SemaphoreType.DMA((5,)),
        ],
        smem=(0,),
        raw=(1, 2, 3, 4, 5),
    )
    kv_up = fetch(kv, dy=1)
    kv_down = fetch(kv, dy=-1)
    own = call(pair, sds(64, QW), [tile, fetch(tile, dz=1)])
    far = fetch(own, dx=2)
    tiles = [own, fetch(own, dx=1), fetch(own, dx=-1), far]

    cut = 2 * HALF + META
    whole = [(0, 0), (cut, HALF)]
    acc, st, span, weight = attend_call(tiles, [kv], [(0, whole)], weight=out_weight)
    far_a = fetch(kv_up[:cut], dy=1)
    far_b = fetch(kv_down[cut:], dy=-1)
    w_up = fetch(weight, dx=1)
    acc, st, *spans = attend_call(tiles, [kv_up, kv_down], [(0, whole), (1, whole)], carry=(acc, st))

    def finish(picks, idle, unit):
        far = [(0, [(0, 0)]), (0, [(0, HALF)])]
        return attend_call(
            [tiles[i] for i in picks],
            [far_a, far_b],
            far,
            spans=[span] + spans,
            carry=(acc, st),
            idle=idle,
            picks=picks,
            unit=unit,
        )

    part_3, part_1, part_2 = finish((3, 1, 2), [w_up], 2)
    got_3, got_1, got_2 = fetch(part_3, dx=-2), fetch(part_1, dx=-1), fetch(part_2, dx=1)
    (part_0,) = finish((0,), [part_3], 4)
    joined, weight = call(join_x, [sds(64, QW), sds(1024, 256)], [part_0, got_1, got_2, got_3, weight])
    weights = [out_weight, w_up, fetch(weight, dx=-1), fetch(weight, dx=2)]
    attended = call(join_z, sds(64, GROUP * HD), [joined, fetch(joined, dz=1)])
    rows = [attended] + [fetch(attended, dy=d) for d in (1, -1, 2)]
    keep, send = call(
        project,
        [sds(128, 1024), sds(128, 1024)],
        [where] + rows + weights,
        scratch=[pltpu.VMEM((256, 1024), BF)],
        smem=(0,),
        flops=2 * 256 * 1024 * 1024,
        nbytes=4 << 20,
    )
    got = lax.ppermute(send, "head", [(h, h ^ 1) for h in range(8)])
    own, *others = call(add_cores, [sds(32, 1024)] * 4, [where, keep, got], smem=(0,))
    others = [lax.ppermute(o, "head", [(h, h ^ (2 * k)) for h in range(8)]) for k, o in zip((1, 2, 3), others)]
    pieces = call(add_z, [sds(32, 256)] * 4, [own] + others)
    pieces = [pieces[0]] + [fetch(pieces[i], dx=-d) for i, d in ((1, 1), (2, -1), (3, 2))]
    pieces = [pieces[0], pieces[2], pieces[1], pieces[3]]
    return call(place, sds(128, 256), [where] + pieces, smem=(0,))


def solution(mesh):
    return jax.shard_map(
        shards,
        mesh=mesh,
        in_specs=(
            P("ctx", "head"),
            P("ctx", "head"),
            P("ctx", "head"),
            P("ctx", "head"),
            P("ctx", "head"),
            P("ctx"),
            P("ctx"),
            P("head", "ctx"),
        ),
        out_specs=P("head", "ctx"),
        check_vma=False,
    )
```

```python
import functools
import math

import jax
import jax.numpy as jnp
from jax import lax
from jax.experimental import pallas as pl
from jax.experimental.pallas import tpu as pltpu
from jax.sharding import PartitionSpec as P

BF = jnp.bfloat16
F32 = jnp.float32
HD = 128
GROUP = 8
HALF = 1024
META = 128
QW = GROUP * HD + 128
LOG2_SCALE = math.log2(math.e) / math.sqrt(HD)
NEG = -1e30


def call(body, out_shape, args, scratch=(), smem=(), idle=(), raw=(), flops=0, nbytes=0, vmem=8 << 20):
    args, specs = list(args), []
    for i in range(len(args)):
        if i in smem:
            specs.append(pl.BlockSpec(memory_space=pltpu.SMEM))
        elif i in raw:
            specs.append(pl.BlockSpec(memory_space=pltpu.HBM))
            args[i] = pltpu.with_memory_space_constraint(args[i], pltpu.HBM)
        elif i in idle:
            specs.append(pl.BlockSpec(memory_space=pl.ANY))
        else:
            specs.append(pl.BlockSpec(memory_space=pltpu.VMEM))
    return pl.pallas_call(
        body,
        out_shape=out_shape,
        in_specs=specs,
        out_specs=jax.tree.map(lambda _: pl.BlockSpec(memory_space=pltpu.VMEM), out_shape),
        scratch_shapes=list(scratch),
        cost_estimate=pl.CostEstimate(flops=flops, bytes_accessed=nbytes, transcendentals=0),
        compiler_params=pltpu.CompilerParams(vmem_limit_bytes=vmem),
    )(*args)


def near(*shape, dtype=BF):
    return pltpu.VMEM(shape, dtype)


def sds(*shape, dtype=BF):
    return jax.ShapeDtypeStruct(shape, dtype)


def pack(len_ref, q_hbm, k_hbm, v_hbm, sk_hbm, sv_hbm, pos_hbm, tile_ref, out_ref, k_ref, v_ref, pos_ref, sems):
    meta = 2 * HALF
    copies = [
        pltpu.make_async_copy(k_hbm, k_ref, sems.at[0]),
        pltpu.make_async_copy(v_hbm, v_ref, sems.at[1]),
        pltpu.make_async_copy(sk_hbm, out_ref.at[meta : meta + 32], sems.at[2]),
        pltpu.make_async_copy(sv_hbm, out_ref.at[meta + 32 : meta + 64], sems.at[3]),
        pltpu.make_async_copy(q_hbm, tile_ref.at[:, : GROUP * HD], sems.at[4]),
    ]
    pos_copy = pltpu.make_async_copy(pos_hbm, pos_ref, sems.at[5])
    pos_copy.start()
    for copy in copies:
        copy.start()
    pos_copy.wait()
    pos = jnp.broadcast_to(pos_ref[...], (32, 32))
    row = lax.broadcasted_iota(jnp.int32, (32, 32), 0)
    col = lax.broadcasted_iota(jnp.int32, (32, 32), 1)
    column = jnp.sum(jnp.where(row == col, pos, 0), axis=1, keepdims=True)
    lane = lax.broadcasted_iota(jnp.int32, (32, 128), 1)
    numbers = jnp.where(lane == 0, column // 32, jnp.where(lane == 1, column % 32, 0))
    tile_ref[:, GROUP * HD :] = numbers.astype(F32).astype(BF)
    for copy in copies:
        copy.wait()
    used = len_ref[0]
    first = jnp.broadcast_to(k_ref[0:1, :].astype(F32), (HD, HD))
    for half in range(2):
        base = half * (2 * HALF + META)
        for block in range(HALF // HD):
            start = half * HALF + block * HD
            seen = lax.broadcasted_iota(jnp.int32, (HD, HD), 0) + start < used
            keys = jnp.where(seen, k_ref[start : start + HD, :].astype(F32), first)
            out_ref[base + block * HD : base + (block + 1) * HD, :] = keys.astype(BF)
            values = jnp.where(seen, v_ref[start : start + HD, :].astype(F32), 0.0)
            out_ref[base + HALF + block * HD : base + HALF + (block + 1) * HD, :] = values.astype(BF)
    pos = jnp.concatenate([pos_ref[...], jnp.zeros((1, 96), jnp.int32)], axis=1)
    pos = jnp.broadcast_to(pos, (64, HD))
    row = lax.broadcasted_iota(jnp.int32, (64, HD), 0)
    lane = lax.broadcasted_iota(jnp.int32, (64, HD), 1)
    extent = jnp.where(lane == 0, used // 32, jnp.where(lane == 1, used % 32, 0))
    numbers = jnp.where(row == 0, pos // 32, jnp.where(row == 1, pos % 32, jnp.where(row == 2, extent, 0)))
    out_ref[meta + 64 : meta + 128, :] = numbers.astype(F32).astype(BF)


def pair(a_ref, b_ref, out_ref):
    out_ref[0:32, :] = a_ref[...]
    out_ref[32:64, :] = b_ref[...]


def attend(layout, span, n_carry, picks, unit, n_tiles, n_idle, has_weight, *refs):
    last, first = picks is not None, n_carry == 0
    refs = list(refs)
    take = lambda n: [refs.pop(0) for _ in range(n)]
    tiles, kvs, spans = take(n_tiles), take(len(layout)), take(3 if span else 0)
    accs_in, sts_in = take(n_carry), take(n_carry)
    w_in = take(int(has_weight))
    take(n_idle)
    if last:
        outs = take(len(picks))
    else:
        acc_out, st_out = take(2)
        for kv in kvs:
            refs.pop(0)[...] = kv[2 * HALF : 2 * HALF + META, :]
    for w in w_in:
        refs.pop(0)[...] = w[...]
    v2, score_a, score_b = refs
    rows = 64 * n_tiles

    def carried(parts, cols):
        if not last:
            return jnp.concatenate([ref[:, cols] for ref in parts], axis=0)
        return jnp.concatenate([parts[0][64 * i : 64 * (i + 1), cols] for i in picks], axis=0)

    blocks = []
    at = 0
    for i, (holder, pieces) in enumerate(layout):
        numbers = kvs[holder][2 * HALF + 64 : 2 * HALF + 80, :].astype(F32)
        used = numbers[2:3, 0:1] * 32.0 + numbers[2:3, 1:2]
        for start, cache_row in pieces:
            v2[at : at + HALF, :HD] = kvs[i][start + HALF : start + 2 * HALF, :]
            index = lax.broadcasted_iota(jnp.int32, (HALF, HD), 0) + cache_row
            v2[at : at + HALF, HD:] = jnp.where(index.astype(F32) < used, 1.0, 0.0).astype(BF)
            blocks += [(at + c, 256, kvs[i], start + c) for c in range(0, HALF, 256)]
            at += HALF
    if span:
        near = [s[...] for s in spans] + [kvs[0][2 * HALF : 2 * HALF + META, :]]
        span_keys = jnp.concatenate([s[0:32, :] for s in near], axis=0)
        for i, s in enumerate(near):
            v2[at + 32 * i : at + 32 * (i + 1), :HD] = s[32:64, :]
        v2[at : at + HD, HD:] = jnp.ones((HD, HD), BF)
        near = [s[64:80, :].astype(F32) for s in near]
        key_pos = jnp.concatenate([s[0:1, 0:32] * 32.0 + s[1:2, 0:32] for s in near], axis=1)
        numbers = jnp.concatenate([t[:, GROUP * HD :] for t in tiles], axis=0).astype(F32)
        query_pos = numbers[:, 0:1] * 32.0 + numbers[:, 1:2]
        seen = key_pos <= query_pos
        blocks.append((at, HD, None, 0))
    if span:
        seen = jnp.concatenate([seen] * unit, axis=0)
    lane = lax.broadcasted_iota(jnp.int32, (rows, HD), 1)
    st = jnp.zeros((rows, HD), F32) if first else carried(sts_in, slice(0, HD))
    new_st = jnp.zeros((rows, HD), F32)
    peak = None
    for step in range(GROUP // unit + 1):
        mine, previous = (score_a, score_b) if step % 2 == 0 else (score_b, score_a)
        heads = range(step * unit, (step + 1) * unit)
        if step < GROUP // unit:
            query = jnp.concatenate([t[:, h * HD : (h + 1) * HD] for h in heads for t in tiles], axis=0)
        top = None
        acc = None
        for c, width, kv, row in blocks:
            if step < GROUP // unit:
                keys = span_keys if kv is None else kv[row : row + width, :]
                s = lax.dot_general(query, keys, (((1,), (1,)), ((), ())), preferred_element_type=F32)
                s = s * LOG2_SCALE
                if kv is None:
                    s = jnp.where(seen, s, NEG)
                mine[:, c : c + width] = s
                for i in range(0, width, HD):
                    top = s[:, i : i + HD] if top is None else jnp.maximum(top, s[:, i : i + HD])
            if step > 0:
                p = jnp.exp2(previous[:, c : c + width] - peak).astype(BF)
                term = jnp.dot(p, v2[c : c + width, :], preferred_element_type=F32)
                acc = term if acc is None else acc + term
        if step > 0:
            for u in range(unit):
                h = (step - 1) * unit + u
                part = slice(u * rows, (u + 1) * rows)
                cols = slice(h * HD, (h + 1) * HD)
                total, weight, shift = acc[part, :HD], acc[part, HD:], peak[part, :]
                if not first:
                    rescale = jnp.exp2(st[:, h : h + 1] - shift)
                    total = total + carried(accs_in, cols) * rescale
                    weight = weight + st[:, GROUP + h : GROUP + h + 1] * rescale
                new_st = jnp.where(lane == h, jnp.broadcast_to(shift, (rows, HD)), new_st)
                new_st = jnp.where(lane == GROUP + h, weight, new_st)
                if last:
                    for i, out in enumerate(outs):
                        out[:, cols] = total[64 * i : 64 * (i + 1), :].astype(BF)
                else:
                    acc_out[:, cols] = total
        if step < GROUP // unit:
            peak = jnp.max(top, axis=1, keepdims=True).astype(BF).astype(F32)
            if not first:
                peak = jnp.maximum(peak, jnp.concatenate([st[:, h : h + 1] for h in heads], axis=0))
    if last:
        high = new_st.astype(BF).astype(F32)
        low = pltpu.roll(new_st - high, GROUP, 1)
        packed = jnp.where(lane < 2 * GROUP, high, jnp.where(lane < 3 * GROUP, low, 0.0)).astype(BF)
        for i, out in enumerate(outs):
            out[:, GROUP * HD :] = packed[64 * i : 64 * (i + 1), :]
    else:
        st_out[...] = new_st


def attend_call(tiles, kvs, layout, spans=(), accs=(), sts=(), weight=None, idle=(), picks=None, unit=1):
    n_keys = HALF * sum(len(p) for _, p in layout) + (HD if spans else 0)
    rows = 64 * len(tiles)
    handed = [] if weight is None else [weight]
    args = list(tiles) + list(kvs) + list(spans) + list(accs) + list(sts) + handed + list(idle)
    if picks is not None:
        out = [sds(64, QW) for _ in picks]
    else:
        out = [sds(rows, GROUP * HD, dtype=F32), sds(rows, HD, dtype=F32)] + [sds(META, HD) for _ in kvs]
    out += [sds(*w.shape) for w in handed]
    return call(
        functools.partial(
            attend, layout, bool(spans), len(accs), picks, unit, len(tiles), len(idle), weight is not None
        ),
        out,
        args,
        scratch=[
            pltpu.VMEM((n_keys, 2 * HD), BF),
            pltpu.VMEM((rows * unit, n_keys), F32),
            pltpu.VMEM((rows * unit, n_keys), F32),
        ],
        idle=range(len(args) - len(idle), len(args)),
        flops=rows * GROUP * n_keys * HD * 8,
        nbytes=4 << 20,
        vmem=24 << 20,
    )


def join(messages, final):
    stats = [m[:, GROUP * HD :].astype(F32) for m in messages]
    sums, peaks, weights = [], [], []
    for h in range(GROUP):
        each = [s[:, h : h + 1] for s in stats]
        peak = functools.reduce(jnp.maximum, each)
        scales = [jnp.exp2(p - peak) for p in each]
        weight = sum(
            (s[:, GROUP + h : GROUP + h + 1] + s[:, 2 * GROUP + h : 2 * GROUP + h + 1]) * c
            for s, c in zip(stats, scales)
        )
        total = sum(m[:, h * HD : (h + 1) * HD].astype(F32) * c for m, c in zip(messages, scales))
        sums.append(total / weight if final else total)
        peaks.append(peak)
        weights.append(weight)
    return sums, peaks, weights


def join_x(a_ref, b_ref, c_ref, d_ref, out_ref):
    messages = [r[...] for r in (a_ref, b_ref, c_ref, d_ref)]
    sums, peaks, weights = join(messages, False)
    lane = lax.broadcasted_iota(jnp.int32, (64, HD), 1)
    numbers = jnp.zeros((64, HD), F32)
    for h in range(GROUP):
        out_ref[:, h * HD : (h + 1) * HD] = sums[h].astype(BF)
        high = weights[h].astype(BF).astype(F32)
        numbers = jnp.where(lane == h, peaks[h], numbers)
        numbers = jnp.where(lane == GROUP + h, high, numbers)
        numbers = jnp.where(lane == 2 * GROUP + h, weights[h] - high, numbers)
    out_ref[:, GROUP * HD :] = numbers.astype(BF)


def join_z(own_ref, other_ref, _, out_ref):
    other = jnp.concatenate([other_ref[32:64, :], other_ref[0:32, :]], axis=0)
    sums, _, _ = join([own_ref[...], other], True)
    for h in range(GROUP):
        out_ref[:, h * HD : (h + 1) * HD] = sums[h].astype(BF)


def project(where_ref, a0, a1, a2, a3, w0, w1, w2, w3, keep_ref, send_ref, rows_ref):
    z, y, core = where_ref[0], where_ref[1], where_ref[2]
    for a, dy in zip((a0, a1, a2, a3), (0, 1, 3, 2)):
        there = lax.rem(y + dy, 4)
        other = lax.rem(there + core, 2)
        for part in range(2):
            z_there = z if part == 0 else 1 - z
            slot = pl.multiple_of((other * 4 + z_there * 2 + there // 2) * 32, 32)
            rows_ref[pl.ds(slot, 32), :] = a[32 * part : 32 * (part + 1), :]
    for i, w in enumerate((w0, w1, w2, w3)):
        out = jnp.dot(rows_ref[...], w[...], preferred_element_type=F32).astype(BF)
        keep_ref[:, i * 256 : (i + 1) * 256] = out[:128, :]
        send_ref[:, i * 256 : (i + 1) * 256] = out[128:, :]


def add_cores(where_ref, keep_ref, got_ref, own_ref, o1, o2, o3):
    z_lo = where_ref[3]
    for k, out in enumerate((own_ref, o1, o2, o3)):
        slot = pl.multiple_of((z_lo ^ k) * 32, 32)
        out[...] = (keep_ref[pl.ds(slot, 32), :].astype(F32) + got_ref[pl.ds(slot, 32), :].astype(F32)).astype(BF)


def add_z(a_ref, b_ref, c_ref, d_ref, o0, o1, o2, o3):
    total = sum(r[...].astype(F32) for r in (a_ref, b_ref, c_ref, d_ref)).astype(BF)
    for i, out in enumerate((o0, o1, o2, o3)):
        out[...] = total[:, i * 256 : (i + 1) * 256]


def place(where_ref, a_ref, b_ref, c_ref, d_ref, out_ref):
    x = where_ref[4]
    for dx, r in zip((0, 1, 3, 2), (a_ref, b_ref, c_ref, d_ref)):
        slot = pl.multiple_of(lax.rem(x + dx, 4) * 32, 32)
        out_ref[pl.ds(slot, 32), :] = r[...]


def ctx_shift(dz, dy, dx):
    pairs = []
    for c in range(32):
        z, y, x = c // 16, (c // 4) % 4, c % 4
        pairs.append((c, ((z + dz) % 2) * 16 + ((y + dy) % 4) * 4 + (x + dx) % 4))
    return pairs


def fetch(value, dz=0, dy=0, dx=0):
    return lax.ppermute(value, "ctx", ctx_shift(-dz, -dy, -dx))


def shards(queries, cache_keys, cache_values, span_keys, span_values, prefix_len, positions, out_weight):
    index = lax.axis_index("ctx")
    head = lax.axis_index("head")
    where = jnp.stack([index // 16, (index // 4) % 4, head % 2, head // 2, index % 4]).astype(jnp.int32)
    pos_row = positions.reshape(1, 32)
    tile, kv = call(
        pack,
        [near(32, QW), near(4 * HALF + META, HD)],
        [prefix_len, queries, cache_keys, cache_values, span_keys, span_values, pos_row],
        scratch=[
            pltpu.VMEM((2 * HALF, HD), BF),
            pltpu.VMEM((2 * HALF, HD), BF),
            pltpu.VMEM((1, 32), jnp.int32),
            pltpu.SemaphoreType.DMA((6,)),
        ],
        smem=(0,),
        raw=(1, 2, 3, 4, 5, 6),
    )
    kv_up = fetch(kv, dy=1)
    kv_down = fetch(kv, dy=-1)
    own = call(pair, sds(64, QW), [tile, fetch(tile, dz=1)])
    far = fetch(own, dx=2)
    tiles = [own, fetch(own, dx=1), fetch(own, dx=-1), far]

    cut = 2 * HALF + META
    whole = [(0, 0), (cut, HALF)]
    acc_a, st_a, span = attend_call(tiles[:1], [kv], [(0, whole)], unit=4)
    acc_b, st_b, _ = attend_call(tiles[1:], [kv], [(0, whole)])
    far_a = fetch(kv_up[:cut], dy=1)
    far_b = fetch(kv_down[cut:], dy=-1)
    acc, st, *spans = attend_call(
        tiles, [kv_up, kv_down], [(0, whole), (1, whole)], accs=[acc_a, acc_b], sts=[st_a, st_b]
    )

    def finish(picks, unit, idle=(), weight=None):
        return attend_call(
            [tiles[i] for i in picks],
            [far_a, far_b],
            [(0, [(0, 0)]), (0, [(0, HALF)])],
            spans=[span] + spans,
            accs=[acc],
            sts=[st],
            weight=weight,
            idle=idle,
            picks=picks,
            unit=unit,
        )

    part_3, part_1, part_2 = finish((3, 1, 2), 2)
    got_3, got_1, got_2 = fetch(part_3, dx=-2), fetch(part_1, dx=-1), fetch(part_2, dx=1)
    part_0, weight = finish((0,), 4, idle=[part_3], weight=out_weight)
    weights = [out_weight, fetch(weight, dx=1), fetch(weight, dx=-1), fetch(weight, dx=2)]
    joined = call(join_x, sds(64, QW), [part_0, got_1, got_2, got_3])
    attended = call(join_z, sds(64, GROUP * HD), [joined, fetch(joined, dz=1), weights[1]], idle=(2,))
    rows = [attended] + [fetch(attended, dy=d) for d in (1, -1, 2)]
    keep, send = call(
        project,
        [sds(128, 1024), sds(128, 1024)],
        [where] + rows + weights,
        scratch=[pltpu.VMEM((256, 1024), BF)],
        smem=(0,),
        flops=2 * 256 * 1024 * 1024,
        nbytes=4 << 20,
    )
    got = lax.ppermute(send, "head", [(h, h ^ 1) for h in range(8)])
    own, *others = call(add_cores, [sds(32, 1024)] * 4, [where, keep, got], smem=(0,))
    others = [lax.ppermute(o, "head", [(h, h ^ (2 * k)) for h in range(8)]) for k, o in zip((1, 2, 3), others)]
    pieces = call(add_z, [sds(32, 256)] * 4, [own] + others)
    pieces = [pieces[0]] + [fetch(pieces[i], dx=-d) for i, d in ((1, 1), (2, -1), (3, 2))]
    pieces = [pieces[0], pieces[2], pieces[1], pieces[3]]
    return call(place, sds(128, 256), [where] + pieces, smem=(0,))


def solution(mesh):
    return jax.shard_map(
        shards,
        mesh=mesh,
        in_specs=(
            P("ctx", "head"),
            P("ctx", "head"),
            P("ctx", "head"),
            P("ctx", "head"),
            P("ctx", "head"),
            P("ctx"),
            P("ctx"),
            P("head", "ctx"),
        ),
        out_specs=P("head", "ctx"),
        check_vma=False,
    )
```

```python
import functools
import math

import jax
import jax.numpy as jnp
from jax import lax
from jax.experimental import pallas as pl
from jax.experimental.pallas import tpu as pltpu
from jax.sharding import PartitionSpec as P

BF = jnp.bfloat16
F32 = jnp.float32
HD = 128
GROUP = 8
HALF = 1024
META = 128
QW = GROUP * HD + 128
LOG2_SCALE = math.log2(math.e) / math.sqrt(HD)
NEG = -1e30


def call(body, out_shape, args, scratch=(), smem=(), idle=(), raw=(), flops=0, nbytes=0, vmem=8 << 20):
    args, specs = list(args), []
    for i in range(len(args)):
        if i in smem:
            specs.append(pl.BlockSpec(memory_space=pltpu.SMEM))
        elif i in raw:
            specs.append(pl.BlockSpec(memory_space=pltpu.HBM))
            args[i] = pltpu.with_memory_space_constraint(args[i], pltpu.HBM)
        elif i in idle:
            specs.append(pl.BlockSpec(memory_space=pl.ANY))
        else:
            specs.append(pl.BlockSpec(memory_space=pltpu.VMEM))
    return pl.pallas_call(
        body,
        out_shape=out_shape,
        in_specs=specs,
        out_specs=jax.tree.map(lambda _: pl.BlockSpec(memory_space=pltpu.VMEM), out_shape),
        scratch_shapes=list(scratch),
        cost_estimate=pl.CostEstimate(flops=flops, bytes_accessed=nbytes, transcendentals=0),
        compiler_params=pltpu.CompilerParams(vmem_limit_bytes=vmem),
    )(*args)


def near(*shape, dtype=BF):
    return pltpu.VMEM(shape, dtype)


def sds(*shape, dtype=BF):
    return jax.ShapeDtypeStruct(shape, dtype)


def pack(len_ref, q_hbm, k_hbm, v_hbm, sk_hbm, sv_hbm, pos_hbm, tile_ref, out_ref, k_ref, v_ref, pos_ref, sems):
    meta = 2 * HALF
    copies = [
        pltpu.make_async_copy(k_hbm, k_ref, sems.at[0]),
        pltpu.make_async_copy(v_hbm, v_ref, sems.at[1]),
        pltpu.make_async_copy(sk_hbm, out_ref.at[meta : meta + 32], sems.at[2]),
        pltpu.make_async_copy(sv_hbm, out_ref.at[meta + 32 : meta + 64], sems.at[3]),
        pltpu.make_async_copy(q_hbm, tile_ref.at[:, : GROUP * HD], sems.at[4]),
    ]
    pos_copy = pltpu.make_async_copy(pos_hbm, pos_ref, sems.at[5])
    pos_copy.start()
    for copy in copies:
        copy.start()
    pos_copy.wait()
    pos = jnp.broadcast_to(pos_ref[...], (32, 32))
    row = lax.broadcasted_iota(jnp.int32, (32, 32), 0)
    col = lax.broadcasted_iota(jnp.int32, (32, 32), 1)
    column = jnp.sum(jnp.where(row == col, pos, 0), axis=1, keepdims=True)
    lane = lax.broadcasted_iota(jnp.int32, (32, 128), 1)
    numbers = jnp.where(lane == 0, column // 32, jnp.where(lane == 1, column % 32, 0))
    tile_ref[:, GROUP * HD :] = numbers.astype(F32).astype(BF)
    for copy in copies:
        copy.wait()
    used = len_ref[0]
    first = jnp.broadcast_to(k_ref[0:1, :].astype(F32), (HD, HD))
    for half in range(2):
        base = half * (2 * HALF + META)
        for block in range(HALF // HD):
            start = half * HALF + block * HD
            seen = lax.broadcasted_iota(jnp.int32, (HD, HD), 0) + start < used
            keys = jnp.where(seen, k_ref[start : start + HD, :].astype(F32), first)
            out_ref[base + block * HD : base + (block + 1) * HD, :] = keys.astype(BF)
            values = jnp.where(seen, v_ref[start : start + HD, :].astype(F32), 0.0)
            out_ref[base + HALF + block * HD : base + HALF + (block + 1) * HD, :] = values.astype(BF)
    pos = jnp.concatenate([pos_ref[...], jnp.zeros((1, 96), jnp.int32)], axis=1)
    pos = jnp.broadcast_to(pos, (64, HD))
    row = lax.broadcasted_iota(jnp.int32, (64, HD), 0)
    lane = lax.broadcasted_iota(jnp.int32, (64, HD), 1)
    extent = jnp.where(lane == 0, used // 32, jnp.where(lane == 1, used % 32, 0))
    numbers = jnp.where(row == 0, pos // 32, jnp.where(row == 1, pos % 32, jnp.where(row == 2, extent, 0)))
    out_ref[meta + 64 : meta + 128, :] = numbers.astype(F32).astype(BF)


def pair(a_ref, b_ref, out_ref):
    out_ref[0:32, :] = a_ref[...]
    out_ref[32:64, :] = b_ref[...]


def attend(layout, span, n_carry, picks, unit, n_tiles, n_idle, has_weight, *refs):
    last, first = picks is not None, n_carry == 0
    refs = list(refs)
    take = lambda n: [refs.pop(0) for _ in range(n)]
    tiles, kvs, spans = take(n_tiles), take(len(layout)), take(3 if span else 0)
    accs_in, sts_in = take(n_carry), take(n_carry)
    w_in = take(int(has_weight))
    take(n_idle)
    if last:
        outs = take(len(picks))
    else:
        acc_out, st_out = take(2)
        for kv in kvs:
            refs.pop(0)[...] = kv[2 * HALF : 2 * HALF + META, :]
    for w in w_in:
        refs.pop(0)[...] = w[...]
    v2, score_a, score_b = refs
    rows = 64 * n_tiles

    def carried(parts, cols):
        if not last:
            return jnp.concatenate([ref[:, cols] for ref in parts], axis=0)
        return jnp.concatenate([parts[0][64 * i : 64 * (i + 1), cols] for i in picks], axis=0)

    blocks = []
    at = 0
    for i, (holder, pieces) in enumerate(layout):
        numbers = kvs[holder][2 * HALF + 64 : 2 * HALF + 80, :].astype(F32)
        used = numbers[2:3, 0:1] * 32.0 + numbers[2:3, 1:2]
        for start, cache_row in pieces:
            v2[at : at + HALF, :HD] = kvs[i][start + HALF : start + 2 * HALF, :]
            index = lax.broadcasted_iota(jnp.int32, (HALF, HD), 0) + cache_row
            v2[at : at + HALF, HD:] = jnp.where(index.astype(F32) < used, 1.0, 0.0).astype(BF)
            blocks += [(at + c, 256, kvs[i], start + c) for c in range(0, HALF, 256)]
            at += HALF
    if span:
        near = [s[...] for s in spans] + [kvs[0][2 * HALF : 2 * HALF + META, :]]
        span_keys = jnp.concatenate([s[0:32, :] for s in near], axis=0)
        for i, s in enumerate(near):
            v2[at + 32 * i : at + 32 * (i + 1), :HD] = s[32:64, :]
        v2[at : at + HD, HD:] = jnp.ones((HD, HD), BF)
        near = [s[64:80, :].astype(F32) for s in near]
        key_pos = jnp.concatenate([s[0:1, 0:32] * 32.0 + s[1:2, 0:32] for s in near], axis=1)
        numbers = jnp.concatenate([t[:, GROUP * HD :] for t in tiles], axis=0).astype(F32)
        query_pos = numbers[:, 0:1] * 32.0 + numbers[:, 1:2]
        seen = key_pos <= query_pos
        blocks.append((at, HD, None, 0))
    if span:
        seen = jnp.concatenate([seen] * unit, axis=0)
    lane = lax.broadcasted_iota(jnp.int32, (rows, HD), 1)
    st = jnp.zeros((rows, HD), F32) if first else carried(sts_in, slice(0, HD))
    new_st = jnp.zeros((rows, HD), F32)
    peak = None
    for step in range(GROUP // unit + 1):
        mine, previous = (score_a, score_b) if step % 2 == 0 else (score_b, score_a)
        heads = range(step * unit, (step + 1) * unit)
        if step < GROUP // unit:
            query = jnp.concatenate([t[:, h * HD : (h + 1) * HD] for h in heads for t in tiles], axis=0)
        top = None
        acc = None
        for c, width, kv, row in blocks:
            if step < GROUP // unit:
                keys = span_keys if kv is None else kv[row : row + width, :]
                s = lax.dot_general(query, keys, (((1,), (1,)), ((), ())), preferred_element_type=F32)
                s = s * LOG2_SCALE
                if kv is None:
                    s = jnp.where(seen, s, NEG)
                mine[:, c : c + width] = s
                for i in range(0, width, HD):
                    top = s[:, i : i + HD] if top is None else jnp.maximum(top, s[:, i : i + HD])
            if step > 0:
                p = jnp.exp2(previous[:, c : c + width] - peak).astype(BF)
                term = jnp.dot(p, v2[c : c + width, :], preferred_element_type=F32)
                acc = term if acc is None else acc + term
        if step > 0:
            for u in range(unit):
                h = (step - 1) * unit + u
                part = slice(u * rows, (u + 1) * rows)
                cols = slice(h * HD, (h + 1) * HD)
                total, weight, shift = acc[part, :HD], acc[part, HD:], peak[part, :]
                if not first:
                    rescale = jnp.exp2(st[:, h : h + 1] - shift)
                    total = total + carried(accs_in, cols) * rescale
                    weight = weight + st[:, GROUP + h : GROUP + h + 1] * rescale
                new_st = jnp.where(lane == h, jnp.broadcast_to(shift, (rows, HD)), new_st)
                new_st = jnp.where(lane == GROUP + h, weight, new_st)
                if last:
                    for i, out in enumerate(outs):
                        out[:, cols] = total[64 * i : 64 * (i + 1), :].astype(BF)
                else:
                    acc_out[:, cols] = total
        if step < GROUP // unit:
            peak = jnp.max(top, axis=1, keepdims=True).astype(BF).astype(F32)
            if not first:
                peak = jnp.maximum(peak, jnp.concatenate([st[:, h : h + 1] for h in heads], axis=0))
    if last:
        high = new_st.astype(BF).astype(F32)
        low = pltpu.roll(new_st - high, GROUP, 1)
        packed = jnp.where(lane < 2 * GROUP, high, jnp.where(lane < 3 * GROUP, low, 0.0)).astype(BF)
        for i, out in enumerate(outs):
            out[:, GROUP * HD :] = packed[64 * i : 64 * (i + 1), :]
    else:
        st_out[...] = new_st


def attend_call(tiles, kvs, layout, spans=(), accs=(), sts=(), weight=None, idle=(), picks=None, unit=1):
    n_keys = HALF * sum(len(p) for _, p in layout) + (HD if spans else 0)
    rows = 64 * len(tiles)
    handed = [] if weight is None else [weight]
    args = list(tiles) + list(kvs) + list(spans) + list(accs) + list(sts) + handed + list(idle)
    if picks is not None:
        out = [sds(64, QW) for _ in picks]
    else:
        out = [sds(rows, GROUP * HD, dtype=F32), sds(rows, HD, dtype=F32)] + [sds(META, HD) for _ in kvs]
    out += [sds(*w.shape) for w in handed]
    return call(
        functools.partial(
            attend, layout, bool(spans), len(accs), picks, unit, len(tiles), len(idle), weight is not None
        ),
        out,
        args,
        scratch=[
            pltpu.VMEM((n_keys, 2 * HD), BF),
            pltpu.VMEM((rows * unit, n_keys), F32),
            pltpu.VMEM((rows * unit, n_keys), F32),
        ],
        idle=range(len(args) - len(idle), len(args)),
        flops=rows * GROUP * n_keys * HD * 8,
        nbytes=4 << 20,
        vmem=24 << 20,
    )


def join(messages, final):
    stats = [m[:, GROUP * HD :].astype(F32) for m in messages]
    sums, peaks, weights = [], [], []
    for h in range(GROUP):
        each = [s[:, h : h + 1] for s in stats]
        peak = functools.reduce(jnp.maximum, each)
        scales = [jnp.exp2(p - peak) for p in each]
        weight = sum(
            (s[:, GROUP + h : GROUP + h + 1] + s[:, 2 * GROUP + h : 2 * GROUP + h + 1]) * c
            for s, c in zip(stats, scales)
        )
        total = sum(m[:, h * HD : (h + 1) * HD].astype(F32) * c for m, c in zip(messages, scales))
        sums.append(total / weight if final else total)
        peaks.append(peak)
        weights.append(weight)
    return sums, peaks, weights


def join_x(a_ref, b_ref, c_ref, d_ref, out_ref):
    messages = [r[...] for r in (a_ref, b_ref, c_ref, d_ref)]
    sums, peaks, weights = join(messages, False)
    lane = lax.broadcasted_iota(jnp.int32, (64, HD), 1)
    numbers = jnp.zeros((64, HD), F32)
    for h in range(GROUP):
        out_ref[:, h * HD : (h + 1) * HD] = sums[h].astype(BF)
        high = weights[h].astype(BF).astype(F32)
        numbers = jnp.where(lane == h, peaks[h], numbers)
        numbers = jnp.where(lane == GROUP + h, high, numbers)
        numbers = jnp.where(lane == 2 * GROUP + h, weights[h] - high, numbers)
    out_ref[:, GROUP * HD :] = numbers.astype(BF)


def join_z(own_ref, other_ref, out_ref):
    other = jnp.concatenate([other_ref[32:64, :], other_ref[0:32, :]], axis=0)
    sums, _, _ = join([own_ref[...], other], True)
    for h in range(GROUP):
        out_ref[:, h * HD : (h + 1) * HD] = sums[h].astype(BF)


def project(where_ref, a0, a1, a2, a3, w_hbm, keep_ref, send_ref, rows_ref, w_ref, sems):
    z, y, core, x = where_ref[0], where_ref[1], where_ref[2], where_ref[4]
    copies = []
    for i, dx in enumerate((0, 1, 3, 2)):
        start = pl.multiple_of(lax.rem(x + dx, 4) * 1024, 1024)
        copies.append(pltpu.make_async_copy(w_hbm.at[pl.ds(start, 1024)], w_ref.at[i], sems.at[i]))
        copies[i].start()
    for a, dy in zip((a0, a1, a2, a3), (0, 1, 3, 2)):
        there = lax.rem(y + dy, 4)
        other = lax.rem(there + core, 2)
        for part in range(2):
            z_there = z if part == 0 else 1 - z
            slot = pl.multiple_of((other * 4 + z_there * 2 + there // 2) * 32, 32)
            rows_ref[pl.ds(slot, 32), :] = a[32 * part : 32 * (part + 1), :]
    for i, copy in enumerate(copies):
        copy.wait()
        out = jnp.dot(rows_ref[...], w_ref[i], preferred_element_type=F32).astype(BF)
        keep_ref[:, i * 256 : (i + 1) * 256] = out[:128, :]
        send_ref[:, i * 256 : (i + 1) * 256] = out[128:, :]


def add_cores(where_ref, keep_ref, got_ref, own_ref, o1, o2, o3):
    z_lo = where_ref[3]
    for k, out in enumerate((own_ref, o1, o2, o3)):
        slot = pl.multiple_of((z_lo ^ k) * 32, 32)
        out[...] = (keep_ref[pl.ds(slot, 32), :].astype(F32) + got_ref[pl.ds(slot, 32), :].astype(F32)).astype(BF)


def add_z(a_ref, b_ref, c_ref, d_ref, o0, o1, o2, o3):
    total = sum(r[...].astype(F32) for r in (a_ref, b_ref, c_ref, d_ref)).astype(BF)
    for i, out in enumerate((o0, o1, o2, o3)):
        out[...] = total[:, i * 256 : (i + 1) * 256]


def place(where_ref, a_ref, b_ref, c_ref, d_ref, out_ref):
    x = where_ref[4]
    for dx, r in zip((0, 1, 3, 2), (a_ref, b_ref, c_ref, d_ref)):
        slot = pl.multiple_of(lax.rem(x + dx, 4) * 32, 32)
        out_ref[pl.ds(slot, 32), :] = r[...]


def ctx_shift(dz, dy, dx):
    pairs = []
    for c in range(32):
        z, y, x = c // 16, (c // 4) % 4, c % 4
        pairs.append((c, ((z + dz) % 2) * 16 + ((y + dy) % 4) * 4 + (x + dx) % 4))
    return pairs


def fetch(value, dz=0, dy=0, dx=0):
    return lax.ppermute(value, "ctx", ctx_shift(-dz, -dy, -dx))


def shards(queries, cache_keys, cache_values, span_keys, span_values, prefix_len, positions, out_weight):
    index = lax.axis_index("ctx")
    head = lax.axis_index("head")
    where = jnp.stack([index // 16, (index // 4) % 4, head % 2, head // 2, index % 4]).astype(jnp.int32)
    pos_row = positions.reshape(1, 32)
    tile, kv = call(
        pack,
        [near(32, QW), near(4 * HALF + META, HD)],
        [prefix_len, queries, cache_keys, cache_values, span_keys, span_values, pos_row],
        scratch=[
            pltpu.VMEM((2 * HALF, HD), BF),
            pltpu.VMEM((2 * HALF, HD), BF),
            pltpu.VMEM((1, 32), jnp.int32),
            pltpu.SemaphoreType.DMA((6,)),
        ],
        smem=(0,),
        raw=(1, 2, 3, 4, 5, 6),
    )
    kv_up = fetch(kv, dy=1)
    kv_down = fetch(kv, dy=-1)
    own = call(pair, sds(64, QW), [tile, fetch(tile, dz=1)])
    far = fetch(own, dx=2)
    tiles = [own, fetch(own, dx=1), fetch(own, dx=-1), far]

    cut = 2 * HALF + META
    whole = [(0, 0), (cut, HALF)]
    acc_a, st_a, span, weight = attend_call(tiles[:1], [kv], [(0, whole)], weight=out_weight, unit=4)
    groups = [[4 * row + x for x in range(4)] for row in range(8)]
    weights = lax.all_gather(weight, "ctx", axis=0, tiled=True, axis_index_groups=groups)
    acc_b, st_b, _ = attend_call(tiles[1:], [kv], [(0, whole)])
    far_a = fetch(kv_up[:cut], dy=1)
    far_b = fetch(kv_down[cut:], dy=-1)
    acc, st, *spans = attend_call(
        tiles, [kv_up, kv_down], [(0, whole), (1, whole)], accs=[acc_a, acc_b], sts=[st_a, st_b]
    )

    def finish(picks, unit, idle=()):
        return attend_call(
            [tiles[i] for i in picks],
            [far_a, far_b],
            [(0, [(0, 0)]), (0, [(0, HALF)])],
            spans=[span] + spans,
            accs=[acc],
            sts=[st],
            idle=idle,
            picks=picks,
            unit=unit,
        )

    part_3, part_1, part_2 = finish((3, 1, 2), 2)
    got_3, got_1, got_2 = fetch(part_3, dx=-2), fetch(part_1, dx=-1), fetch(part_2, dx=1)
    (part_0,) = finish((0,), 4, idle=[part_3])
    joined = call(join_x, sds(64, QW), [part_0, got_1, got_2, got_3])
    attended = call(join_z, sds(64, GROUP * HD), [joined, fetch(joined, dz=1)])
    rows = [attended] + [fetch(attended, dy=d) for d in (1, -1, 2)]
    keep, send = call(
        project,
        [sds(128, 1024), sds(128, 1024)],
        [where] + rows + [weights],
        scratch=[
            pltpu.VMEM((256, 1024), BF),
            pltpu.VMEM((4, 1024, 256), BF),
            pltpu.SemaphoreType.DMA((4,)),
        ],
        smem=(0,),
        raw=(5,),
        flops=2 * 256 * 1024 * 1024,
        nbytes=4 << 20,
    )
    got = lax.ppermute(send, "head", [(h, h ^ 1) for h in range(8)])
    own, *others = call(add_cores, [sds(32, 1024)] * 4, [where, keep, got], smem=(0,))
    others = [lax.ppermute(o, "head", [(h, h ^ (2 * k)) for h in range(8)]) for k, o in zip((1, 2, 3), others)]
    pieces = call(add_z, [sds(32, 256)] * 4, [own] + others)
    pieces = [pieces[0]] + [fetch(pieces[i], dx=-d) for i, d in ((1, 1), (2, -1), (3, 2))]
    pieces = [pieces[0], pieces[2], pieces[1], pieces[3]]
    return call(place, sds(128, 256), [where] + pieces, smem=(0,))


def solution(mesh):
    return jax.shard_map(
        shards,
        mesh=mesh,
        in_specs=(
            P("ctx", "head"),
            P("ctx", "head"),
            P("ctx", "head"),
            P("ctx", "head"),
            P("ctx", "head"),
            P("ctx"),
            P("ctx"),
            P("head", "ctx"),
        ),
        out_specs=P("head", "ctx"),
        check_vma=False,
    )
```

```python
import functools
import math

import jax
import jax.numpy as jnp
from jax import lax
from jax.experimental import pallas as pl
from jax.experimental.pallas import tpu as pltpu
from jax.sharding import PartitionSpec as P

BF = jnp.bfloat16
F32 = jnp.float32
HD = 128
GROUP = 8
HALF = 1024
META = 128
QW = GROUP * HD + 128
LOG2_SCALE = math.log2(math.e) / math.sqrt(HD)
NEG = -1e30


def call(body, out_shape, args, scratch=(), smem=(), idle=(), raw=(), flops=0, nbytes=0, vmem=8 << 20):
    args, specs = list(args), []
    for i in range(len(args)):
        if i in smem:
            specs.append(pl.BlockSpec(memory_space=pltpu.SMEM))
        elif i in raw:
            specs.append(pl.BlockSpec(memory_space=pltpu.HBM))
            args[i] = pltpu.with_memory_space_constraint(args[i], pltpu.HBM)
        elif i in idle:
            specs.append(pl.BlockSpec(memory_space=pl.ANY))
        else:
            specs.append(pl.BlockSpec(memory_space=pltpu.VMEM))
    return pl.pallas_call(
        body,
        out_shape=out_shape,
        in_specs=specs,
        out_specs=jax.tree.map(lambda _: pl.BlockSpec(memory_space=pltpu.VMEM), out_shape),
        scratch_shapes=list(scratch),
        cost_estimate=pl.CostEstimate(flops=flops, bytes_accessed=nbytes, transcendentals=0),
        compiler_params=pltpu.CompilerParams(vmem_limit_bytes=vmem),
    )(*args)


def near(*shape, dtype=BF):
    return pltpu.VMEM(shape, dtype)


def sds(*shape, dtype=BF):
    return jax.ShapeDtypeStruct(shape, dtype)


def pack(len_ref, q_hbm, k_hbm, v_hbm, sk_hbm, sv_hbm, pos_hbm, tile_ref, out_ref, k_ref, v_ref, pos_ref, sems):
    meta = 2 * HALF
    copies = [
        pltpu.make_async_copy(k_hbm, k_ref, sems.at[0]),
        pltpu.make_async_copy(v_hbm, v_ref, sems.at[1]),
        pltpu.make_async_copy(sk_hbm, out_ref.at[meta : meta + 32], sems.at[2]),
        pltpu.make_async_copy(sv_hbm, out_ref.at[meta + 32 : meta + 64], sems.at[3]),
        pltpu.make_async_copy(q_hbm, tile_ref.at[:, : GROUP * HD], sems.at[4]),
    ]
    pos_copy = pltpu.make_async_copy(pos_hbm, pos_ref, sems.at[5])
    pos_copy.start()
    for copy in copies:
        copy.start()
    pos_copy.wait()
    pos = jnp.broadcast_to(pos_ref[...], (32, 32))
    row = lax.broadcasted_iota(jnp.int32, (32, 32), 0)
    col = lax.broadcasted_iota(jnp.int32, (32, 32), 1)
    column = jnp.sum(jnp.where(row == col, pos, 0), axis=1, keepdims=True)
    lane = lax.broadcasted_iota(jnp.int32, (32, 128), 1)
    numbers = jnp.where(lane == 0, column // 32, jnp.where(lane == 1, column % 32, 0))
    tile_ref[:, GROUP * HD :] = numbers.astype(F32).astype(BF)
    for copy in copies:
        copy.wait()
    used = len_ref[0]
    first = jnp.broadcast_to(k_ref[0:1, :].astype(F32), (HD, HD))
    for half in range(2):
        base = half * (2 * HALF + META)
        for block in range(HALF // HD):
            start = half * HALF + block * HD
            seen = lax.broadcasted_iota(jnp.int32, (HD, HD), 0) + start < used
            keys = jnp.where(seen, k_ref[start : start + HD, :].astype(F32), first)
            out_ref[base + block * HD : base + (block + 1) * HD, :] = keys.astype(BF)
            values = jnp.where(seen, v_ref[start : start + HD, :].astype(F32), 0.0)
            out_ref[base + HALF + block * HD : base + HALF + (block + 1) * HD, :] = values.astype(BF)
    pos = jnp.concatenate([pos_ref[...], jnp.zeros((1, 96), jnp.int32)], axis=1)
    pos = jnp.broadcast_to(pos, (64, HD))
    row = lax.broadcasted_iota(jnp.int32, (64, HD), 0)
    lane = lax.broadcasted_iota(jnp.int32, (64, HD), 1)
    extent = jnp.where(lane == 0, used // 32, jnp.where(lane == 1, used % 32, 0))
    numbers = jnp.where(row == 0, pos // 32, jnp.where(row == 1, pos % 32, jnp.where(row == 2, extent, 0)))
    out_ref[meta + 64 : meta + 128, :] = numbers.astype(F32).astype(BF)


def pair(a_ref, b_ref, out_ref):
    out_ref[0:32, :] = a_ref[...]
    out_ref[32:64, :] = b_ref[...]


def attend(layout, span, n_carry, picks, unit, n_tiles, n_idle, has_weight, *refs):
    last, first = picks is not None, n_carry == 0
    refs = list(refs)
    take = lambda n: [refs.pop(0) for _ in range(n)]
    tiles, kvs, spans = take(n_tiles), take(len(layout)), take(3 if span else 0)
    accs_in, sts_in = take(n_carry), take(n_carry)
    w_in = take(int(has_weight))
    take(n_idle)
    if last:
        outs = take(len(picks))
    else:
        acc_out, st_out = take(2)
        for kv in kvs:
            refs.pop(0)[...] = kv[2 * HALF : 2 * HALF + META, :]
    for w in w_in:
        refs.pop(0)[...] = w[...]
    v2, score_a, score_b = refs
    rows = 64 * n_tiles

    def carried(parts, cols):
        if not last:
            return jnp.concatenate([ref[:, cols] for ref in parts], axis=0)
        return jnp.concatenate([parts[0][64 * i : 64 * (i + 1), cols] for i in picks], axis=0)

    blocks = []
    at = 0
    for i, (holder, pieces) in enumerate(layout):
        numbers = kvs[holder][2 * HALF + 64 : 2 * HALF + 80, :].astype(F32)
        used = numbers[2:3, 0:1] * 32.0 + numbers[2:3, 1:2]
        for start, cache_row in pieces:
            v2[at : at + HALF, :HD] = kvs[i][start + HALF : start + 2 * HALF, :]
            index = lax.broadcasted_iota(jnp.int32, (HALF, HD), 0) + cache_row
            v2[at : at + HALF, HD:] = jnp.where(index.astype(F32) < used, 1.0, 0.0).astype(BF)
            blocks += [(at + c, 256, kvs[i], start + c) for c in range(0, HALF, 256)]
            at += HALF
    if span:
        near = [s[...] for s in spans] + [kvs[0][2 * HALF : 2 * HALF + META, :]]
        span_keys = jnp.concatenate([s[0:32, :] for s in near], axis=0)
        for i, s in enumerate(near):
            v2[at + 32 * i : at + 32 * (i + 1), :HD] = s[32:64, :]
        v2[at : at + HD, HD:] = jnp.ones((HD, HD), BF)
        near = [s[64:80, :].astype(F32) for s in near]
        key_pos = jnp.concatenate([s[0:1, 0:32] * 32.0 + s[1:2, 0:32] for s in near], axis=1)
        numbers = jnp.concatenate([t[:, GROUP * HD :] for t in tiles], axis=0).astype(F32)
        query_pos = numbers[:, 0:1] * 32.0 + numbers[:, 1:2]
        seen = key_pos <= query_pos
        blocks.append((at, HD, None, 0))
    if span:
        seen = jnp.concatenate([seen] * unit, axis=0)
    lane = lax.broadcasted_iota(jnp.int32, (rows, HD), 1)
    st = jnp.zeros((rows, HD), F32) if first else carried(sts_in, slice(0, HD))
    new_st = jnp.zeros((rows, HD), F32)
    peak = None
    for step in range(GROUP // unit + 1):
        mine, previous = (score_a, score_b) if step % 2 == 0 else (score_b, score_a)
        heads = range(step * unit, (step + 1) * unit)
        if step < GROUP // unit:
            query = jnp.concatenate([t[:, h * HD : (h + 1) * HD] for h in heads for t in tiles], axis=0)
        top = None
        acc = None
        for c, width, kv, row in blocks:
            if step < GROUP // unit:
                keys = span_keys if kv is None else kv[row : row + width, :]
                s = lax.dot_general(query, keys, (((1,), (1,)), ((), ())), preferred_element_type=F32)
                s = s * LOG2_SCALE
                if kv is None:
                    s = jnp.where(seen, s, NEG)
                mine[:, c : c + width] = s
                for i in range(0, width, HD):
                    top = s[:, i : i + HD] if top is None else jnp.maximum(top, s[:, i : i + HD])
            if step > 0:
                p = jnp.exp2(previous[:, c : c + width] - peak).astype(BF)
                term = jnp.dot(p, v2[c : c + width, :], preferred_element_type=F32)
                acc = term if acc is None else acc + term
        if step > 0:
            for u in range(unit):
                h = (step - 1) * unit + u
                part = slice(u * rows, (u + 1) * rows)
                cols = slice(h * HD, (h + 1) * HD)
                total, weight, shift = acc[part, :HD], acc[part, HD:], peak[part, :]
                if not first:
                    rescale = jnp.exp2(st[:, h : h + 1] - shift)
                    total = total + carried(accs_in, cols) * rescale
                    weight = weight + st[:, GROUP + h : GROUP + h + 1] * rescale
                new_st = jnp.where(lane == h, jnp.broadcast_to(shift, (rows, HD)), new_st)
                new_st = jnp.where(lane == GROUP + h, weight, new_st)
                if last:
                    for i, out in enumerate(outs):
                        out[:, cols] = total[64 * i : 64 * (i + 1), :].astype(BF)
                else:
                    acc_out[:, cols] = total
        if step < GROUP // unit:
            peak = jnp.max(top, axis=1, keepdims=True).astype(BF).astype(F32)
            if not first:
                peak = jnp.maximum(peak, jnp.concatenate([st[:, h : h + 1] for h in heads], axis=0))
    if last:
        high = new_st.astype(BF).astype(F32)
        low = pltpu.roll(new_st - high, GROUP, 1)
        packed = jnp.where(lane < 2 * GROUP, high, jnp.where(lane < 3 * GROUP, low, 0.0)).astype(BF)
        for i, out in enumerate(outs):
            out[:, GROUP * HD :] = packed[64 * i : 64 * (i + 1), :]
    else:
        st_out[...] = new_st


def attend_call(tiles, kvs, layout, spans=(), accs=(), sts=(), weight=None, idle=(), picks=None, unit=1):
    n_keys = HALF * sum(len(p) for _, p in layout) + (HD if spans else 0)
    rows = 64 * len(tiles)
    handed = [] if weight is None else [weight]
    args = list(tiles) + list(kvs) + list(spans) + list(accs) + list(sts) + handed + list(idle)
    if picks is not None:
        out = [sds(64, QW) for _ in picks]
    else:
        out = [sds(rows, GROUP * HD, dtype=F32), sds(rows, HD, dtype=F32)] + [sds(META, HD) for _ in kvs]
    out += [sds(*w.shape) for w in handed]
    return call(
        functools.partial(
            attend, layout, bool(spans), len(accs), picks, unit, len(tiles), len(idle), weight is not None
        ),
        out,
        args,
        scratch=[
            pltpu.VMEM((n_keys, 2 * HD), BF),
            pltpu.VMEM((rows * unit, n_keys), F32),
            pltpu.VMEM((rows * unit, n_keys), F32),
        ],
        idle=range(len(args) - len(idle), len(args)),
        flops=rows * GROUP * n_keys * HD * 8,
        nbytes=4 << 20,
        vmem=24 << 20,
    )


def join(messages, final):
    stats = [m[:, GROUP * HD :].astype(F32) for m in messages]
    sums, peaks, weights = [], [], []
    for h in range(GROUP):
        each = [s[:, h : h + 1] for s in stats]
        peak = functools.reduce(jnp.maximum, each)
        scales = [jnp.exp2(p - peak) for p in each]
        weight = sum(
            (s[:, GROUP + h : GROUP + h + 1] + s[:, 2 * GROUP + h : 2 * GROUP + h + 1]) * c
            for s, c in zip(stats, scales)
        )
        total = sum(m[:, h * HD : (h + 1) * HD].astype(F32) * c for m, c in zip(messages, scales))
        sums.append(total / weight if final else total)
        peaks.append(peak)
        weights.append(weight)
    return sums, peaks, weights


def join_x(a_ref, b_ref, c_ref, d_ref, out_ref):
    messages = [r[...] for r in (a_ref, b_ref, c_ref, d_ref)]
    sums, peaks, weights = join(messages, False)
    lane = lax.broadcasted_iota(jnp.int32, (64, HD), 1)
    numbers = jnp.zeros((64, HD), F32)
    for h in range(GROUP):
        out_ref[:, h * HD : (h + 1) * HD] = sums[h].astype(BF)
        high = weights[h].astype(BF).astype(F32)
        numbers = jnp.where(lane == h, peaks[h], numbers)
        numbers = jnp.where(lane == GROUP + h, high, numbers)
        numbers = jnp.where(lane == 2 * GROUP + h, weights[h] - high, numbers)
    out_ref[:, GROUP * HD :] = numbers.astype(BF)


def join_z(own_ref, other_ref, out_ref):
    other = jnp.concatenate([other_ref[32:64, :], other_ref[0:32, :]], axis=0)
    sums, _, _ = join([own_ref[...], other], True)
    for h in range(GROUP):
        out_ref[:, h * HD : (h + 1) * HD] = sums[h].astype(BF)


def project(where_ref, a0, a1, a2, a3, w0, w1, w2, w3, keep_ref, send_ref, rows_ref):
    z, y, core = where_ref[0], where_ref[1], where_ref[2]
    for a, dy in zip((a0, a1, a2, a3), (0, 1, 3, 2)):
        there = lax.rem(y + dy, 4)
        other = lax.rem(there + core, 2)
        for part in range(2):
            z_there = z if part == 0 else 1 - z
            slot = pl.multiple_of((other * 4 + z_there * 2 + there // 2) * 32, 32)
            rows_ref[pl.ds(slot, 32), :] = a[32 * part : 32 * (part + 1), :]
    for i, w in enumerate((w0, w1, w2, w3)):
        out = jnp.dot(rows_ref[...], w[...], preferred_element_type=F32).astype(BF)
        keep_ref[:, i * 256 : (i + 1) * 256] = out[:128, :]
        send_ref[:, i * 256 : (i + 1) * 256] = out[128:, :]


def add_cores(where_ref, keep_ref, got_ref, own_ref, o1, o2, o3):
    z_lo = where_ref[3]
    for k, out in enumerate((own_ref, o1, o2, o3)):
        slot = pl.multiple_of((z_lo ^ k) * 32, 32)
        out[...] = (keep_ref[pl.ds(slot, 32), :].astype(F32) + got_ref[pl.ds(slot, 32), :].astype(F32)).astype(BF)


def add_z(a_ref, b_ref, c_ref, d_ref, o0, o1, o2, o3):
    total = sum(r[...].astype(F32) for r in (a_ref, b_ref, c_ref, d_ref)).astype(BF)
    for i, out in enumerate((o0, o1, o2, o3)):
        out[...] = total[:, i * 256 : (i + 1) * 256]


def place(where_ref, a_ref, b_ref, c_ref, d_ref, out_ref):
    x = where_ref[4]
    for dx, r in zip((0, 1, 3, 2), (a_ref, b_ref, c_ref, d_ref)):
        slot = pl.multiple_of(lax.rem(x + dx, 4) * 32, 32)
        out_ref[pl.ds(slot, 32), :] = r[...]


def ctx_shift(dz, dy, dx):
    pairs = []
    for c in range(32):
        z, y, x = c // 16, (c // 4) % 4, c % 4
        pairs.append((c, ((z + dz) % 2) * 16 + ((y + dy) % 4) * 4 + (x + dx) % 4))
    return pairs


def fetch(value, dz=0, dy=0, dx=0):
    return lax.ppermute(value, "ctx", ctx_shift(-dz, -dy, -dx))


def shards(queries, cache_keys, cache_values, span_keys, span_values, prefix_len, positions, out_weight):
    index = lax.axis_index("ctx")
    head = lax.axis_index("head")
    where = jnp.stack([index // 16, (index // 4) % 4, head % 2, head // 2, index % 4]).astype(jnp.int32)
    pos_row = positions.reshape(1, 32)
    tile, kv = call(
        pack,
        [near(32, QW), near(4 * HALF + META, HD)],
        [prefix_len, queries, cache_keys, cache_values, span_keys, span_values, pos_row],
        scratch=[
            pltpu.VMEM((2 * HALF, HD), BF),
            pltpu.VMEM((2 * HALF, HD), BF),
            pltpu.VMEM((1, 32), jnp.int32),
            pltpu.SemaphoreType.DMA((6,)),
        ],
        smem=(0,),
        raw=(1, 2, 3, 4, 5, 6),
    )
    kv_up = fetch(kv, dy=1)
    kv_down = fetch(kv, dy=-1)
    own = call(pair, sds(64, QW), [tile, fetch(tile, dz=1)])
    far = fetch(own, dx=2)
    tiles = [own, fetch(own, dx=1), fetch(own, dx=-1), far]

    cut = 2 * HALF + META
    whole = [(0, 0), (cut, HALF)]
    acc_a, st_a, span = attend_call(tiles[:1], [kv], [(0, whole)], unit=4)
    acc_b, st_b, _ = attend_call(tiles[1:], [kv], [(0, whole)])
    far_a = fetch(kv_up[:cut], dy=1)
    far_b = fetch(kv_down[cut:], dy=-1)
    acc, st, *spans = attend_call(
        tiles, [kv_up, kv_down], [(0, whole), (1, whole)], accs=[acc_a, acc_b], sts=[st_a, st_b]
    )

    def finish(picks, unit, idle=(), weight=None):
        return attend_call(
            [tiles[i] for i in picks],
            [far_a, far_b],
            [(0, [(0, 0)]), (0, [(0, HALF)])],
            spans=[span] + spans,
            accs=[acc],
            sts=[st],
            weight=weight,
            idle=idle,
            picks=picks,
            unit=unit,
        )

    part_3, part_1, part_2 = finish((3, 1, 2), 2)
    got_3, got_1, got_2 = fetch(part_3, dx=-2), fetch(part_1, dx=-1), fetch(part_2, dx=1)
    part_0, weight = finish((0,), 4, idle=[part_3], weight=out_weight)
    weights = [out_weight, fetch(weight, dx=1), fetch(weight, dx=-1), fetch(weight, dx=2)]
    joined = call(join_x, sds(64, QW), [part_0, got_1, got_2, got_3])
    attended = call(join_z, sds(64, GROUP * HD), [joined, fetch(joined, dz=1)])
    rows = [attended] + [fetch(attended, dy=d) for d in (1, -1, 2)]
    keep, send = call(
        project,
        [sds(128, 1024), sds(128, 1024)],
        [where] + rows + weights,
        scratch=[pltpu.VMEM((256, 1024), BF)],
        smem=(0,),
        flops=2 * 256 * 1024 * 1024,
        nbytes=4 << 20,
    )
    got = lax.ppermute(send, "head", [(h, h ^ 1) for h in range(8)])
    own, *others = call(add_cores, [sds(32, 1024)] * 4, [where, keep, got], smem=(0,))
    others = [lax.ppermute(o, "head", [(h, h ^ (2 * k)) for h in range(8)]) for k, o in zip((1, 2, 3), others)]
    pieces = call(add_z, [sds(32, 256)] * 4, [own] + others)
    pieces = [pieces[0]] + [fetch(pieces[i], dx=-d) for i, d in ((1, 1), (2, -1), (3, 2))]
    pieces = [pieces[0], pieces[2], pieces[1], pieces[3]]
    return call(place, sds(128, 256), [where] + pieces, smem=(0,))


def solution(mesh):
    return jax.shard_map(
        shards,
        mesh=mesh,
        in_specs=(
            P("ctx", "head"),
            P("ctx", "head"),
            P("ctx", "head"),
            P("ctx", "head"),
            P("ctx", "head"),
            P("ctx"),
            P("ctx"),
            P("head", "ctx"),
        ),
        out_specs=P("head", "ctx"),
        check_vma=False,
    )
```

```python
import functools
import math

import jax
import jax.numpy as jnp
from jax import lax
from jax.experimental import pallas as pl
from jax.experimental.pallas import tpu as pltpu
from jax.sharding import PartitionSpec as P

BF = jnp.bfloat16
F32 = jnp.float32
HD = 128
GROUP = 8
HALF = 1024
META = 128
QW = GROUP * HD + 128
LOG2_SCALE = math.log2(math.e) / math.sqrt(HD)
NEG = -1e30


def call(body, out_shape, args, scratch=(), smem=(), idle=(), raw=(), flops=0, nbytes=0, vmem=8 << 20):
    args, specs = list(args), []
    for i in range(len(args)):
        if i in smem:
            specs.append(pl.BlockSpec(memory_space=pltpu.SMEM))
        elif i in raw:
            specs.append(pl.BlockSpec(memory_space=pltpu.HBM))
            args[i] = pltpu.with_memory_space_constraint(args[i], pltpu.HBM)
        elif i in idle:
            specs.append(pl.BlockSpec(memory_space=pl.ANY))
        else:
            specs.append(pl.BlockSpec(memory_space=pltpu.VMEM))
    return pl.pallas_call(
        body,
        out_shape=out_shape,
        in_specs=specs,
        out_specs=jax.tree.map(lambda _: pl.BlockSpec(memory_space=pltpu.VMEM), out_shape),
        scratch_shapes=list(scratch),
        cost_estimate=pl.CostEstimate(flops=flops, bytes_accessed=nbytes, transcendentals=0),
        compiler_params=pltpu.CompilerParams(vmem_limit_bytes=vmem),
    )(*args)


def sds(*shape, dtype=BF):
    return jax.ShapeDtypeStruct(shape, dtype)


def pack(len_ref, q_hbm, k_hbm, v_hbm, sk_hbm, sv_hbm, pos_hbm, tile_ref, out_ref, k_ref, v_ref, pos_ref, sems):
    meta = 2 * HALF
    copies = [
        pltpu.make_async_copy(k_hbm, k_ref, sems.at[0]),
        pltpu.make_async_copy(v_hbm, v_ref, sems.at[1]),
        pltpu.make_async_copy(sk_hbm, out_ref.at[meta : meta + 32], sems.at[2]),
        pltpu.make_async_copy(sv_hbm, out_ref.at[meta + 32 : meta + 64], sems.at[3]),
        pltpu.make_async_copy(q_hbm, tile_ref.at[:, : GROUP * HD], sems.at[4]),
    ]
    pos_copy = pltpu.make_async_copy(pos_hbm, pos_ref, sems.at[5])
    pos_copy.start()
    for copy in copies:
        copy.start()
    pos_copy.wait()
    pos = jnp.broadcast_to(pos_ref[...], (32, 32))
    row = lax.broadcasted_iota(jnp.int32, (32, 32), 0)
    col = lax.broadcasted_iota(jnp.int32, (32, 32), 1)
    column = jnp.sum(jnp.where(row == col, pos, 0), axis=1, keepdims=True)
    lane = lax.broadcasted_iota(jnp.int32, (32, 128), 1)
    numbers = jnp.where(lane == 0, column // 32, jnp.where(lane == 1, column % 32, 0))
    tile_ref[:, GROUP * HD :] = numbers.astype(F32).astype(BF)
    for copy in copies:
        copy.wait()
    used = len_ref[0]
    first = jnp.broadcast_to(k_ref[0:1, :].astype(F32), (HD, HD))
    for half in range(2):
        base = half * (2 * HALF + META)
        for block in range(HALF // HD):
            start = half * HALF + block * HD
            seen = lax.broadcasted_iota(jnp.int32, (HD, HD), 0) + start < used
            keys = jnp.where(seen, k_ref[start : start + HD, :].astype(F32), first)
            out_ref[base + block * HD : base + (block + 1) * HD, :] = keys.astype(BF)
            values = jnp.where(seen, v_ref[start : start + HD, :].astype(F32), 0.0)
            out_ref[base + HALF + block * HD : base + HALF + (block + 1) * HD, :] = values.astype(BF)
    pos = jnp.concatenate([pos_ref[...], jnp.zeros((1, 96), jnp.int32)], axis=1)
    pos = jnp.broadcast_to(pos, (64, HD))
    row = lax.broadcasted_iota(jnp.int32, (64, HD), 0)
    lane = lax.broadcasted_iota(jnp.int32, (64, HD), 1)
    extent = jnp.where(lane == 0, used // 32, jnp.where(lane == 1, used % 32, 0))
    numbers = jnp.where(row == 0, pos // 32, jnp.where(row == 1, pos % 32, jnp.where(row == 2, extent, 0)))
    out_ref[meta + 64 : meta + 128, :] = numbers.astype(F32).astype(BF)


def pair(a_ref, b_ref, out_ref):
    out_ref[0:32, :] = a_ref[...]
    out_ref[32:64, :] = b_ref[...]


def attend(layout, span, n_carry, picks, unit, n_tiles, n_idle, has_weight, *refs):
    last, first = picks is not None, n_carry == 0
    refs = list(refs)
    take = lambda n: [refs.pop(0) for _ in range(n)]
    tiles, kvs, spans = take(n_tiles), take(len(layout)), take(3 if span else 0)
    accs_in, sts_in = take(n_carry), take(n_carry)
    w_in = take(int(has_weight))
    take(n_idle)
    if last:
        outs = take(len(picks))
    else:
        acc_out, st_out = take(2)
        for kv in kvs:
            refs.pop(0)[...] = kv[2 * HALF : 2 * HALF + META, :]
    for w in w_in:
        refs.pop(0)[...] = w[...]
    open_ref, score_a, score_b = refs
    rows = 64 * n_tiles

    def carried(parts, cols):
        if not last:
            return jnp.concatenate([ref[:, cols] for ref in parts], axis=0)
        return jnp.concatenate([parts[0][64 * i : 64 * (i + 1), cols] for i in picks], axis=0)

    blocks = []
    at = 0
    for i, (holder, pieces) in enumerate(layout):
        numbers = kvs[holder][2 * HALF + 64 : 2 * HALF + 80, :].astype(F32)
        used = numbers[2:3, 0:1] * 32.0 + numbers[2:3, 1:2]
        for start, cache_row in pieces:
            index = lax.broadcasted_iota(jnp.int32, (HALF, HD), 0) + cache_row
            open_ref[at : at + HALF, :] = jnp.where(index.astype(F32) < used, 1.0, 0.0).astype(BF)
            blocks += [(at + c, 256, kvs[i], start + c) for c in range(0, HALF, 256)]
            at += HALF
    if span:
        near = [s[...] for s in spans] + [kvs[0][2 * HALF : 2 * HALF + META, :]]
        span_keys = jnp.concatenate([s[0:32, :] for s in near], axis=0)
        span_values = jnp.concatenate([s[32:64, :] for s in near], axis=0)
        open_ref[at : at + HD, :] = jnp.ones((HD, HD), BF)
        near = [s[64:80, :].astype(F32) for s in near]
        key_pos = jnp.concatenate([s[0:1, 0:32] * 32.0 + s[1:2, 0:32] for s in near], axis=1)
        numbers = jnp.concatenate([t[:, GROUP * HD :] for t in tiles], axis=0).astype(F32)
        query_pos = numbers[:, 0:1] * 32.0 + numbers[:, 1:2]
        seen = key_pos <= query_pos
        blocks.append((at, HD, None, 0))
    if span:
        seen = jnp.concatenate([seen] * unit, axis=0)
    lane = lax.broadcasted_iota(jnp.int32, (rows, HD), 1)
    st = jnp.zeros((rows, HD), F32) if first else carried(sts_in, slice(0, HD))
    new_st = jnp.zeros((rows, HD), F32)
    peak = None
    for step in range(GROUP // unit + 1):
        mine, previous = (score_a, score_b) if step % 2 == 0 else (score_b, score_a)
        heads = range(step * unit, (step + 1) * unit)
        if step < GROUP // unit:
            query = jnp.concatenate([t[:, h * HD : (h + 1) * HD] for h in heads for t in tiles], axis=0)
            query = query.astype(F32) * LOG2_SCALE
            high = query.astype(BF)
            query = jnp.concatenate([high, (query - high.astype(F32)).astype(BF)], axis=1)
        top = None
        acc = None
        for c, width, kv, row in blocks:
            if step < GROUP // unit:
                keys = span_keys if kv is None else kv[row : row + width, :]
                keys = jnp.concatenate([keys, keys], axis=1)
                s = lax.dot_general(query, keys, (((1,), (1,)), ((), ())), preferred_element_type=F32)
                if kv is None:
                    s = jnp.where(seen, s, NEG)
                mine[:, c : c + width] = s
                for i in range(0, width, HD):
                    top = s[:, i : i + HD] if top is None else jnp.maximum(top, s[:, i : i + HD])
            if step > 0:
                p = jnp.exp2(previous[:, c : c + width] - peak).astype(BF)
                values = span_values if kv is None else kv[row + HALF : row + HALF + width, :]
                values = jnp.concatenate([values, open_ref[c : c + width, :]], axis=1)
                term = jnp.dot(p, values, preferred_element_type=F32)
                acc = term if acc is None else acc + term
        if step > 0:
            for u in range(unit):
                h = (step - 1) * unit + u
                part = slice(u * rows, (u + 1) * rows)
                cols = slice(h * HD, (h + 1) * HD)
                total, weight, shift = acc[part, :HD], acc[part, HD:], peak[part, :]
                if not first:
                    rescale = jnp.exp2(st[:, h : h + 1] - shift)
                    total = total + carried(accs_in, cols) * rescale
                    weight = weight + st[:, GROUP + h : GROUP + h + 1] * rescale
                new_st = jnp.where(lane == h, jnp.broadcast_to(shift, (rows, HD)), new_st)
                new_st = jnp.where(lane == GROUP + h, weight, new_st)
                if last:
                    for i, out in enumerate(outs):
                        out[:, cols] = total[64 * i : 64 * (i + 1), :].astype(BF)
                else:
                    acc_out[:, cols] = total
        if step < GROUP // unit:
            peak = jnp.max(top, axis=1, keepdims=True).astype(BF).astype(F32)
            if not first:
                peak = jnp.maximum(peak, jnp.concatenate([st[:, h : h + 1] for h in heads], axis=0))
    if last:
        high = new_st.astype(BF).astype(F32)
        low = pltpu.roll(new_st - high, GROUP, 1)
        packed = jnp.where(lane < 2 * GROUP, high, jnp.where(lane < 3 * GROUP, low, 0.0)).astype(BF)
        for i, out in enumerate(outs):
            out[:, GROUP * HD :] = packed[64 * i : 64 * (i + 1), :]
    else:
        st_out[...] = new_st


def attend_call(tiles, kvs, layout, spans=(), accs=(), sts=(), weight=None, idle=(), picks=None, unit=1):
    n_keys = HALF * sum(len(p) for _, p in layout) + (HD if spans else 0)
    rows = 64 * len(tiles)
    handed = [] if weight is None else [weight]
    args = list(tiles) + list(kvs) + list(spans) + list(accs) + list(sts) + handed + list(idle)
    if picks is not None:
        out = [sds(64, QW) for _ in picks]
    else:
        out = [sds(rows, GROUP * HD, dtype=F32), sds(rows, HD, dtype=F32)] + [sds(META, HD) for _ in kvs]
    out += [sds(*w.shape) for w in handed]
    return call(
        functools.partial(
            attend, layout, bool(spans), len(accs), picks, unit, len(tiles), len(idle), weight is not None
        ),
        out,
        args,
        scratch=[
            pltpu.VMEM((n_keys, HD), BF),
            pltpu.VMEM((rows * unit, n_keys), F32),
            pltpu.VMEM((rows * unit, n_keys), F32),
        ],
        idle=range(len(args) - len(idle), len(args)),
        flops=rows * GROUP * n_keys * HD * 8,
        nbytes=4 << 20,
        vmem=(rows * unit * n_keys * 8) + (8 << 20),
    )


def join(messages, final):
    stats = [m[:, GROUP * HD :].astype(F32) for m in messages]
    sums, peaks, weights = [], [], []
    for h in range(GROUP):
        each = [s[:, h : h + 1] for s in stats]
        peak = functools.reduce(jnp.maximum, each)
        scales = [jnp.exp2(p - peak) for p in each]
        weight = sum(
            (s[:, GROUP + h : GROUP + h + 1] + s[:, 2 * GROUP + h : 2 * GROUP + h + 1]) * c
            for s, c in zip(stats, scales)
        )
        total = sum(m[:, h * HD : (h + 1) * HD].astype(F32) * c for m, c in zip(messages, scales))
        sums.append(total / weight if final else total)
        peaks.append(peak)
        weights.append(weight)
    return sums, peaks, weights


def join_x(a_ref, b_ref, c_ref, d_ref, out_ref):
    messages = [r[...] for r in (a_ref, b_ref, c_ref, d_ref)]
    sums, peaks, weights = join(messages, False)
    lane = lax.broadcasted_iota(jnp.int32, (64, HD), 1)
    numbers = jnp.zeros((64, HD), F32)
    for h in range(GROUP):
        out_ref[:, h * HD : (h + 1) * HD] = sums[h].astype(BF)
        high = weights[h].astype(BF).astype(F32)
        numbers = jnp.where(lane == h, peaks[h], numbers)
        numbers = jnp.where(lane == GROUP + h, high, numbers)
        numbers = jnp.where(lane == 2 * GROUP + h, weights[h] - high, numbers)
    out_ref[:, GROUP * HD :] = numbers.astype(BF)


def join_z(own_ref, other_ref, out_ref):
    other = jnp.concatenate([other_ref[32:64, :], other_ref[0:32, :]], axis=0)
    sums, _, _ = join([own_ref[...], other], True)
    for h in range(GROUP):
        out_ref[:, h * HD : (h + 1) * HD] = sums[h].astype(BF)


def project(where_ref, a0, a1, a2, a3, w0, w1, w2, w3, keep_ref, send_ref, rows_ref):
    z, y, core = where_ref[0], where_ref[1], where_ref[2]
    for a, dy in zip((a0, a1, a2, a3), (0, 1, 3, 2)):
        there = lax.rem(y + dy, 4)
        other = lax.rem(there + core, 2)
        for part in range(2):
            z_there = z if part == 0 else 1 - z
            slot = pl.multiple_of((other * 4 + z_there * 2 + there // 2) * 32, 32)
            rows_ref[pl.ds(slot, 32), :] = a[32 * part : 32 * (part + 1), :]
    for i, w in enumerate((w0, w1, w2, w3)):
        out = jnp.dot(rows_ref[...], w[...], preferred_element_type=F32).astype(BF)
        keep_ref[:, i * 256 : (i + 1) * 256] = out[:128, :]
        send_ref[:, i * 256 : (i + 1) * 256] = out[128:, :]


def add_cores(where_ref, keep_ref, got_ref, own_ref, o1, o2, o3):
    z_lo = where_ref[3]
    for k, out in enumerate((own_ref, o1, o2, o3)):
        slot = pl.multiple_of((z_lo ^ k) * 32, 32)
        out[...] = (keep_ref[pl.ds(slot, 32), :].astype(F32) + got_ref[pl.ds(slot, 32), :].astype(F32)).astype(BF)


def add_z(a_ref, b_ref, c_ref, d_ref, o0, o1, o2, o3):
    total = sum(r[...].astype(F32) for r in (a_ref, b_ref, c_ref, d_ref)).astype(BF)
    for i, out in enumerate((o0, o1, o2, o3)):
        out[...] = total[:, i * 256 : (i + 1) * 256]


def place(where_ref, a_ref, b_ref, c_ref, d_ref, out_ref):
    x = where_ref[4]
    for dx, r in zip((0, 1, 3, 2), (a_ref, b_ref, c_ref, d_ref)):
        slot = pl.multiple_of(lax.rem(x + dx, 4) * 32, 32)
        out_ref[pl.ds(slot, 32), :] = r[...]


def ctx_shift(dz, dy, dx):
    pairs = []
    for c in range(32):
        z, y, x = c // 16, (c // 4) % 4, c % 4
        pairs.append((c, ((z + dz) % 2) * 16 + ((y + dy) % 4) * 4 + (x + dx) % 4))
    return pairs


def fetch(value, dz=0, dy=0, dx=0):
    return lax.ppermute(value, "ctx", ctx_shift(-dz, -dy, -dx))


def shards(queries, cache_keys, cache_values, span_keys, span_values, prefix_len, positions, out_weight):
    index = lax.axis_index("ctx")
    head = lax.axis_index("head")
    where = jnp.stack([index // 16, (index // 4) % 4, head % 2, head // 2, index % 4]).astype(jnp.int32)
    pos_row = positions.reshape(1, 32)
    tile, kv = call(
        pack,
        [sds(32, QW), sds(4 * HALF + META, HD)],
        [prefix_len, queries, cache_keys, cache_values, span_keys, span_values, pos_row],
        scratch=[
            pltpu.VMEM((2 * HALF, HD), BF),
            pltpu.VMEM((2 * HALF, HD), BF),
            pltpu.VMEM((1, 32), jnp.int32),
            pltpu.SemaphoreType.DMA((6,)),
        ],
        smem=(0,),
        raw=(1, 2, 3, 4, 5, 6),
    )
    kv_up = fetch(kv, dy=1)
    kv_down = fetch(kv, dy=-1)
    own = call(pair, sds(64, QW), [tile, fetch(tile, dz=1)])
    far = fetch(own, dx=2)
    tiles = [own, fetch(own, dx=1), fetch(own, dx=-1), far]

    cut = 2 * HALF + META
    whole = [(0, 0), (cut, HALF)]
    acc_a, st_a, span, weight = attend_call(tiles[:1], [kv], [(0, whole)], weight=out_weight, unit=4)
    w_up, w_down = fetch(weight, dx=1), fetch(weight, dx=-1)
    acc_b, st_b, _, weight = attend_call(tiles[1:], [kv], [(0, whole)], weight=weight, unit=4)
    far_a = fetch(kv_up[:cut], dy=1)
    far_b = fetch(kv_down[cut:], dy=-1)
    acc, st, *spans = attend_call(
        tiles, [kv_up, kv_down], [(0, whole), (1, whole)], accs=[acc_a, acc_b], sts=[st_a, st_b], unit=2
    )

    def finish(picks, unit, idle=(), weight=None):
        return attend_call(
            [tiles[i] for i in picks],
            [far_a, far_b],
            [(0, [(0, 0)]), (0, [(0, HALF)])],
            spans=[span] + spans,
            accs=[acc],
            sts=[st],
            weight=weight,
            idle=idle,
            picks=picks,
            unit=unit,
        )

    part_3, part_1, part_2 = finish((3, 1, 2), 4, idle=[w_up, w_down])
    got_3, got_1, got_2 = fetch(part_3, dx=-2), fetch(part_1, dx=-1), fetch(part_2, dx=1)
    (part_0,) = finish((0,), 4, idle=[part_3])
    weights = [out_weight, w_up, w_down, fetch(weight, dx=2)]
    joined = call(join_x, sds(64, QW), [part_0, got_1, got_2, got_3])
    attended = call(join_z, sds(64, GROUP * HD), [joined, fetch(joined, dz=1)])
    rows = [attended] + [fetch(attended, dy=d) for d in (1, -1, 2)]
    keep, send = call(
        project,
        [sds(128, 1024), sds(128, 1024)],
        [where] + rows + weights,
        scratch=[pltpu.VMEM((256, 1024), BF)],
        smem=(0,),
        flops=2 * 256 * 1024 * 1024,
        nbytes=4 << 20,
    )
    got = lax.ppermute(send, "head", [(h, h ^ 1) for h in range(8)])
    own, *others = call(add_cores, [sds(32, 1024)] * 4, [where, keep, got], smem=(0,))
    others = [lax.ppermute(o, "head", [(h, h ^ (2 * k)) for h in range(8)]) for k, o in zip((1, 2, 3), others)]
    pieces = call(add_z, [sds(32, 256)] * 4, [own] + others)
    pieces = [pieces[0]] + [fetch(pieces[i], dx=-d) for i, d in ((1, 1), (2, -1), (3, 2))]
    pieces = [pieces[0], pieces[2], pieces[1], pieces[3]]
    return call(place, sds(128, 256), [where] + pieces, smem=(0,))


def solution(mesh):
    return jax.shard_map(
        shards,
        mesh=mesh,
        in_specs=(
            P("ctx", "head"),
            P("ctx", "head"),
            P("ctx", "head"),
            P("ctx", "head"),
            P("ctx", "head"),
            P("ctx"),
            P("ctx"),
            P("head", "ctx"),
        ),
        out_specs=P("head", "ctx"),
        check_vma=False,
    )
```

```python
import functools
import math

import jax
import jax.numpy as jnp
from jax import lax
from jax.experimental import pallas as pl
from jax.experimental.pallas import tpu as pltpu
from jax.sharding import PartitionSpec as P

BF = jnp.bfloat16
F32 = jnp.float32
HD = 128
GROUP = 8
HALF = 1024
META = 128
QW = GROUP * HD + 128
LOG2_SCALE = math.log2(math.e) / math.sqrt(HD)
NEG = -1e30


def call(body, out_shape, args, scratch=(), smem=(), idle=(), raw=(), flops=0, nbytes=0, vmem=8 << 20):
    args, specs = list(args), []
    for i in range(len(args)):
        if i in smem:
            specs.append(pl.BlockSpec(memory_space=pltpu.SMEM))
        elif i in raw:
            specs.append(pl.BlockSpec(memory_space=pltpu.HBM))
            args[i] = pltpu.with_memory_space_constraint(args[i], pltpu.HBM)
        elif i in idle:
            specs.append(pl.BlockSpec(memory_space=pl.ANY))
        else:
            specs.append(pl.BlockSpec(memory_space=pltpu.VMEM))
    return pl.pallas_call(
        body,
        out_shape=out_shape,
        in_specs=specs,
        out_specs=jax.tree.map(lambda _: pl.BlockSpec(memory_space=pltpu.VMEM), out_shape),
        scratch_shapes=list(scratch),
        cost_estimate=pl.CostEstimate(flops=flops, bytes_accessed=nbytes, transcendentals=0),
        compiler_params=pltpu.CompilerParams(vmem_limit_bytes=vmem),
    )(*args)


def sds(*shape, dtype=BF):
    return jax.ShapeDtypeStruct(shape, dtype)


def pack(len_ref, q_hbm, k_hbm, v_hbm, sk_hbm, sv_hbm, pos_hbm, tile_ref, out_ref, k_ref, v_ref, pos_ref, sems):
    meta = 2 * HALF
    copies = [
        pltpu.make_async_copy(k_hbm, k_ref, sems.at[0]),
        pltpu.make_async_copy(v_hbm, v_ref, sems.at[1]),
        pltpu.make_async_copy(sk_hbm, out_ref.at[meta : meta + 32], sems.at[2]),
        pltpu.make_async_copy(sv_hbm, out_ref.at[meta + 32 : meta + 64], sems.at[3]),
        pltpu.make_async_copy(q_hbm, tile_ref.at[:, : GROUP * HD], sems.at[4]),
    ]
    pos_copy = pltpu.make_async_copy(pos_hbm, pos_ref, sems.at[5])
    pos_copy.start()
    for copy in copies:
        copy.start()
    pos_copy.wait()
    pos = jnp.broadcast_to(pos_ref[...], (32, 32))
    row = lax.broadcasted_iota(jnp.int32, (32, 32), 0)
    col = lax.broadcasted_iota(jnp.int32, (32, 32), 1)
    column = jnp.sum(jnp.where(row == col, pos, 0), axis=1, keepdims=True)
    lane = lax.broadcasted_iota(jnp.int32, (32, 128), 1)
    numbers = jnp.where(lane == 0, column // 32, jnp.where(lane == 1, column % 32, 0))
    tile_ref[:, GROUP * HD :] = numbers.astype(F32).astype(BF)
    for copy in copies:
        copy.wait()
    used = len_ref[0]
    first = jnp.broadcast_to(k_ref[0:1, :].astype(F32), (HD, HD))
    for half in range(2):
        base = half * (2 * HALF + META)
        for block in range(HALF // HD):
            start = half * HALF + block * HD
            seen = lax.broadcasted_iota(jnp.int32, (HD, HD), 0) + start < used
            keys = jnp.where(seen, k_ref[start : start + HD, :].astype(F32), first)
            out_ref[base + block * HD : base + (block + 1) * HD, :] = keys.astype(BF)
            values = jnp.where(seen, v_ref[start : start + HD, :].astype(F32), 0.0)
            out_ref[base + HALF + block * HD : base + HALF + (block + 1) * HD, :] = values.astype(BF)
    pos = jnp.concatenate([pos_ref[...], jnp.zeros((1, 96), jnp.int32)], axis=1)
    pos = jnp.broadcast_to(pos, (64, HD))
    row = lax.broadcasted_iota(jnp.int32, (64, HD), 0)
    lane = lax.broadcasted_iota(jnp.int32, (64, HD), 1)
    extent = jnp.where(lane == 0, used // 32, jnp.where(lane == 1, used % 32, 0))
    numbers = jnp.where(row == 0, pos // 32, jnp.where(row == 1, pos % 32, jnp.where(row == 2, extent, 0)))
    out_ref[meta + 64 : meta + 128, :] = numbers.astype(F32).astype(BF)


def pair(a_ref, b_ref, out_ref):
    out_ref[0:32, :] = a_ref[...]
    out_ref[32:64, :] = b_ref[...]


def attend(layout, span, n_carry, picks, unit, n_tiles, n_idle, has_weight, *refs):
    last, first = picks is not None, n_carry == 0
    refs = list(refs)
    take = lambda n: [refs.pop(0) for _ in range(n)]
    tiles, kvs, spans = take(n_tiles), take(len(layout)), take(3 if span else 0)
    accs_in, sts_in = take(n_carry), take(n_carry)
    w_in = take(int(has_weight))
    take(n_idle)
    if last:
        outs = take(len(picks))
    else:
        acc_out, st_out = take(2)
        for kv in kvs:
            refs.pop(0)[...] = kv[2 * HALF : 2 * HALF + META, :]
    for w in w_in:
        refs.pop(0)[...] = w[...]
    open_ref, score_a, score_b = refs
    rows = 64 * n_tiles

    def widen(shift, width):
        return shift if shift.shape[1] == 1 else jnp.concatenate([shift] * (width // HD), axis=1)

    def carried(parts, cols):
        if not last:
            return jnp.concatenate([ref[:, cols] for ref in parts], axis=0)
        return jnp.concatenate([parts[0][64 * i : 64 * (i + 1), cols] for i in picks], axis=0)

    blocks = []
    at = 0
    for i, (holder, pieces) in enumerate(layout):
        numbers = kvs[holder][2 * HALF + 64 : 2 * HALF + 80, :].astype(F32)
        used = numbers[2:3, 0:1] * 32.0 + numbers[2:3, 1:2]
        for start, cache_row in pieces:
            index = lax.broadcasted_iota(jnp.int32, (HALF, HD), 0) + cache_row
            open_ref[at : at + HALF, :] = jnp.where(index.astype(F32) < used, 1.0, 0.0).astype(BF)
            blocks += [(at + c, 256, kvs[i], start + c) for c in range(0, HALF, 256)]
            at += HALF
    if span:
        near = [s[...] for s in spans] + [kvs[0][2 * HALF : 2 * HALF + META, :]]
        span_keys = jnp.concatenate([s[0:32, :] for s in near], axis=0)
        span_values = jnp.concatenate([s[32:64, :] for s in near], axis=0)
        open_ref[at : at + HD, :] = jnp.ones((HD, HD), BF)
        near = [s[64:80, :].astype(F32) for s in near]
        key_pos = jnp.concatenate([s[0:1, 0:32] * 32.0 + s[1:2, 0:32] for s in near], axis=1)
        numbers = jnp.concatenate([t[:, GROUP * HD :] for t in tiles], axis=0).astype(F32)
        query_pos = numbers[:, 0:1] * 32.0 + numbers[:, 1:2]
        seen = key_pos <= query_pos
        blocks.append((at, HD, None, 0))
    if span:
        seen = jnp.concatenate([seen] * unit, axis=0)
    lane = lax.broadcasted_iota(jnp.int32, (rows, HD), 1)
    new_st = jnp.zeros((rows, HD), F32)
    peak = None
    for step in range(GROUP // unit + 1):
        mine, previous = (score_a, score_b) if step % 2 == 0 else (score_b, score_a)
        heads = range(step * unit, (step + 1) * unit)
        if step < GROUP // unit:
            query = jnp.concatenate([t[:, h * HD : (h + 1) * HD] for h in heads for t in tiles], axis=0)
            query = query.astype(F32) * LOG2_SCALE
            high = query.astype(BF)
            query = jnp.concatenate([high, (query - high.astype(F32)).astype(BF)], axis=1)
        top = None
        acc = None
        for c, width, kv, row in blocks:
            if step < GROUP // unit:
                keys = span_keys if kv is None else kv[row : row + width, :]
                keys = jnp.concatenate([keys, keys], axis=1)
                s = lax.dot_general(query, keys, (((1,), (1,)), ((), ())), preferred_element_type=F32)
                if kv is None:
                    s = jnp.where(seen, s, NEG)
                mine[:, c : c + width] = s
                for i in range(0, width, HD):
                    top = s[:, i : i + HD] if top is None else jnp.maximum(top, s[:, i : i + HD])
            if step > 0:
                p = jnp.exp2(previous[:, c : c + width] - widen(peak, width)).astype(BF)
                values = span_values if kv is None else kv[row + HALF : row + HALF + width, :]
                values = jnp.concatenate([values, open_ref[c : c + width, :]], axis=1)
                term = jnp.dot(p, values, preferred_element_type=F32)
                acc = term if acc is None else acc + term
        if step > 0:
            for u in range(unit):
                h = (step - 1) * unit + u
                part = slice(u * rows, (u + 1) * rows)
                cols = slice(h * HD, (h + 1) * HD)
                wide = slice(2 * h * HD, 2 * (h + 1) * HD)
                total, shift = acc[part, :], jnp.broadcast_to(peak[part, :], (rows, HD))
                if not first:
                    rescale = jnp.exp2(carried(sts_in, cols) - shift)
                    total = total + carried(accs_in, wide) * jnp.concatenate([rescale, rescale], axis=1)
                if last:
                    new_st = jnp.where(lane == h, shift, new_st)
                    new_st = jnp.where(lane == GROUP + h, total[:, HD:], new_st)
                    for i, out in enumerate(outs):
                        out[:, cols] = total[64 * i : 64 * (i + 1), :HD].astype(BF)
                else:
                    acc_out[:, wide] = total
                    st_out[:, cols] = shift
        if step < GROUP // unit:
            peak = jnp.max(top, axis=1, keepdims=True).astype(BF).astype(F32)
            if not first:
                before = [carried(sts_in, slice(h * HD, (h + 1) * HD)) for h in heads]
                peak = jnp.maximum(peak, jnp.concatenate(before, axis=0))
    if last:
        high = new_st.astype(BF).astype(F32)
        low = pltpu.roll(new_st - high, GROUP, 1)
        packed = jnp.where(lane < 2 * GROUP, high, jnp.where(lane < 3 * GROUP, low, 0.0)).astype(BF)
        for i, out in enumerate(outs):
            out[:, GROUP * HD :] = packed[64 * i : 64 * (i + 1), :]


def attend_call(tiles, kvs, layout, spans=(), accs=(), sts=(), weight=None, idle=(), picks=None, unit=1):
    n_keys = HALF * sum(len(p) for _, p in layout) + (HD if spans else 0)
    rows = 64 * len(tiles)
    handed = [] if weight is None else [weight]
    args = list(tiles) + list(kvs) + list(spans) + list(accs) + list(sts) + handed + list(idle)
    if picks is not None:
        out = [sds(64, QW) for _ in picks]
    else:
        out = [sds(rows, 2 * GROUP * HD, dtype=F32), sds(rows, GROUP * HD, dtype=F32)] + [sds(META, HD) for _ in kvs]
    out += [sds(*w.shape) for w in handed]
    return call(
        functools.partial(
            attend, layout, bool(spans), len(accs), picks, unit, len(tiles), len(idle), weight is not None
        ),
        out,
        args,
        scratch=[
            pltpu.VMEM((n_keys, HD), BF),
            pltpu.VMEM((rows * unit, n_keys), F32),
            pltpu.VMEM((rows * unit, n_keys), F32),
        ],
        idle=range(len(args) - len(idle), len(args)),
        flops=rows * GROUP * n_keys * HD * 8,
        nbytes=4 << 20,
        vmem=(rows * unit * n_keys * 8) + (8 << 20),
    )


def join(messages, final):
    stats = [m[:, GROUP * HD :].astype(F32) for m in messages]
    sums, peaks, weights = [], [], []
    for h in range(GROUP):
        each = [s[:, h : h + 1] for s in stats]
        peak = functools.reduce(jnp.maximum, each)
        scales = [jnp.exp2(p - peak) for p in each]
        weight = sum(
            (s[:, GROUP + h : GROUP + h + 1] + s[:, 2 * GROUP + h : 2 * GROUP + h + 1]) * c
            for s, c in zip(stats, scales)
        )
        total = sum(m[:, h * HD : (h + 1) * HD].astype(F32) * c for m, c in zip(messages, scales))
        sums.append(total / weight if final else total)
        peaks.append(peak)
        weights.append(weight)
    return sums, peaks, weights


def join_x(a_ref, b_ref, c_ref, d_ref, out_ref):
    messages = [r[...] for r in (a_ref, b_ref, c_ref, d_ref)]
    sums, peaks, weights = join(messages, False)
    lane = lax.broadcasted_iota(jnp.int32, (64, HD), 1)
    numbers = jnp.zeros((64, HD), F32)
    for h in range(GROUP):
        out_ref[:, h * HD : (h + 1) * HD] = sums[h].astype(BF)
        high = weights[h].astype(BF).astype(F32)
        numbers = jnp.where(lane == h, peaks[h], numbers)
        numbers = jnp.where(lane == GROUP + h, high, numbers)
        numbers = jnp.where(lane == 2 * GROUP + h, weights[h] - high, numbers)
    out_ref[:, GROUP * HD :] = numbers.astype(BF)


def join_z(own_ref, other_ref, out_ref):
    other = jnp.concatenate([other_ref[32:64, :], other_ref[0:32, :]], axis=0)
    sums, _, _ = join([own_ref[...], other], True)
    for h in range(GROUP):
        out_ref[:, h * HD : (h + 1) * HD] = sums[h].astype(BF)


def project(a0, a1, a2, a3, w0, w1, w2, w3, keep_ref, send_ref, rows_ref):
    index, core = lax.axis_index("ctx"), lax.rem(lax.axis_index("head"), 2)
    z, y = index // 16, lax.rem(index // 4, 4)
    for a, dy in zip((a0, a1, a2, a3), (0, 1, 3, 2)):
        there = lax.rem(y + dy, 4)
        other = lax.rem(there + core, 2)
        for part in range(2):
            z_there = z if part == 0 else 1 - z
            slot = pl.multiple_of((other * 4 + z_there * 2 + there // 2) * 32, 32)
            rows_ref[pl.ds(slot, 32), :] = a[32 * part : 32 * (part + 1), :]
    for i, w in enumerate((w0, w1, w2, w3)):
        out = jnp.dot(rows_ref[...], w[...], preferred_element_type=F32).astype(BF)
        keep_ref[:, i * 256 : (i + 1) * 256] = out[:128, :]
        send_ref[:, i * 256 : (i + 1) * 256] = out[128:, :]


def add_cores(keep_ref, got_ref, own_ref, o1, o2, o3):
    z_lo = lax.axis_index("head") // 2
    for k, out in enumerate((own_ref, o1, o2, o3)):
        slot = pl.multiple_of((z_lo ^ k) * 32, 32)
        out[...] = (keep_ref[pl.ds(slot, 32), :].astype(F32) + got_ref[pl.ds(slot, 32), :].astype(F32)).astype(BF)


def add_z(a_ref, b_ref, c_ref, d_ref, o0, o1, o2, o3):
    total = sum(r[...].astype(F32) for r in (a_ref, b_ref, c_ref, d_ref)).astype(BF)
    for i, out in enumerate((o0, o1, o2, o3)):
        out[...] = total[:, i * 256 : (i + 1) * 256]


def place(a_ref, b_ref, c_ref, d_ref, out_ref):
    x = lax.rem(lax.axis_index("ctx"), 4)
    for dx, r in zip((0, 1, 3, 2), (a_ref, b_ref, c_ref, d_ref)):
        slot = pl.multiple_of(lax.rem(x + dx, 4) * 32, 32)
        out_ref[pl.ds(slot, 32), :] = r[...]


def ctx_shift(dz, dy, dx):
    pairs = []
    for c in range(32):
        z, y, x = c // 16, (c // 4) % 4, c % 4
        pairs.append((c, ((z + dz) % 2) * 16 + ((y + dy) % 4) * 4 + (x + dx) % 4))
    return pairs


def fetch(value, dz=0, dy=0, dx=0):
    return lax.ppermute(value, "ctx", ctx_shift(-dz, -dy, -dx))


def shards(queries, cache_keys, cache_values, span_keys, span_values, prefix_len, positions, out_weight):
    pos_row = positions.reshape(1, 32)
    tile, kv = call(
        pack,
        [sds(32, QW), sds(4 * HALF + META, HD)],
        [prefix_len, queries, cache_keys, cache_values, span_keys, span_values, pos_row],
        scratch=[
            pltpu.VMEM((2 * HALF, HD), BF),
            pltpu.VMEM((2 * HALF, HD), BF),
            pltpu.VMEM((1, 32), jnp.int32),
            pltpu.SemaphoreType.DMA((6,)),
        ],
        smem=(0,),
        raw=(1, 2, 3, 4, 5, 6),
    )
    kv_up = fetch(kv, dy=1)
    kv_down = fetch(kv, dy=-1)
    own = call(pair, sds(64, QW), [tile, fetch(tile, dz=1)])
    far = fetch(own, dx=2)
    tiles = [own, fetch(own, dx=1), fetch(own, dx=-1), far]

    cut = 2 * HALF + META
    whole = [(0, 0), (cut, HALF)]
    acc_a, st_a, span, weight = attend_call(tiles[:1], [kv], [(0, whole)], weight=out_weight, unit=4)
    w_up, w_down = fetch(weight, dx=1), fetch(weight, dx=-1)
    acc_b, st_b, _, weight = attend_call(tiles[1:], [kv], [(0, whole)], weight=weight, unit=4)
    far_a = fetch(kv_up[:cut], dy=1)
    far_b = fetch(kv_down[cut:], dy=-1)
    acc, st, *spans = attend_call(
        tiles, [kv_up, kv_down], [(0, whole), (1, whole)], accs=[acc_a, acc_b], sts=[st_a, st_b], unit=2
    )

    def finish(picks, unit, idle=(), weight=None):
        return attend_call(
            [tiles[i] for i in picks],
            [far_a, far_b],
            [(0, [(0, 0)]), (0, [(0, HALF)])],
            spans=[span] + spans,
            accs=[acc],
            sts=[st],
            weight=weight,
            idle=idle,
            picks=picks,
            unit=unit,
        )

    part_3, part_1, part_2 = finish((3, 1, 2), 2, idle=[w_up, w_down])
    got_3, got_1, got_2 = fetch(part_3, dx=-2), fetch(part_1, dx=-1), fetch(part_2, dx=1)
    (part_0,) = finish((0,), 4, idle=[part_3])
    weights = [out_weight, w_up, w_down, fetch(weight, dx=2)]
    joined = call(join_x, sds(64, QW), [part_0, got_1, got_2, got_3])
    attended = call(join_z, sds(64, GROUP * HD), [joined, fetch(joined, dz=1)])
    rows = [attended] + [fetch(attended, dy=d) for d in (1, -1, 2)]
    keep, send = call(
        project,
        [sds(128, 1024), sds(128, 1024)],
        rows + weights,
        scratch=[pltpu.VMEM((256, 1024), BF)],
        flops=2 * 256 * 1024 * 1024,
        nbytes=4 << 20,
    )
    got = lax.ppermute(send, "head", [(h, h ^ 1) for h in range(8)])
    own, *others = call(add_cores, [sds(32, 1024)] * 4, [keep, got])
    others = [lax.ppermute(o, "head", [(h, h ^ (2 * k)) for h in range(8)]) for k, o in zip((1, 2, 3), others)]
    pieces = call(add_z, [sds(32, 256)] * 4, [own] + others)
    pieces = [pieces[0]] + [fetch(pieces[i], dx=-d) for i, d in ((1, 1), (2, -1), (3, 2))]
    pieces = [pieces[0], pieces[2], pieces[1], pieces[3]]
    return call(place, sds(128, 256), pieces)


def solution(mesh):
    return jax.shard_map(
        shards,
        mesh=mesh,
        in_specs=(
            P("ctx", "head"),
            P("ctx", "head"),
            P("ctx", "head"),
            P("ctx", "head"),
            P("ctx", "head"),
            P("ctx"),
            P("ctx"),
            P("head", "ctx"),
        ),
        out_specs=P("head", "ctx"),
        check_vma=False,
    )
```

```python
import functools
import math

import jax
import jax.numpy as jnp
from jax import lax
from jax.experimental import pallas as pl
from jax.experimental.pallas import tpu as pltpu
from jax.sharding import PartitionSpec as P

BF = jnp.bfloat16
F32 = jnp.float32
HD = 128
GROUP = 8
HALF = 1024
META = 128
QW = GROUP * HD + 128
LOG2_SCALE = math.log2(math.e) / math.sqrt(HD)
NEG = -1e30


def call(body, out_shape, args, scratch=(), smem=(), idle=(), raw=(), flops=0, nbytes=0, vmem=8 << 20):
    args, specs = list(args), []
    for i in range(len(args)):
        if i in smem:
            specs.append(pl.BlockSpec(memory_space=pltpu.SMEM))
        elif i in raw:
            specs.append(pl.BlockSpec(memory_space=pltpu.HBM))
            args[i] = pltpu.with_memory_space_constraint(args[i], pltpu.HBM)
        elif i in idle:
            specs.append(pl.BlockSpec(memory_space=pl.ANY))
        else:
            specs.append(pl.BlockSpec(memory_space=pltpu.VMEM))
    return pl.pallas_call(
        body,
        out_shape=out_shape,
        in_specs=specs,
        out_specs=jax.tree.map(lambda _: pl.BlockSpec(memory_space=pltpu.VMEM), out_shape),
        scratch_shapes=list(scratch),
        cost_estimate=pl.CostEstimate(flops=flops, bytes_accessed=nbytes, transcendentals=0),
        compiler_params=pltpu.CompilerParams(vmem_limit_bytes=vmem),
    )(*args)


def sds(*shape, dtype=BF):
    return jax.ShapeDtypeStruct(shape, dtype)


def pack(len_ref, q_hbm, k_hbm, v_hbm, sk_hbm, sv_hbm, pos_hbm, tile_ref, out_ref, k_ref, v_ref, pos_ref, sems):
    meta = 2 * HALF
    copies = [
        pltpu.make_async_copy(k_hbm, k_ref, sems.at[0]),
        pltpu.make_async_copy(v_hbm, v_ref, sems.at[1]),
        pltpu.make_async_copy(sk_hbm, out_ref.at[meta : meta + 32], sems.at[2]),
        pltpu.make_async_copy(sv_hbm, out_ref.at[meta + 32 : meta + 64], sems.at[3]),
        pltpu.make_async_copy(q_hbm, tile_ref.at[:, : GROUP * HD], sems.at[4]),
    ]
    pos_copy = pltpu.make_async_copy(pos_hbm, pos_ref, sems.at[5])
    pos_copy.start()
    for copy in copies:
        copy.start()
    pos_copy.wait()
    pos = jnp.broadcast_to(pos_ref[...], (32, 32))
    row = lax.broadcasted_iota(jnp.int32, (32, 32), 0)
    col = lax.broadcasted_iota(jnp.int32, (32, 32), 1)
    column = jnp.sum(jnp.where(row == col, pos, 0), axis=1, keepdims=True)
    lane = lax.broadcasted_iota(jnp.int32, (32, 128), 1)
    numbers = jnp.where(lane == 0, column // 32, jnp.where(lane == 1, column % 32, 0))
    tile_ref[:, GROUP * HD :] = numbers.astype(F32).astype(BF)
    for copy in copies:
        copy.wait()
    used = len_ref[0]
    first = jnp.broadcast_to(k_ref[0:1, :].astype(F32), (HD, HD))
    for half in range(2):
        base = half * (2 * HALF + META)
        for block in range(HALF // HD):
            start = half * HALF + block * HD
            seen = lax.broadcasted_iota(jnp.int32, (HD, HD), 0) + start < used
            keys = jnp.where(seen, k_ref[start : start + HD, :].astype(F32), first)
            out_ref[base + block * HD : base + (block + 1) * HD, :] = keys.astype(BF)
            values = jnp.where(seen, v_ref[start : start + HD, :].astype(F32), 0.0)
            out_ref[base + HALF + block * HD : base + HALF + (block + 1) * HD, :] = values.astype(BF)
    pos = jnp.concatenate([pos_ref[...], jnp.zeros((1, 96), jnp.int32)], axis=1)
    pos = jnp.broadcast_to(pos, (64, HD))
    row = lax.broadcasted_iota(jnp.int32, (64, HD), 0)
    lane = lax.broadcasted_iota(jnp.int32, (64, HD), 1)
    extent = jnp.where(lane == 0, used // 32, jnp.where(lane == 1, used % 32, 0))
    numbers = jnp.where(row == 0, pos // 32, jnp.where(row == 1, pos % 32, jnp.where(row == 2, extent, 0)))
    out_ref[meta + 64 : meta + 128, :] = numbers.astype(F32).astype(BF)


def pair(a_ref, b_ref, out_ref):
    out_ref[0:32, :] = a_ref[...]
    out_ref[32:64, :] = b_ref[...]


def attend(layout, span, n_carry, picks, unit, n_tiles, n_idle, has_weight, *refs):
    last, first = picks is not None, n_carry == 0
    refs = list(refs)
    take = lambda n: [refs.pop(0) for _ in range(n)]
    tiles, kvs, spans = take(n_tiles), take(len(layout)), take(3 if span else 0)
    accs_in, sts_in = take(n_carry), take(n_carry)
    w_in = take(int(has_weight))
    take(n_idle)
    if last:
        outs = take(len(picks))
    else:
        acc_out, st_out = take(2)
        for kv in kvs:
            refs.pop(0)[...] = kv[2 * HALF : 2 * HALF + META, :]
    for w in w_in:
        refs.pop(0)[...] = w[...]
    open_ref, score_a, score_b = refs
    rows = 64 * n_tiles

    def widen(shift, width):
        return shift if shift.shape[1] == 1 else jnp.concatenate([shift] * (width // HD), axis=1)

    def carried(parts, cols):
        if not last:
            return jnp.concatenate([ref[:, cols] for ref in parts], axis=0)
        return jnp.concatenate([parts[0][64 * i : 64 * (i + 1), cols] for i in picks], axis=0)

    blocks = []
    at = 0
    for i, (holder, pieces) in enumerate(layout):
        numbers = kvs[holder][2 * HALF + 64 : 2 * HALF + 80, :].astype(F32)
        used = numbers[2:3, 0:1] * 32.0 + numbers[2:3, 1:2]
        for start, cache_row in pieces:
            index = lax.broadcasted_iota(jnp.int32, (HALF, HD), 0) + cache_row
            open_ref[at : at + HALF, :] = jnp.where(index.astype(F32) < used, 1.0, 0.0).astype(BF)
            blocks += [(at + c, 256, kvs[i], start + c) for c in range(0, HALF, 256)]
            at += HALF
    if span:
        near = [s[...] for s in spans] + [kvs[0][2 * HALF : 2 * HALF + META, :]]
        span_keys = jnp.concatenate([s[0:32, :] for s in near], axis=0)
        span_values = jnp.concatenate([s[32:64, :] for s in near], axis=0)
        open_ref[at : at + HD, :] = jnp.ones((HD, HD), BF)
        near = [s[64:80, :].astype(F32) for s in near]
        key_pos = jnp.concatenate([s[0:1, 0:32] * 32.0 + s[1:2, 0:32] for s in near], axis=1)
        numbers = jnp.concatenate([t[:, GROUP * HD :] for t in tiles], axis=0).astype(F32)
        query_pos = numbers[:, 0:1] * 32.0 + numbers[:, 1:2]
        seen = key_pos <= query_pos
        blocks.append((at, HD, None, 0))
    if span:
        seen = jnp.concatenate([seen] * unit, axis=0)
    lane = lax.broadcasted_iota(jnp.int32, (rows, HD), 1)
    new_st = jnp.zeros((rows, HD), F32)
    peak = None
    for step in range(GROUP // unit + 1):
        mine, previous = (score_a, score_b) if step % 2 == 0 else (score_b, score_a)
        heads = range(step * unit, (step + 1) * unit)
        if step < GROUP // unit:
            query = jnp.concatenate([t[:, h * HD : (h + 1) * HD] for h in heads for t in tiles], axis=0)
            query = query.astype(F32) * LOG2_SCALE
            high = query.astype(BF)
            query = jnp.concatenate([high, (query - high.astype(F32)).astype(BF)], axis=1)
        top = None
        acc = None
        for c, width, kv, row in blocks:
            if step < GROUP // unit:
                keys = span_keys if kv is None else kv[row : row + width, :]
                keys = jnp.concatenate([keys, keys], axis=1)
                s = lax.dot_general(query, keys, (((1,), (1,)), ((), ())), preferred_element_type=F32)
                if kv is None:
                    s = jnp.where(seen, s, NEG)
                mine[:, c : c + width] = s
                for i in range(0, width, HD):
                    top = s[:, i : i + HD] if top is None else jnp.maximum(top, s[:, i : i + HD])
            if step > 0:
                p = jnp.exp2(previous[:, c : c + width] - widen(peak, width)).astype(BF)
                values = span_values if kv is None else kv[row + HALF : row + HALF + width, :]
                values = jnp.concatenate([values, open_ref[c : c + width, :]], axis=1)
                term = jnp.dot(p, values, preferred_element_type=F32)
                acc = term if acc is None else acc + term
        if step > 0:
            for u in range(unit):
                h = (step - 1) * unit + u
                part = slice(u * rows, (u + 1) * rows)
                cols = slice(h * HD, (h + 1) * HD)
                wide = slice(2 * h * HD, 2 * (h + 1) * HD)
                total, shift = acc[part, :], jnp.broadcast_to(peak[part, :], (rows, HD))
                if not first:
                    rescale = jnp.exp2(carried(sts_in, cols) - shift)
                    total = total + carried(accs_in, wide) * jnp.concatenate([rescale, rescale], axis=1)
                if last:
                    new_st = jnp.where(lane == h, shift, new_st)
                    new_st = jnp.where(lane == GROUP + h, total[:, HD:], new_st)
                    for i, out in enumerate(outs):
                        out[:, cols] = total[64 * i : 64 * (i + 1), :HD].astype(BF)
                else:
                    acc_out[:, wide] = total
                    st_out[:, cols] = shift
        if step < GROUP // unit:
            peak = jnp.max(top, axis=1, keepdims=True).astype(BF).astype(F32)
            if not first:
                before = [carried(sts_in, slice(h * HD, h * HD + (HD if last else 1))) for h in heads]
                peak = jnp.maximum(peak, jnp.concatenate(before, axis=0))
    if last:
        high = new_st.astype(BF).astype(F32)
        low = pltpu.roll(new_st - high, GROUP, 1)
        packed = jnp.where(lane < 2 * GROUP, high, jnp.where(lane < 3 * GROUP, low, 0.0)).astype(BF)
        for i, out in enumerate(outs):
            out[:, GROUP * HD :] = packed[64 * i : 64 * (i + 1), :]


def attend_call(tiles, kvs, layout, spans=(), accs=(), sts=(), weight=None, idle=(), picks=None, unit=1):
    n_keys = HALF * sum(len(p) for _, p in layout) + (HD if spans else 0)
    rows = 64 * len(tiles)
    handed = [] if weight is None else [weight]
    args = list(tiles) + list(kvs) + list(spans) + list(accs) + list(sts) + handed + list(idle)
    if picks is not None:
        out = [sds(64, QW) for _ in picks]
    else:
        out = [sds(rows, 2 * GROUP * HD, dtype=F32), sds(rows, GROUP * HD, dtype=F32)] + [sds(META, HD) for _ in kvs]
    out += [sds(*w.shape) for w in handed]
    return call(
        functools.partial(
            attend, layout, bool(spans), len(accs), picks, unit, len(tiles), len(idle), weight is not None
        ),
        out,
        args,
        scratch=[
            pltpu.VMEM((n_keys, HD), BF),
            pltpu.VMEM((rows * unit, n_keys), F32),
            pltpu.VMEM((rows * unit, n_keys), F32),
        ],
        idle=range(len(args) - len(idle), len(args)),
        flops=rows * GROUP * n_keys * HD * 8,
        nbytes=4 << 20,
        vmem=(rows * unit * n_keys * 8) + (8 << 20),
    )


def join(messages, final):
    stats = [m[:, GROUP * HD :].astype(F32) for m in messages]
    sums, peaks, weights = [], [], []
    for h in range(GROUP):
        each = [s[:, h : h + 1] for s in stats]
        peak = functools.reduce(jnp.maximum, each)
        scales = [jnp.exp2(p - peak) for p in each]
        weight = sum(
            (s[:, GROUP + h : GROUP + h + 1] + s[:, 2 * GROUP + h : 2 * GROUP + h + 1]) * c
            for s, c in zip(stats, scales)
        )
        total = sum(m[:, h * HD : (h + 1) * HD].astype(F32) * c for m, c in zip(messages, scales))
        sums.append(total / weight if final else total)
        peaks.append(peak)
        weights.append(weight)
    return sums, peaks, weights


def join_x(a_ref, b_ref, c_ref, d_ref, out_ref):
    messages = [r[...] for r in (a_ref, b_ref, c_ref, d_ref)]
    sums, peaks, weights = join(messages, False)
    lane = lax.broadcasted_iota(jnp.int32, (64, HD), 1)
    numbers = jnp.zeros((64, HD), F32)
    for h in range(GROUP):
        out_ref[:, h * HD : (h + 1) * HD] = sums[h].astype(BF)
        high = weights[h].astype(BF).astype(F32)
        numbers = jnp.where(lane == h, peaks[h], numbers)
        numbers = jnp.where(lane == GROUP + h, high, numbers)
        numbers = jnp.where(lane == 2 * GROUP + h, weights[h] - high, numbers)
    out_ref[:, GROUP * HD :] = numbers.astype(BF)


def join_z(own_ref, other_ref, out_ref):
    other = jnp.concatenate([other_ref[32:64, :], other_ref[0:32, :]], axis=0)
    sums, _, _ = join([own_ref[...], other], True)
    for h in range(GROUP):
        out_ref[:, h * HD : (h + 1) * HD] = sums[h].astype(BF)


def project(a0, a1, a2, a3, w0, w1, w2, w3, keep_ref, send_ref, rows_ref):
    index, core = lax.axis_index("ctx"), lax.rem(lax.axis_index("head"), 2)
    z, y = index // 16, lax.rem(index // 4, 4)
    for a, dy in zip((a0, a1, a2, a3), (0, 1, 3, 2)):
        there = lax.rem(y + dy, 4)
        other = lax.rem(there + core, 2)
        for part in range(2):
            z_there = z if part == 0 else 1 - z
            slot = pl.multiple_of((other * 4 + z_there * 2 + there // 2) * 32, 32)
            rows_ref[pl.ds(slot, 32), :] = a[32 * part : 32 * (part + 1), :]
    for i, w in enumerate((w0, w1, w2, w3)):
        out = jnp.dot(rows_ref[...], w[...], preferred_element_type=F32).astype(BF)
        keep_ref[:, i * 256 : (i + 1) * 256] = out[:128, :]
        send_ref[:, i * 256 : (i + 1) * 256] = out[128:, :]


def add_cores(keep_ref, got_ref, own_ref, o1, o2, o3):
    z_lo = lax.axis_index("head") // 2
    for k, out in enumerate((own_ref, o1, o2, o3)):
        slot = pl.multiple_of((z_lo ^ k) * 32, 32)
        out[...] = (keep_ref[pl.ds(slot, 32), :].astype(F32) + got_ref[pl.ds(slot, 32), :].astype(F32)).astype(BF)


def add_z(a_ref, b_ref, c_ref, d_ref, o0, o1, o2, o3):
    total = sum(r[...].astype(F32) for r in (a_ref, b_ref, c_ref, d_ref)).astype(BF)
    for i, out in enumerate((o0, o1, o2, o3)):
        out[...] = total[:, i * 256 : (i + 1) * 256]


def place(a_ref, b_ref, c_ref, d_ref, out_ref):
    x = lax.rem(lax.axis_index("ctx"), 4)
    for dx, r in zip((0, 1, 3, 2), (a_ref, b_ref, c_ref, d_ref)):
        slot = pl.multiple_of(lax.rem(x + dx, 4) * 32, 32)
        out_ref[pl.ds(slot, 32), :] = r[...]


def ctx_shift(dz, dy, dx):
    pairs = []
    for c in range(32):
        z, y, x = c // 16, (c // 4) % 4, c % 4
        pairs.append((c, ((z + dz) % 2) * 16 + ((y + dy) % 4) * 4 + (x + dx) % 4))
    return pairs


def fetch(value, dz=0, dy=0, dx=0):
    return lax.ppermute(value, "ctx", ctx_shift(-dz, -dy, -dx))


def shards(queries, cache_keys, cache_values, span_keys, span_values, prefix_len, positions, out_weight):
    pos_row = positions.reshape(1, 32)
    tile, kv = call(
        pack,
        [sds(32, QW), sds(4 * HALF + META, HD)],
        [prefix_len, queries, cache_keys, cache_values, span_keys, span_values, pos_row],
        scratch=[
            pltpu.VMEM((2 * HALF, HD), BF),
            pltpu.VMEM((2 * HALF, HD), BF),
            pltpu.VMEM((1, 32), jnp.int32),
            pltpu.SemaphoreType.DMA((6,)),
        ],
        smem=(0,),
        raw=(1, 2, 3, 4, 5, 6),
    )
    kv_up = fetch(kv, dy=1)
    kv_down = fetch(kv, dy=-1)
    own = call(pair, sds(64, QW), [tile, fetch(tile, dz=1)])
    far = fetch(own, dx=2)
    tiles = [own, fetch(own, dx=1), fetch(own, dx=-1), far]

    cut = 2 * HALF + META
    whole = [(0, 0), (cut, HALF)]
    acc_a, st_a, span, weight = attend_call(tiles[:1], [kv], [(0, whole)], weight=out_weight, unit=4)
    w_up, w_down = fetch(weight, dx=1), fetch(weight, dx=-1)
    acc_b, st_b, _, weight = attend_call(tiles[1:], [kv], [(0, whole)], weight=weight, unit=4)
    far_a = fetch(kv_up[:cut], dy=1)
    far_b = fetch(kv_down[cut:], dy=-1)
    acc, st, *spans = attend_call(
        tiles, [kv_up, kv_down], [(0, whole), (1, whole)], accs=[acc_a, acc_b], sts=[st_a, st_b], unit=2
    )

    def finish(picks, unit, idle=(), weight=None):
        return attend_call(
            [tiles[i] for i in picks],
            [far_a, far_b],
            [(0, [(0, 0)]), (0, [(0, HALF)])],
            spans=[span] + spans,
            accs=[acc],
            sts=[st],
            weight=weight,
            idle=idle,
            picks=picks,
            unit=unit,
        )

    (part_3,) = finish((3,), 4, idle=[w_up, w_down])
    got_3 = fetch(part_3, dx=-2)
    part_1, part_2 = finish((1, 2), 2, idle=[part_3])
    got_1, got_2 = fetch(part_1, dx=-1), fetch(part_2, dx=1)
    (part_0,) = finish((0,), 4, idle=[got_3])
    weights = [out_weight, w_up, w_down, fetch(weight, dx=2)]
    joined = call(join_x, sds(64, QW), [part_0, got_1, got_2, got_3])
    attended = call(join_z, sds(64, GROUP * HD), [joined, fetch(joined, dz=1)])
    rows = [attended] + [fetch(attended, dy=d) for d in (1, -1, 2)]
    keep, send = call(
        project,
        [sds(128, 1024), sds(128, 1024)],
        rows + weights,
        scratch=[pltpu.VMEM((256, 1024), BF)],
        flops=2 * 256 * 1024 * 1024,
        nbytes=4 << 20,
    )
    got = lax.ppermute(send, "head", [(h, h ^ 1) for h in range(8)])
    own, *others = call(add_cores, [sds(32, 1024)] * 4, [keep, got])
    others = [lax.ppermute(o, "head", [(h, h ^ (2 * k)) for h in range(8)]) for k, o in zip((1, 2, 3), others)]
    pieces = call(add_z, [sds(32, 256)] * 4, [own] + others)
    pieces = [pieces[0]] + [fetch(pieces[i], dx=-d) for i, d in ((1, 1), (2, -1), (3, 2))]
    pieces = [pieces[0], pieces[2], pieces[1], pieces[3]]
    return call(place, sds(128, 256), pieces)


def solution(mesh):
    return jax.shard_map(
        shards,
        mesh=mesh,
        in_specs=(
            P("ctx", "head"),
            P("ctx", "head"),
            P("ctx", "head"),
            P("ctx", "head"),
            P("ctx", "head"),
            P("ctx"),
            P("ctx"),
            P("head", "ctx"),
        ),
        out_specs=P("head", "ctx"),
        check_vma=False,
    )
```

```python
import functools
import math

import jax
import jax.numpy as jnp
from jax import lax
from jax.experimental import pallas as pl
from jax.experimental.pallas import tpu as pltpu
from jax.sharding import PartitionSpec as P

BF = jnp.bfloat16
F32 = jnp.float32
HD = 128
GROUP = 8
HALF = 1024
META = 128
QW = GROUP * HD + 128
LOG2_SCALE = math.log2(math.e) / math.sqrt(HD)
NEG = -1e30


def call(body, out_shape, args, scratch=(), smem=(), idle=(), raw=(), flops=0, nbytes=0, vmem=8 << 20):
    args, specs = list(args), []
    for i in range(len(args)):
        if i in smem:
            specs.append(pl.BlockSpec(memory_space=pltpu.SMEM))
        elif i in raw:
            specs.append(pl.BlockSpec(memory_space=pltpu.HBM))
            args[i] = pltpu.with_memory_space_constraint(args[i], pltpu.HBM)
        elif i in idle:
            specs.append(pl.BlockSpec(memory_space=pl.ANY))
        else:
            specs.append(pl.BlockSpec(memory_space=pltpu.VMEM))
    return pl.pallas_call(
        body,
        out_shape=out_shape,
        in_specs=specs,
        out_specs=jax.tree.map(lambda _: pl.BlockSpec(memory_space=pltpu.VMEM), out_shape),
        scratch_shapes=list(scratch),
        cost_estimate=pl.CostEstimate(flops=flops, bytes_accessed=nbytes, transcendentals=0),
        compiler_params=pltpu.CompilerParams(vmem_limit_bytes=vmem),
    )(*args)


def sds(*shape, dtype=BF):
    return jax.ShapeDtypeStruct(shape, dtype)


def pack(len_ref, q_hbm, k_hbm, v_hbm, sk_hbm, sv_hbm, pos_hbm, tile_ref, out_ref, k_ref, v_ref, pos_ref, sems):
    meta = 2 * HALF
    copies = [
        pltpu.make_async_copy(k_hbm, k_ref, sems.at[0]),
        pltpu.make_async_copy(v_hbm, v_ref, sems.at[1]),
        pltpu.make_async_copy(sk_hbm, out_ref.at[meta : meta + 32], sems.at[2]),
        pltpu.make_async_copy(sv_hbm, out_ref.at[meta + 32 : meta + 64], sems.at[3]),
        pltpu.make_async_copy(q_hbm, tile_ref.at[:, : GROUP * HD], sems.at[4]),
    ]
    pos_copy = pltpu.make_async_copy(pos_hbm, pos_ref, sems.at[5])
    pos_copy.start()
    for copy in copies:
        copy.start()
    pos_copy.wait()
    pos = jnp.broadcast_to(pos_ref[...], (32, 32))
    row = lax.broadcasted_iota(jnp.int32, (32, 32), 0)
    col = lax.broadcasted_iota(jnp.int32, (32, 32), 1)
    column = jnp.sum(jnp.where(row == col, pos, 0), axis=1, keepdims=True)
    lane = lax.broadcasted_iota(jnp.int32, (32, 128), 1)
    numbers = jnp.where(lane == 0, column // 32, jnp.where(lane == 1, column % 32, 0))
    tile_ref[:, GROUP * HD :] = numbers.astype(F32).astype(BF)
    for copy in copies:
        copy.wait()
    used = len_ref[0]
    first = jnp.broadcast_to(k_ref[0:1, :].astype(F32), (HD, HD))
    for half in range(2):
        base = half * (2 * HALF + META)
        for block in range(HALF // HD):
            start = half * HALF + block * HD
            seen = lax.broadcasted_iota(jnp.int32, (HD, HD), 0) + start < used
            keys = jnp.where(seen, k_ref[start : start + HD, :].astype(F32), first)
            out_ref[base + block * HD : base + (block + 1) * HD, :] = keys.astype(BF)
            values = jnp.where(seen, v_ref[start : start + HD, :].astype(F32), 0.0)
            out_ref[base + HALF + block * HD : base + HALF + (block + 1) * HD, :] = values.astype(BF)
    pos = jnp.concatenate([pos_ref[...], jnp.zeros((1, 96), jnp.int32)], axis=1)
    pos = jnp.broadcast_to(pos, (64, HD))
    row = lax.broadcasted_iota(jnp.int32, (64, HD), 0)
    lane = lax.broadcasted_iota(jnp.int32, (64, HD), 1)
    extent = jnp.where(lane == 0, used // 32, jnp.where(lane == 1, used % 32, 0))
    numbers = jnp.where(row == 0, pos // 32, jnp.where(row == 1, pos % 32, jnp.where(row == 2, extent, 0)))
    out_ref[meta + 64 : meta + 128, :] = numbers.astype(F32).astype(BF)


def pair(a_ref, b_ref, out_ref):
    out_ref[0:32, :] = a_ref[...]
    out_ref[32:64, :] = b_ref[...]


def attend(layout, span, n_carry, picks, unit, n_tiles, n_idle, has_weight, *refs):
    last, first = picks is not None, n_carry == 0
    refs = list(refs)
    take = lambda n: [refs.pop(0) for _ in range(n)]
    tiles, kvs, spans = take(n_tiles), take(len(layout)), take(3 if span else 0)
    accs_in, sts_in = take(n_carry), take(n_carry)
    w_in = take(int(has_weight))
    take(n_idle)
    if last:
        outs = take(len(picks))
    else:
        acc_out, st_out = take(2)
        for kv in kvs:
            refs.pop(0)[...] = kv[2 * HALF : 2 * HALF + META, :]
    for w in w_in:
        refs.pop(0)[...] = w[...]
    open_ref, score_a, score_b = refs
    rows = 64 * n_tiles

    def widen(shift, width):
        return shift if shift.shape[1] == 1 else jnp.concatenate([shift] * (width // HD), axis=1)

    def carried(parts, cols):
        if not last:
            return jnp.concatenate([ref[:, cols] for ref in parts], axis=0)
        return jnp.concatenate([parts[0][64 * i : 64 * (i + 1), cols] for i in picks], axis=0)

    blocks = []
    at = 0
    for i, (holder, pieces) in enumerate(layout):
        numbers = kvs[holder][2 * HALF + 64 : 2 * HALF + 80, :].astype(F32)
        used = numbers[2:3, 0:1] * 32.0 + numbers[2:3, 1:2]
        for start, cache_row in pieces:
            index = lax.broadcasted_iota(jnp.int32, (HALF, HD), 0) + cache_row
            open_ref[at : at + HALF, :] = jnp.where(index.astype(F32) < used, 1.0, 0.0).astype(BF)
            blocks += [(at + c, 256, kvs[i], start + c) for c in range(0, HALF, 256)]
            at += HALF
    if span:
        near = [s[...] for s in spans] + [kvs[0][2 * HALF : 2 * HALF + META, :]]
        span_keys = jnp.concatenate([s[0:32, :] for s in near], axis=0)
        span_values = jnp.concatenate([s[32:64, :] for s in near], axis=0)
        open_ref[at : at + HD, :] = jnp.ones((HD, HD), BF)
        near = [s[64:80, :].astype(F32) for s in near]
        key_pos = jnp.concatenate([s[0:1, 0:32] * 32.0 + s[1:2, 0:32] for s in near], axis=1)
        numbers = jnp.concatenate([t[:, GROUP * HD :] for t in tiles], axis=0).astype(F32)
        query_pos = numbers[:, 0:1] * 32.0 + numbers[:, 1:2]
        seen = key_pos <= query_pos
        blocks.append((at, HD, None, 0))
    if span:
        seen = jnp.concatenate([seen] * unit, axis=0)
    lane = lax.broadcasted_iota(jnp.int32, (rows, HD), 1)
    new_st = jnp.zeros((rows, HD), F32)
    peak = None
    for step in range(GROUP // unit + 1):
        mine, previous = (score_a, score_b) if step % 2 == 0 else (score_b, score_a)
        heads = range(step * unit, (step + 1) * unit)
        if step < GROUP // unit:
            query = jnp.concatenate([t[:, h * HD : (h + 1) * HD] for h in heads for t in tiles], axis=0)
            query = query.astype(F32) * LOG2_SCALE
            high = query.astype(BF)
            query = jnp.concatenate([high, (query - high.astype(F32)).astype(BF)], axis=1)
        top = None
        acc = None
        for c, width, kv, row in blocks:
            if step < GROUP // unit:
                keys = span_keys if kv is None else kv[row : row + width, :]
                keys = jnp.concatenate([keys, keys], axis=1)
                s = lax.dot_general(query, keys, (((1,), (1,)), ((), ())), preferred_element_type=F32)
                if kv is None:
                    s = jnp.where(seen, s, NEG)
                mine[:, c : c + width] = s
                for i in range(0, width, HD):
                    top = s[:, i : i + HD] if top is None else jnp.maximum(top, s[:, i : i + HD])
            if step > 0:
                p = jnp.exp2(previous[:, c : c + width] - widen(peak, width)).astype(BF)
                values = span_values if kv is None else kv[row + HALF : row + HALF + width, :]
                values = jnp.concatenate([values, open_ref[c : c + width, :]], axis=1)
                term = jnp.dot(p, values, preferred_element_type=F32)
                acc = term if acc is None else acc + term
        if step > 0:
            for u in range(unit):
                h = (step - 1) * unit + u
                part = slice(u * rows, (u + 1) * rows)
                cols = slice(h * HD, (h + 1) * HD)
                wide = slice(2 * h * HD, 2 * (h + 1) * HD)
                total, shift = acc[part, :], jnp.broadcast_to(peak[part, :], (rows, HD))
                if not first:
                    rescale = jnp.exp2(carried(sts_in, cols) - shift)
                    total = total + carried(accs_in, wide) * jnp.concatenate([rescale, rescale], axis=1)
                if last:
                    new_st = jnp.where(lane == h, shift, new_st)
                    new_st = jnp.where(lane == GROUP + h, total[:, HD:], new_st)
                    for i, out in enumerate(outs):
                        out[:, cols] = total[64 * i : 64 * (i + 1), :HD].astype(BF)
                else:
                    acc_out[:, wide] = total
                    st_out[:, cols] = shift
        if step < GROUP // unit:
            peak = jnp.max(top, axis=1, keepdims=True).astype(BF).astype(F32)
            if not first:
                before = [carried(sts_in, slice(h * HD, h * HD + (HD if last else 1))) for h in heads]
                peak = jnp.maximum(peak, jnp.concatenate(before, axis=0))
    if last:
        high = new_st.astype(BF).astype(F32)
        low = pltpu.roll(new_st - high, GROUP, 1)
        packed = jnp.where(lane < 2 * GROUP, high, jnp.where(lane < 3 * GROUP, low, 0.0)).astype(BF)
        for i, out in enumerate(outs):
            out[:, GROUP * HD :] = packed[64 * i : 64 * (i + 1), :]


def attend_call(tiles, kvs, layout, spans=(), accs=(), sts=(), weight=None, idle=(), picks=None, unit=1):
    n_keys = HALF * sum(len(p) for _, p in layout) + (HD if spans else 0)
    rows = 64 * len(tiles)
    handed = [] if weight is None else [weight]
    args = list(tiles) + list(kvs) + list(spans) + list(accs) + list(sts) + handed + list(idle)
    if picks is not None:
        out = [sds(64, QW) for _ in picks]
    else:
        out = [sds(rows, 2 * GROUP * HD, dtype=F32), sds(rows, GROUP * HD, dtype=F32)] + [sds(META, HD) for _ in kvs]
    out += [sds(*w.shape) for w in handed]
    return call(
        functools.partial(
            attend, layout, bool(spans), len(accs), picks, unit, len(tiles), len(idle), weight is not None
        ),
        out,
        args,
        scratch=[
            pltpu.VMEM((n_keys, HD), BF),
            pltpu.VMEM((rows * unit, n_keys), F32),
            pltpu.VMEM((rows * unit, n_keys), F32),
        ],
        idle=range(len(args) - len(idle), len(args)),
        flops=rows * GROUP * n_keys * HD * 8,
        nbytes=4 << 20,
        vmem=(rows * unit * n_keys * 8) + (8 << 20),
    )


def join(messages, final):
    stats = [m[:, GROUP * HD :].astype(F32) for m in messages]
    sums, peaks, weights = [], [], []
    for h in range(GROUP):
        each = [s[:, h : h + 1] for s in stats]
        peak = functools.reduce(jnp.maximum, each)
        scales = [jnp.exp2(p - peak) for p in each]
        weight = sum(
            (s[:, GROUP + h : GROUP + h + 1] + s[:, 2 * GROUP + h : 2 * GROUP + h + 1]) * c
            for s, c in zip(stats, scales)
        )
        total = sum(m[:, h * HD : (h + 1) * HD].astype(F32) * c for m, c in zip(messages, scales))
        sums.append(total / weight if final else total)
        peaks.append(peak)
        weights.append(weight)
    return sums, peaks, weights


def join_x(a_ref, b_ref, c_ref, d_ref, out_ref):
    messages = [r[...] for r in (a_ref, b_ref, c_ref, d_ref)]
    sums, peaks, weights = join(messages, False)
    lane = lax.broadcasted_iota(jnp.int32, (64, HD), 1)
    numbers = jnp.zeros((64, HD), F32)
    for h in range(GROUP):
        out_ref[:, h * HD : (h + 1) * HD] = sums[h].astype(BF)
        high = weights[h].astype(BF).astype(F32)
        numbers = jnp.where(lane == h, peaks[h], numbers)
        numbers = jnp.where(lane == GROUP + h, high, numbers)
        numbers = jnp.where(lane == 2 * GROUP + h, weights[h] - high, numbers)
    out_ref[:, GROUP * HD :] = numbers.astype(BF)


def join_z(own_ref, other_ref, out_ref):
    other = jnp.concatenate([other_ref[32:64, :], other_ref[0:32, :]], axis=0)
    sums, _, _ = join([own_ref[...], other], True)
    for h in range(GROUP):
        out_ref[:, h * HD : (h + 1) * HD] = sums[h].astype(BF)


def project(a0, a1, a2, a3, w0, w1, w2, w3, keep_ref, send_ref, rows_ref):
    index, core = lax.axis_index("ctx"), lax.rem(lax.axis_index("head"), 2)
    z, y = index // 16, lax.rem(index // 4, 4)
    for a, dy in zip((a0, a1, a2, a3), (0, 1, 3, 2)):
        there = lax.rem(y + dy, 4)
        other = lax.rem(there + core, 2)
        for part in range(2):
            z_there = z if part == 0 else 1 - z
            slot = pl.multiple_of((other * 4 + z_there * 2 + there // 2) * 32, 32)
            rows_ref[pl.ds(slot, 32), :] = a[32 * part : 32 * (part + 1), :]
    for i, w in enumerate((w0, w1, w2, w3)):
        out = jnp.dot(rows_ref[...], w[...], preferred_element_type=F32).astype(BF)
        keep_ref[:, i * 256 : (i + 1) * 256] = out[:128, :]
        send_ref[:, i * 256 : (i + 1) * 256] = out[128:, :]


def add_cores(keep_ref, got_ref, own_ref, o1, o2, o3):
    z_lo = lax.axis_index("head") // 2
    for k, out in enumerate((own_ref, o1, o2, o3)):
        slot = pl.multiple_of((z_lo ^ k) * 32, 32)
        out[...] = (keep_ref[pl.ds(slot, 32), :].astype(F32) + got_ref[pl.ds(slot, 32), :].astype(F32)).astype(BF)


def add_z(a_ref, b_ref, c_ref, d_ref, o0, o1, o2, o3):
    total = sum(r[...].astype(F32) for r in (a_ref, b_ref, c_ref, d_ref)).astype(BF)
    for i, out in enumerate((o0, o1, o2, o3)):
        out[...] = total[:, i * 256 : (i + 1) * 256]


def place(a_ref, b_ref, c_ref, d_ref, out_ref):
    x = lax.rem(lax.axis_index("ctx"), 4)
    for dx, r in zip((0, 1, 3, 2), (a_ref, b_ref, c_ref, d_ref)):
        slot = pl.multiple_of(lax.rem(x + dx, 4) * 32, 32)
        out_ref[pl.ds(slot, 32), :] = r[...]


def ctx_shift(dz, dy, dx):
    pairs = []
    for c in range(32):
        z, y, x = c // 16, (c // 4) % 4, c % 4
        pairs.append((c, ((z + dz) % 2) * 16 + ((y + dy) % 4) * 4 + (x + dx) % 4))
    return pairs


def fetch(value, dz=0, dy=0, dx=0):
    return lax.ppermute(value, "ctx", ctx_shift(-dz, -dy, -dx))


def shards(queries, cache_keys, cache_values, span_keys, span_values, prefix_len, positions, out_weight):
    pos_row = positions.reshape(1, 32)
    tile, kv = call(
        pack,
        [sds(32, QW), sds(4 * HALF + META, HD)],
        [prefix_len, queries, cache_keys, cache_values, span_keys, span_values, pos_row],
        scratch=[
            pltpu.VMEM((2 * HALF, HD), BF),
            pltpu.VMEM((2 * HALF, HD), BF),
            pltpu.VMEM((1, 32), jnp.int32),
            pltpu.SemaphoreType.DMA((6,)),
        ],
        smem=(0,),
        raw=(1, 2, 3, 4, 5, 6),
    )
    kv_up = fetch(kv, dy=1)
    kv_down = fetch(kv, dy=-1)
    own = call(pair, sds(64, QW), [tile, fetch(tile, dz=1)])
    far = fetch(own, dx=2)
    tiles = [own, fetch(own, dx=1), fetch(own, dx=-1), far]

    cut = 2 * HALF + META
    whole = [(0, 0), (cut, HALF)]
    acc_a, st_a, span, weight = attend_call(tiles[:1], [kv], [(0, whole)], weight=out_weight, unit=4)
    w_up, w_down = fetch(weight, dx=1), fetch(weight, dx=-1)
    acc_b, st_b, _, weight = attend_call(tiles[1:], [kv], [(0, whole)], weight=weight, unit=4)
    far_a = fetch(kv_up[:cut], dy=1)
    far_b = fetch(kv_down[cut:], dy=-1)
    acc, st, *spans = attend_call(
        tiles, [kv_up, kv_down], [(0, whole), (1, whole)], accs=[acc_a, acc_b], sts=[st_a, st_b], unit=2
    )

    def finish(picks, unit, idle=(), weight=None):
        return attend_call(
            [tiles[i] for i in picks],
            [far_a, far_b],
            [(0, [(0, 0)]), (0, [(0, HALF)])],
            spans=[span] + spans,
            accs=[acc],
            sts=[st],
            weight=weight,
            idle=idle,
            picks=picks,
            unit=unit,
        )

    (part_3,) = finish((3,), 4)
    got_3 = fetch(part_3, dx=-2)
    part_1, part_2 = finish((1, 2), 2, idle=[part_3, w_up, w_down])
    got_1, got_2 = fetch(part_1, dx=-1), fetch(part_2, dx=1)
    (part_0,) = finish((0,), 4, idle=[got_3])
    weights = [out_weight, w_up, w_down, fetch(weight, dx=2)]
    joined = call(join_x, sds(64, QW), [part_0, got_1, got_2, got_3])
    attended = call(join_z, sds(64, GROUP * HD), [joined, fetch(joined, dz=1)])
    rows = [attended] + [fetch(attended, dy=d) for d in (1, -1, 2)]
    keep, send = call(
        project,
        [sds(128, 1024), sds(128, 1024)],
        rows + weights,
        scratch=[pltpu.VMEM((256, 1024), BF)],
        flops=2 * 256 * 1024 * 1024,
        nbytes=4 << 20,
    )
    got = lax.ppermute(send, "head", [(h, h ^ 1) for h in range(8)])
    own, *others = call(add_cores, [sds(32, 1024)] * 4, [keep, got])
    others = [lax.ppermute(o, "head", [(h, h ^ (2 * k)) for h in range(8)]) for k, o in zip((1, 2, 3), others)]
    pieces = call(add_z, [sds(32, 256)] * 4, [own] + others)
    pieces = [pieces[0]] + [fetch(pieces[i], dx=-d) for i, d in ((1, 1), (2, -1), (3, 2))]
    pieces = [pieces[0], pieces[2], pieces[1], pieces[3]]
    return call(place, sds(128, 256), pieces)


def solution(mesh):
    return jax.shard_map(
        shards,
        mesh=mesh,
        in_specs=(
            P("ctx", "head"),
            P("ctx", "head"),
            P("ctx", "head"),
            P("ctx", "head"),
            P("ctx", "head"),
            P("ctx"),
            P("ctx"),
            P("head", "ctx"),
        ),
        out_specs=P("head", "ctx"),
        check_vma=False,
    )
```

```python
import functools
import math

import jax
import jax.numpy as jnp
from jax import lax
from jax.experimental import pallas as pl
from jax.experimental.pallas import tpu as pltpu
from jax.sharding import PartitionSpec as P

BF = jnp.bfloat16
F32 = jnp.float32
HD = 128
GROUP = 8
HALF = 1024
META = 128
QW = GROUP * HD + 128
LOG2_SCALE = math.log2(math.e) / math.sqrt(HD)
NEG = -1e30


def call(body, out_shape, args, scratch=(), smem=(), idle=(), raw=(), flops=0, nbytes=0, vmem=8 << 20):
    args, specs = list(args), []
    for i in range(len(args)):
        if i in smem:
            specs.append(pl.BlockSpec(memory_space=pltpu.SMEM))
        elif i in raw:
            specs.append(pl.BlockSpec(memory_space=pltpu.HBM))
            args[i] = pltpu.with_memory_space_constraint(args[i], pltpu.HBM)
        elif i in idle:
            specs.append(pl.BlockSpec(memory_space=pl.ANY))
        else:
            specs.append(pl.BlockSpec(memory_space=pltpu.VMEM))
    return pl.pallas_call(
        body,
        out_shape=out_shape,
        in_specs=specs,
        out_specs=jax.tree.map(lambda _: pl.BlockSpec(memory_space=pltpu.VMEM), out_shape),
        scratch_shapes=list(scratch),
        cost_estimate=pl.CostEstimate(flops=flops, bytes_accessed=nbytes, transcendentals=0),
        compiler_params=pltpu.CompilerParams(vmem_limit_bytes=vmem),
    )(*args)


def sds(*shape, dtype=BF):
    return jax.ShapeDtypeStruct(shape, dtype)


def pack(len_ref, q_hbm, k_hbm, v_hbm, sk_hbm, sv_hbm, pos_hbm, tile_ref, out_ref, k_ref, v_ref, pos_ref, sems):
    meta = 2 * HALF
    copies = [
        pltpu.make_async_copy(k_hbm, k_ref, sems.at[0]),
        pltpu.make_async_copy(v_hbm, v_ref, sems.at[1]),
        pltpu.make_async_copy(sk_hbm, out_ref.at[meta : meta + 32], sems.at[2]),
        pltpu.make_async_copy(sv_hbm, out_ref.at[meta + 32 : meta + 64], sems.at[3]),
        pltpu.make_async_copy(q_hbm, tile_ref.at[:, : GROUP * HD], sems.at[4]),
    ]
    pos_copy = pltpu.make_async_copy(pos_hbm, pos_ref, sems.at[5])
    pos_copy.start()
    for copy in copies:
        copy.start()
    pos_copy.wait()
    pos = jnp.broadcast_to(pos_ref[...], (32, 32))
    row = lax.broadcasted_iota(jnp.int32, (32, 32), 0)
    col = lax.broadcasted_iota(jnp.int32, (32, 32), 1)
    column = jnp.sum(jnp.where(row == col, pos, 0), axis=1, keepdims=True)
    lane = lax.broadcasted_iota(jnp.int32, (32, 128), 1)
    numbers = jnp.where(lane == 0, column // 32, jnp.where(lane == 1, column % 32, 0))
    tile_ref[:, GROUP * HD :] = numbers.astype(F32).astype(BF)
    for copy in copies:
        copy.wait()
    used = len_ref[0]
    first = jnp.broadcast_to(k_ref[0:1, :].astype(F32), (HD, HD))
    for half in range(2):
        base = half * (2 * HALF + META)
        for block in range(HALF // HD):
            start = half * HALF + block * HD
            seen = lax.broadcasted_iota(jnp.int32, (HD, HD), 0) + start < used
            keys = jnp.where(seen, k_ref[start : start + HD, :].astype(F32), first)
            out_ref[base + block * HD : base + (block + 1) * HD, :] = keys.astype(BF)
            values = jnp.where(seen, v_ref[start : start + HD, :].astype(F32), 0.0)
            out_ref[base + HALF + block * HD : base + HALF + (block + 1) * HD, :] = values.astype(BF)
    pos = jnp.concatenate([pos_ref[...], jnp.zeros((1, 96), jnp.int32)], axis=1)
    pos = jnp.broadcast_to(pos, (64, HD))
    row = lax.broadcasted_iota(jnp.int32, (64, HD), 0)
    lane = lax.broadcasted_iota(jnp.int32, (64, HD), 1)
    extent = jnp.where(lane == 0, used // 32, jnp.where(lane == 1, used % 32, 0))
    numbers = jnp.where(row == 0, pos // 32, jnp.where(row == 1, pos % 32, jnp.where(row == 2, extent, 0)))
    out_ref[meta + 64 : meta + 128, :] = numbers.astype(F32).astype(BF)


def pair(a_ref, b_ref, out_ref):
    out_ref[0:32, :] = a_ref[...]
    out_ref[32:64, :] = b_ref[...]


def attend(layout, span, n_carry, picks, unit, n_tiles, n_idle, has_weight, *refs):
    last, first = picks is not None, n_carry == 0
    refs = list(refs)
    take = lambda n: [refs.pop(0) for _ in range(n)]
    tiles, kvs, spans = take(n_tiles), take(len(layout)), take(3 if span else 0)
    accs_in, sts_in = take(n_carry), take(n_carry)
    w_in = take(int(has_weight))
    take(n_idle)
    if last:
        outs = take(len(picks))
    else:
        acc_out, st_out = take(2)
        for kv in kvs:
            refs.pop(0)[...] = kv[2 * HALF : 2 * HALF + META, :]
    for w in w_in:
        refs.pop(0)[...] = w[...]
    open_ref, score_a, score_b = refs
    rows = 64 * n_tiles

    def widen(shift, width):
        return shift if shift.shape[1] == 1 else jnp.concatenate([shift] * (width // HD), axis=1)

    def carried(parts, cols):
        if not last:
            return jnp.concatenate([ref[:, cols] for ref in parts], axis=0)
        return jnp.concatenate([parts[0][64 * i : 64 * (i + 1), cols] for i in picks], axis=0)

    blocks = []
    at = 0
    for i, (holder, pieces) in enumerate(layout):
        numbers = kvs[holder][2 * HALF + 64 : 2 * HALF + 80, :].astype(F32)
        used = numbers[2:3, 0:1] * 32.0 + numbers[2:3, 1:2]
        for start, cache_row in pieces:
            index = lax.broadcasted_iota(jnp.int32, (HALF, HD), 0) + cache_row
            open_ref[at : at + HALF, :] = jnp.where(index.astype(F32) < used, 1.0, 0.0).astype(BF)
            blocks += [(at + c, 256, kvs[i], start + c) for c in range(0, HALF, 256)]
            at += HALF
    if span:
        near = [s[...] for s in spans] + [kvs[0][2 * HALF : 2 * HALF + META, :]]
        span_keys = jnp.concatenate([s[0:32, :] for s in near], axis=0)
        span_values = jnp.concatenate([s[32:64, :] for s in near], axis=0)
        open_ref[at : at + HD, :] = jnp.ones((HD, HD), BF)
        near = [s[64:80, :].astype(F32) for s in near]
        key_pos = jnp.concatenate([s[0:1, 0:32] * 32.0 + s[1:2, 0:32] for s in near], axis=1)
        numbers = jnp.concatenate([t[:, GROUP * HD :] for t in tiles], axis=0).astype(F32)
        query_pos = numbers[:, 0:1] * 32.0 + numbers[:, 1:2]
        seen = key_pos <= query_pos
        blocks.append((at, HD, None, 0))
    if span:
        seen = jnp.concatenate([seen] * unit, axis=0)
    lane = lax.broadcasted_iota(jnp.int32, (rows, HD), 1)
    new_st = jnp.zeros((rows, HD), F32)
    peak = None
    for step in range(GROUP // unit + 1):
        mine, previous = (score_a, score_b) if step % 2 == 0 else (score_b, score_a)
        heads = range(step * unit, (step + 1) * unit)
        if step < GROUP // unit:
            query = jnp.concatenate([t[:, h * HD : (h + 1) * HD] for h in heads for t in tiles], axis=0)
            query = query.astype(F32) * LOG2_SCALE
            high = query.astype(BF)
            query = jnp.concatenate([high, (query - high.astype(F32)).astype(BF)], axis=1)
        top = None
        acc = None
        for c, width, kv, row in blocks:
            if step < GROUP // unit:
                keys = span_keys if kv is None else kv[row : row + width, :]
                keys = jnp.concatenate([keys, keys], axis=1)
                s = lax.dot_general(query, keys, (((1,), (1,)), ((), ())), preferred_element_type=F32)
                if kv is None:
                    s = jnp.where(seen, s, NEG)
                mine[:, c : c + width] = s
                for i in range(0, width, HD):
                    top = s[:, i : i + HD] if top is None else jnp.maximum(top, s[:, i : i + HD])
            if step > 0:
                p = jnp.exp2(previous[:, c : c + width] - widen(peak, width)).astype(BF)
                values = span_values if kv is None else kv[row + HALF : row + HALF + width, :]
                values = jnp.concatenate([values, open_ref[c : c + width, :]], axis=1)
                term = jnp.dot(p, values, preferred_element_type=F32)
                acc = term if acc is None else acc + term
        if step > 0:
            for u in range(unit):
                h = (step - 1) * unit + u
                part = slice(u * rows, (u + 1) * rows)
                cols = slice(h * HD, (h + 1) * HD)
                wide = slice(2 * h * HD, 2 * (h + 1) * HD)
                total, shift = acc[part, :], jnp.broadcast_to(peak[part, :], (rows, HD))
                if not first:
                    rescale = jnp.exp2(carried(sts_in, cols) - shift)
                    total = total + carried(accs_in, wide) * jnp.concatenate([rescale, rescale], axis=1)
                if last:
                    new_st = jnp.where(lane == h, shift, new_st)
                    new_st = jnp.where(lane == GROUP + h, total[:, HD:], new_st)
                    for i, out in enumerate(outs):
                        out[:, cols] = total[64 * i : 64 * (i + 1), :HD].astype(BF)
                else:
                    acc_out[:, wide] = total
                    st_out[:, cols] = shift
        if step < GROUP // unit:
            peak = jnp.max(top, axis=1, keepdims=True).astype(BF).astype(F32)
            if not first:
                before = [carried(sts_in, slice(h * HD, h * HD + (HD if last else 1))) for h in heads]
                peak = jnp.maximum(peak, jnp.concatenate(before, axis=0))
    if last:
        high = new_st.astype(BF).astype(F32)
        low = pltpu.roll(new_st - high, GROUP, 1)
        packed = jnp.where(lane < 2 * GROUP, high, jnp.where(lane < 3 * GROUP, low, 0.0)).astype(BF)
        for i, out in enumerate(outs):
            out[:, GROUP * HD :] = packed[64 * i : 64 * (i + 1), :]


def attend_call(tiles, kvs, layout, spans=(), accs=(), sts=(), weight=None, idle=(), picks=None, unit=1):
    n_keys = HALF * sum(len(p) for _, p in layout) + (HD if spans else 0)
    rows = 64 * len(tiles)
    handed = [] if weight is None else [weight]
    args = list(tiles) + list(kvs) + list(spans) + list(accs) + list(sts) + handed + list(idle)
    if picks is not None:
        out = [sds(64, QW) for _ in picks]
    else:
        out = [sds(rows, 2 * GROUP * HD, dtype=F32), sds(rows, GROUP * HD, dtype=F32)] + [sds(META, HD) for _ in kvs]
    out += [sds(*w.shape) for w in handed]
    return call(
        functools.partial(
            attend, layout, bool(spans), len(accs), picks, unit, len(tiles), len(idle), weight is not None
        ),
        out,
        args,
        scratch=[
            pltpu.VMEM((n_keys, HD), BF),
            pltpu.VMEM((rows * unit, n_keys), F32),
            pltpu.VMEM((rows * unit, n_keys), F32),
        ],
        idle=range(len(args) - len(idle), len(args)),
        flops=rows * GROUP * n_keys * HD * 8,
        nbytes=4 << 20,
        vmem=(rows * unit * n_keys * 8) + (8 << 20),
    )


def join(messages, final):
    stats = [m[:, GROUP * HD :].astype(F32) for m in messages]
    sums, peaks, weights = [], [], []
    for h in range(GROUP):
        each = [s[:, h : h + 1] for s in stats]
        peak = functools.reduce(jnp.maximum, each)
        scales = [jnp.exp2(p - peak) for p in each]
        weight = sum(
            (s[:, GROUP + h : GROUP + h + 1] + s[:, 2 * GROUP + h : 2 * GROUP + h + 1]) * c
            for s, c in zip(stats, scales)
        )
        total = sum(m[:, h * HD : (h + 1) * HD].astype(F32) * c for m, c in zip(messages, scales))
        sums.append(total / weight if final else total)
        peaks.append(peak)
        weights.append(weight)
    return sums, peaks, weights


def join_x(a_ref, b_ref, c_ref, d_ref, out_ref):
    messages = [r[...] for r in (a_ref, b_ref, c_ref, d_ref)]
    sums, peaks, weights = join(messages, False)
    lane = lax.broadcasted_iota(jnp.int32, (64, HD), 1)
    numbers = jnp.zeros((64, HD), F32)
    for h in range(GROUP):
        out_ref[:, h * HD : (h + 1) * HD] = sums[h].astype(BF)
        high = weights[h].astype(BF).astype(F32)
        numbers = jnp.where(lane == h, peaks[h], numbers)
        numbers = jnp.where(lane == GROUP + h, high, numbers)
        numbers = jnp.where(lane == 2 * GROUP + h, weights[h] - high, numbers)
    out_ref[:, GROUP * HD :] = numbers.astype(BF)


def hand(w_ref, _, *outs):
    depth = w_ref.shape[0] // len(outs)
    for i, out in enumerate(outs):
        out[...] = w_ref[i * depth : (i + 1) * depth, :]


def join_z(own_ref, other_ref, out_ref):
    other = jnp.concatenate([other_ref[32:64, :], other_ref[0:32, :]], axis=0)
    sums, _, _ = join([own_ref[...], other], True)
    for h in range(GROUP):
        out_ref[:, h * HD : (h + 1) * HD] = sums[h].astype(BF)


def project(a0, a1, a2, a3, w0, w1, w2, *refs):
    *w3, keep_ref, send_ref, rows_ref = refs
    index, core = lax.axis_index("ctx"), lax.rem(lax.axis_index("head"), 2)
    z, y = index // 16, lax.rem(index // 4, 4)
    for a, dy in zip((a0, a1, a2, a3), (0, 1, 3, 2)):
        there = lax.rem(y + dy, 4)
        other = lax.rem(there + core, 2)
        for part in range(2):
            z_there = z if part == 0 else 1 - z
            slot = pl.multiple_of((other * 4 + z_there * 2 + there // 2) * 32, 32)
            rows_ref[pl.ds(slot, 32), :] = a[32 * part : 32 * (part + 1), :]
    for i, ws in enumerate(((w0,), (w1,), (w2,), w3)):
        depth = 1024 // len(ws)
        out = sum(
            jnp.dot(rows_ref[:, k * depth : (k + 1) * depth], w[...], preferred_element_type=F32)
            for k, w in enumerate(ws)
        ).astype(BF)
        keep_ref[:, i * 256 : (i + 1) * 256] = out[:128, :]
        send_ref[:, i * 256 : (i + 1) * 256] = out[128:, :]


def add_cores(keep_ref, got_ref, own_ref, o1, o2, o3):
    z_lo = lax.axis_index("head") // 2
    for k, out in enumerate((own_ref, o1, o2, o3)):
        slot = pl.multiple_of((z_lo ^ k) * 32, 32)
        out[...] = (keep_ref[pl.ds(slot, 32), :].astype(F32) + got_ref[pl.ds(slot, 32), :].astype(F32)).astype(BF)


def add_z(a_ref, b_ref, c_ref, d_ref, o0, o1, o2, o3):
    total = sum(r[...].astype(F32) for r in (a_ref, b_ref, c_ref, d_ref)).astype(BF)
    for i, out in enumerate((o0, o1, o2, o3)):
        out[...] = total[:, i * 256 : (i + 1) * 256]


def place(a_ref, b_ref, c_ref, d_ref, out_ref):
    x = lax.rem(lax.axis_index("ctx"), 4)
    for dx, r in zip((0, 1, 3, 2), (a_ref, b_ref, c_ref, d_ref)):
        slot = pl.multiple_of(lax.rem(x + dx, 4) * 32, 32)
        out_ref[pl.ds(slot, 32), :] = r[...]


def ctx_shift(dz, dy, dx):
    pairs = []
    for c in range(32):
        z, y, x = c // 16, (c // 4) % 4, c % 4
        pairs.append((c, ((z + dz) % 2) * 16 + ((y + dy) % 4) * 4 + (x + dx) % 4))
    return pairs


def fetch(value, dz=0, dy=0, dx=0):
    return lax.ppermute(value, "ctx", ctx_shift(-dz, -dy, -dx))


def shards(queries, cache_keys, cache_values, span_keys, span_values, prefix_len, positions, out_weight):
    pos_row = positions.reshape(1, 32)
    tile, kv = call(
        pack,
        [sds(32, QW), sds(4 * HALF + META, HD)],
        [prefix_len, queries, cache_keys, cache_values, span_keys, span_values, pos_row],
        scratch=[
            pltpu.VMEM((2 * HALF, HD), BF),
            pltpu.VMEM((2 * HALF, HD), BF),
            pltpu.VMEM((1, 32), jnp.int32),
            pltpu.SemaphoreType.DMA((6,)),
        ],
        smem=(0,),
        raw=(1, 2, 3, 4, 5, 6),
    )
    kv_up = fetch(kv, dy=1)
    kv_down = fetch(kv, dy=-1)
    own = call(pair, sds(64, QW), [tile, fetch(tile, dz=1)])
    far = fetch(own, dx=2)
    tiles = [own, fetch(own, dx=1), fetch(own, dx=-1), far]

    cut = 2 * HALF + META
    whole = [(0, 0), (cut, HALF)]
    acc_a, st_a, span, weight = attend_call(tiles[:1], [kv], [(0, whole)], weight=out_weight, unit=4)
    w_up, w_down = fetch(weight, dx=1), fetch(weight, dx=-1)
    acc_b, st_b, _ = attend_call(tiles[1:], [kv], [(0, whole)], unit=4)
    far_a = fetch(kv_up[:cut], dy=1)
    far_b = fetch(kv_down[cut:], dy=-1)
    acc, st, *spans = attend_call(
        tiles, [kv_up, kv_down], [(0, whole), (1, whole)], accs=[acc_a, acc_b], sts=[st_a, st_b], unit=2
    )

    def finish(picks, unit, idle=(), weight=None):
        return attend_call(
            [tiles[i] for i in picks],
            [far_a, far_b],
            [(0, [(0, 0)]), (0, [(0, HALF)])],
            spans=[span] + spans,
            accs=[acc],
            sts=[st],
            weight=weight,
            idle=idle,
            picks=picks,
            unit=unit,
        )

    (part_3,) = finish((3,), 4)
    got_3 = fetch(part_3, dx=-2)
    part_1, part_2 = finish((1, 2), 2, idle=[part_3, w_up, w_down])
    got_1, got_2 = fetch(part_1, dx=-1), fetch(part_2, dx=1)
    (part_0,) = finish((0,), 4, idle=[got_3])
    joined = call(join_x, sds(64, QW), [part_0, got_1, got_2, got_3])
    halves = call(hand, [sds(512, 256)] * 2, [weight, joined], idle=(1,))
    weights = [out_weight, w_up, w_down] + [fetch(h, dx=2) for h in halves]
    attended = call(join_z, sds(64, GROUP * HD), [joined, fetch(joined, dz=1)])
    rows = [attended] + [fetch(attended, dy=d) for d in (1, -1, 2)]
    keep, send = call(
        project,
        [sds(128, 1024), sds(128, 1024)],
        rows + weights,
        scratch=[pltpu.VMEM((256, 1024), BF)],
        flops=2 * 256 * 1024 * 1024,
        nbytes=4 << 20,
    )
    got = lax.ppermute(send, "head", [(h, h ^ 1) for h in range(8)])
    own, *others = call(add_cores, [sds(32, 1024)] * 4, [keep, got])
    others = [lax.ppermute(o, "head", [(h, h ^ (2 * k)) for h in range(8)]) for k, o in zip((1, 2, 3), others)]
    pieces = call(add_z, [sds(32, 256)] * 4, [own] + others)
    pieces = [pieces[0]] + [fetch(pieces[i], dx=-d) for i, d in ((1, 1), (2, -1), (3, 2))]
    pieces = [pieces[0], pieces[2], pieces[1], pieces[3]]
    return call(place, sds(128, 256), pieces)


def solution(mesh):
    return jax.shard_map(
        shards,
        mesh=mesh,
        in_specs=(
            P("ctx", "head"),
            P("ctx", "head"),
            P("ctx", "head"),
            P("ctx", "head"),
            P("ctx", "head"),
            P("ctx"),
            P("ctx"),
            P("head", "ctx"),
        ),
        out_specs=P("head", "ctx"),
        check_vma=False,
    )
```

```python
import functools
import math

import jax
import jax.numpy as jnp
from jax import lax
from jax.experimental import pallas as pl
from jax.experimental.pallas import tpu as pltpu
from jax.sharding import PartitionSpec as P

BF = jnp.bfloat16
F32 = jnp.float32
HD = 128
GROUP = 8
HALF = 1024
META = 128
QW = GROUP * HD + 128
LOG2_SCALE = math.log2(math.e) / math.sqrt(HD)
NEG = -1e30


def call(body, out_shape, args, scratch=(), smem=(), idle=(), raw=(), flops=0, nbytes=0, vmem=8 << 20):
    args, specs = list(args), []
    for i in range(len(args)):
        if i in smem:
            specs.append(pl.BlockSpec(memory_space=pltpu.SMEM))
        elif i in raw:
            specs.append(pl.BlockSpec(memory_space=pltpu.HBM))
            args[i] = pltpu.with_memory_space_constraint(args[i], pltpu.HBM)
        elif i in idle:
            specs.append(pl.BlockSpec(memory_space=pl.ANY))
        else:
            specs.append(pl.BlockSpec(memory_space=pltpu.VMEM))
    return pl.pallas_call(
        body,
        out_shape=out_shape,
        in_specs=specs,
        out_specs=jax.tree.map(lambda _: pl.BlockSpec(memory_space=pltpu.VMEM), out_shape),
        scratch_shapes=list(scratch),
        cost_estimate=pl.CostEstimate(flops=flops, bytes_accessed=nbytes, transcendentals=0),
        compiler_params=pltpu.CompilerParams(vmem_limit_bytes=vmem),
    )(*args)


def sds(*shape, dtype=BF):
    return jax.ShapeDtypeStruct(shape, dtype)


def pack(len_ref, q_hbm, k_hbm, v_hbm, sk_hbm, sv_hbm, pos_hbm, tile_ref, out_ref, k_ref, v_ref, pos_ref, sems):
    meta = 2 * HALF
    copies = [
        pltpu.make_async_copy(k_hbm, k_ref, sems.at[0]),
        pltpu.make_async_copy(v_hbm, v_ref, sems.at[1]),
        pltpu.make_async_copy(sk_hbm, out_ref.at[meta : meta + 32], sems.at[2]),
        pltpu.make_async_copy(sv_hbm, out_ref.at[meta + 32 : meta + 64], sems.at[3]),
        pltpu.make_async_copy(q_hbm, tile_ref.at[:, : GROUP * HD], sems.at[4]),
    ]
    pos_copy = pltpu.make_async_copy(pos_hbm, pos_ref, sems.at[5])
    pos_copy.start()
    for copy in copies:
        copy.start()
    pos_copy.wait()
    pos = jnp.broadcast_to(pos_ref[...], (32, 32))
    row = lax.broadcasted_iota(jnp.int32, (32, 32), 0)
    col = lax.broadcasted_iota(jnp.int32, (32, 32), 1)
    column = jnp.sum(jnp.where(row == col, pos, 0), axis=1, keepdims=True)
    lane = lax.broadcasted_iota(jnp.int32, (32, 128), 1)
    numbers = jnp.where(lane == 0, column // 32, jnp.where(lane == 1, column % 32, 0))
    tile_ref[:, GROUP * HD :] = numbers.astype(F32).astype(BF)
    for copy in copies:
        copy.wait()
    used = len_ref[0]
    first = jnp.broadcast_to(k_ref[0:1, :].astype(F32), (HD, HD))
    for half in range(2):
        base = half * (2 * HALF + META)
        for block in range(HALF // HD):
            start = half * HALF + block * HD
            seen = lax.broadcasted_iota(jnp.int32, (HD, HD), 0) + start < used
            keys = jnp.where(seen, k_ref[start : start + HD, :].astype(F32), first)
            out_ref[base + block * HD : base + (block + 1) * HD, :] = keys.astype(BF)
            values = jnp.where(seen, v_ref[start : start + HD, :].astype(F32), 0.0)
            out_ref[base + HALF + block * HD : base + HALF + (block + 1) * HD, :] = values.astype(BF)
    pos = jnp.concatenate([pos_ref[...], jnp.zeros((1, 96), jnp.int32)], axis=1)
    pos = jnp.broadcast_to(pos, (64, HD))
    row = lax.broadcasted_iota(jnp.int32, (64, HD), 0)
    lane = lax.broadcasted_iota(jnp.int32, (64, HD), 1)
    extent = jnp.where(lane == 0, used // 32, jnp.where(lane == 1, used % 32, 0))
    numbers = jnp.where(row == 0, pos // 32, jnp.where(row == 1, pos % 32, jnp.where(row == 2, extent, 0)))
    out_ref[meta + 64 : meta + 128, :] = numbers.astype(F32).astype(BF)


def pair(a_ref, b_ref, out_ref):
    out_ref[0:32, :] = a_ref[...]
    out_ref[32:64, :] = b_ref[...]


def attend(layout, span, n_carry, picks, unit, n_tiles, n_idle, has_weight, *refs):
    last, first = picks is not None, n_carry == 0
    refs = list(refs)
    take = lambda n: [refs.pop(0) for _ in range(n)]
    tiles, kvs, spans = take(n_tiles), take(len(layout)), take(3 if span else 0)
    accs_in, sts_in = take(n_carry), take(n_carry)
    w_in = take(int(has_weight))
    take(n_idle)
    if last:
        outs = take(len(picks))
    else:
        acc_out, st_out = take(2)
        for kv in kvs:
            refs.pop(0)[...] = kv[2 * HALF : 2 * HALF + META, :]
    for w in w_in:
        refs.pop(0)[...] = w[...]
    open_ref, score_a, score_b = refs
    rows = 64 * n_tiles

    def widen(shift, width):
        return shift if shift.shape[1] == 1 else jnp.concatenate([shift] * (width // HD), axis=1)

    def carried(parts, cols):
        if not last:
            return jnp.concatenate([ref[:, cols] for ref in parts], axis=0)
        return jnp.concatenate([parts[0][64 * i : 64 * (i + 1), cols] for i in picks], axis=0)

    blocks = []
    at = 0
    for i, (holder, pieces) in enumerate(layout):
        numbers = kvs[holder][2 * HALF + 64 : 2 * HALF + 80, :].astype(F32)
        used = numbers[2:3, 0:1] * 32.0 + numbers[2:3, 1:2]
        for start, cache_row in pieces:
            index = lax.broadcasted_iota(jnp.int32, (HALF, HD), 0) + cache_row
            open_ref[at : at + HALF, :] = jnp.where(index.astype(F32) < used, 1.0, 0.0).astype(BF)
            blocks += [(at + c, 256, kvs[i], start + c) for c in range(0, HALF, 256)]
            at += HALF
    if span:
        near = [s[...] for s in spans] + [kvs[0][2 * HALF : 2 * HALF + META, :]]
        span_keys = jnp.concatenate([s[0:32, :] for s in near], axis=0)
        span_values = jnp.concatenate([s[32:64, :] for s in near], axis=0)
        open_ref[at : at + HD, :] = jnp.ones((HD, HD), BF)
        near = [s[64:80, :].astype(F32) for s in near]
        key_pos = jnp.concatenate([s[0:1, 0:32] * 32.0 + s[1:2, 0:32] for s in near], axis=1)
        numbers = jnp.concatenate([t[:, GROUP * HD :] for t in tiles], axis=0).astype(F32)
        query_pos = numbers[:, 0:1] * 32.0 + numbers[:, 1:2]
        seen = key_pos <= query_pos
        blocks.append((at, HD, None, 0))
    if span:
        seen = jnp.concatenate([seen] * unit, axis=0)
    lane = lax.broadcasted_iota(jnp.int32, (rows, HD), 1)
    new_st = jnp.zeros((rows, HD), F32)
    peak = None
    for step in range(GROUP // unit + 1):
        mine, previous = (score_a, score_b) if step % 2 == 0 else (score_b, score_a)
        heads = range(step * unit, (step + 1) * unit)
        if step < GROUP // unit:
            query = jnp.concatenate([t[:, h * HD : (h + 1) * HD] for h in heads for t in tiles], axis=0)
            query = query.astype(F32) * LOG2_SCALE
            high = query.astype(BF)
            query = jnp.concatenate([high, (query - high.astype(F32)).astype(BF)], axis=1)
        top = None
        acc = None
        for c, width, kv, row in blocks:
            if step < GROUP // unit:
                keys = span_keys if kv is None else kv[row : row + width, :]
                keys = jnp.concatenate([keys, keys], axis=1)
                s = lax.dot_general(query, keys, (((1,), (1,)), ((), ())), preferred_element_type=F32)
                if kv is None:
                    s = jnp.where(seen, s, NEG)
                mine[:, c : c + width] = s
                for i in range(0, width, HD):
                    top = s[:, i : i + HD] if top is None else jnp.maximum(top, s[:, i : i + HD])
            if step > 0:
                p = jnp.exp2(previous[:, c : c + width] - widen(peak, width)).astype(BF)
                values = span_values if kv is None else kv[row + HALF : row + HALF + width, :]
                values = jnp.concatenate([values, open_ref[c : c + width, :]], axis=1)
                term = jnp.dot(p, values, preferred_element_type=F32)
                acc = term if acc is None else acc + term
        if step > 0:
            for u in range(unit):
                h = (step - 1) * unit + u
                part = slice(u * rows, (u + 1) * rows)
                cols = slice(h * HD, (h + 1) * HD)
                wide = slice(2 * h * HD, 2 * (h + 1) * HD)
                total, shift = acc[part, :], jnp.broadcast_to(peak[part, :], (rows, HD))
                if not first:
                    rescale = jnp.exp2(carried(sts_in, cols) - shift)
                    total = total + carried(accs_in, wide) * jnp.concatenate([rescale, rescale], axis=1)
                if last:
                    new_st = jnp.where(lane == h, shift, new_st)
                    new_st = jnp.where(lane == GROUP + h, total[:, HD:], new_st)
                    for i, out in enumerate(outs):
                        out[:, cols] = total[64 * i : 64 * (i + 1), :HD].astype(BF)
                else:
                    acc_out[:, wide] = total
                    st_out[:, cols] = shift
        if step < GROUP // unit:
            peak = jnp.max(top, axis=1, keepdims=True).astype(BF).astype(F32)
            if not first:
                before = [carried(sts_in, slice(h * HD, h * HD + (HD if last else 1))) for h in heads]
                peak = jnp.maximum(peak, jnp.concatenate(before, axis=0))
    if last:
        high = new_st.astype(BF).astype(F32)
        low = pltpu.roll(new_st - high, GROUP, 1)
        packed = jnp.where(lane < 2 * GROUP, high, jnp.where(lane < 3 * GROUP, low, 0.0)).astype(BF)
        for i, out in enumerate(outs):
            out[:, GROUP * HD :] = packed[64 * i : 64 * (i + 1), :]


def attend_call(tiles, kvs, layout, spans=(), accs=(), sts=(), weight=None, idle=(), picks=None, unit=1):
    n_keys = HALF * sum(len(p) for _, p in layout) + (HD if spans else 0)
    rows = 64 * len(tiles)
    handed = [] if weight is None else [weight]
    args = list(tiles) + list(kvs) + list(spans) + list(accs) + list(sts) + handed + list(idle)
    if picks is not None:
        out = [sds(64, QW) for _ in picks]
    else:
        out = [sds(rows, 2 * GROUP * HD, dtype=F32), sds(rows, GROUP * HD, dtype=F32)] + [sds(META, HD) for _ in kvs]
    out += [sds(*w.shape) for w in handed]
    return call(
        functools.partial(
            attend, layout, bool(spans), len(accs), picks, unit, len(tiles), len(idle), weight is not None
        ),
        out,
        args,
        scratch=[
            pltpu.VMEM((n_keys, HD), BF),
            pltpu.VMEM((rows * unit, n_keys), F32),
            pltpu.VMEM((rows * unit, n_keys), F32),
        ],
        idle=range(len(args) - len(idle), len(args)),
        flops=rows * GROUP * n_keys * HD * 8,
        nbytes=4 << 20,
        vmem=(rows * unit * n_keys * 8) + (8 << 20),
    )


def join(messages, final):
    stats = [m[:, GROUP * HD :].astype(F32) for m in messages]
    sums, peaks, weights = [], [], []
    for h in range(GROUP):
        each = [s[:, h : h + 1] for s in stats]
        peak = functools.reduce(jnp.maximum, each)
        scales = [jnp.exp2(p - peak) for p in each]
        weight = sum(
            (s[:, GROUP + h : GROUP + h + 1] + s[:, 2 * GROUP + h : 2 * GROUP + h + 1]) * c
            for s, c in zip(stats, scales)
        )
        total = sum(m[:, h * HD : (h + 1) * HD].astype(F32) * c for m, c in zip(messages, scales))
        sums.append(total / weight if final else total)
        peaks.append(peak)
        weights.append(weight)
    return sums, peaks, weights


def join_x(a_ref, b_ref, c_ref, d_ref, out_ref):
    messages = [r[...] for r in (a_ref, b_ref, c_ref, d_ref)]
    sums, peaks, weights = join(messages, False)
    lane = lax.broadcasted_iota(jnp.int32, (64, HD), 1)
    numbers = jnp.zeros((64, HD), F32)
    for h in range(GROUP):
        out_ref[:, h * HD : (h + 1) * HD] = sums[h].astype(BF)
        high = weights[h].astype(BF).astype(F32)
        numbers = jnp.where(lane == h, peaks[h], numbers)
        numbers = jnp.where(lane == GROUP + h, high, numbers)
        numbers = jnp.where(lane == 2 * GROUP + h, weights[h] - high, numbers)
    out_ref[:, GROUP * HD :] = numbers.astype(BF)


def hand(w_ref, _, *outs):
    depth = w_ref.shape[0] // len(outs)
    for i, out in enumerate(outs):
        out[...] = w_ref[i * depth : (i + 1) * depth, :]


def join_z(own_ref, other_ref, out_ref):
    other = jnp.concatenate([other_ref[32:64, :], other_ref[0:32, :]], axis=0)
    sums, _, _ = join([own_ref[...], other], True)
    for h in range(GROUP):
        out_ref[:, h * HD : (h + 1) * HD] = sums[h].astype(BF)


def project(a0, a1, a2, a3, w0, w1, w2, *refs):
    *w3, keep_ref, send_ref, rows_ref = refs
    index, core = lax.axis_index("ctx"), lax.rem(lax.axis_index("head"), 2)
    z, y = index // 16, lax.rem(index // 4, 4)
    for a, dy in zip((a0, a1, a2, a3), (0, 1, 3, 2)):
        there = lax.rem(y + dy, 4)
        other = lax.rem(there + core, 2)
        for part in range(2):
            z_there = z if part == 0 else 1 - z
            slot = pl.multiple_of((other * 4 + z_there * 2 + there // 2) * 32, 32)
            rows_ref[pl.ds(slot, 32), :] = a[32 * part : 32 * (part + 1), :]
    for i, ws in enumerate(((w0,), (w1,), (w2,), w3)):
        depth = 1024 // len(ws)
        out = sum(
            jnp.dot(rows_ref[:, k * depth : (k + 1) * depth], w[...], preferred_element_type=F32)
            for k, w in enumerate(ws)
        ).astype(BF)
        keep_ref[:, i * 256 : (i + 1) * 256] = out[:128, :]
        send_ref[:, i * 256 : (i + 1) * 256] = out[128:, :]


def add_cores(keep_ref, got_ref, *outs):
    z_lo = lax.axis_index("head") // 2
    for half, columns in enumerate(((3, 1), (2, 0))):
        for k in range(4):
            slot = pl.multiple_of((z_lo ^ k) * 32, 32)
            for j, c in enumerate(columns):
                cols = slice(c * 256, (c + 1) * 256)
                total = keep_ref[pl.ds(slot, 32), cols].astype(F32) + got_ref[pl.ds(slot, 32), cols].astype(F32)
                outs[half * 4 + k][:, j * 256 : (j + 1) * 256] = total.astype(BF)


def add_z(a_ref, b_ref, c_ref, d_ref, *rest):
    *_, o0, o1 = rest
    total = sum(r[...].astype(F32) for r in (a_ref, b_ref, c_ref, d_ref)).astype(BF)
    o0[...] = total[:, :256]
    o1[...] = total[:, 256:]


def place(a_ref, b_ref, c_ref, d_ref, out_ref):
    x = lax.rem(lax.axis_index("ctx"), 4)
    for dx, r in zip((0, 1, 3, 2), (a_ref, b_ref, c_ref, d_ref)):
        slot = pl.multiple_of(lax.rem(x + dx, 4) * 32, 32)
        out_ref[pl.ds(slot, 32), :] = r[...]


def ctx_shift(dz, dy, dx):
    pairs = []
    for c in range(32):
        z, y, x = c // 16, (c // 4) % 4, c % 4
        pairs.append((c, ((z + dz) % 2) * 16 + ((y + dy) % 4) * 4 + (x + dx) % 4))
    return pairs


def fetch(value, dz=0, dy=0, dx=0):
    return lax.ppermute(value, "ctx", ctx_shift(-dz, -dy, -dx))


def shards(queries, cache_keys, cache_values, span_keys, span_values, prefix_len, positions, out_weight):
    pos_row = positions.reshape(1, 32)
    tile, kv = call(
        pack,
        [sds(32, QW), sds(4 * HALF + META, HD)],
        [prefix_len, queries, cache_keys, cache_values, span_keys, span_values, pos_row],
        scratch=[
            pltpu.VMEM((2 * HALF, HD), BF),
            pltpu.VMEM((2 * HALF, HD), BF),
            pltpu.VMEM((1, 32), jnp.int32),
            pltpu.SemaphoreType.DMA((6,)),
        ],
        smem=(0,),
        raw=(1, 2, 3, 4, 5, 6),
    )
    kv_up = fetch(kv, dy=1)
    kv_down = fetch(kv, dy=-1)
    own = call(pair, sds(64, QW), [tile, fetch(tile, dz=1)])
    far = fetch(own, dx=2)
    tiles = [own, fetch(own, dx=1), fetch(own, dx=-1), far]

    cut = 2 * HALF + META
    whole = [(0, 0), (cut, HALF)]
    acc_a, st_a, span, weight = attend_call(tiles[:1], [kv], [(0, whole)], weight=out_weight, unit=4)
    w_up, w_down = fetch(weight, dx=1), fetch(weight, dx=-1)
    acc_b, st_b, _ = attend_call(tiles[1:], [kv], [(0, whole)], unit=4)
    far_a = fetch(kv_up[:cut], dy=1)
    far_b = fetch(kv_down[cut:], dy=-1)
    acc, st, *spans = attend_call(
        tiles, [kv_up, kv_down], [(0, whole), (1, whole)], accs=[acc_a, acc_b], sts=[st_a, st_b], unit=2
    )

    def finish(picks, unit, idle=(), weight=None):
        return attend_call(
            [tiles[i] for i in picks],
            [far_a, far_b],
            [(0, [(0, 0)]), (0, [(0, HALF)])],
            spans=[span] + spans,
            accs=[acc],
            sts=[st],
            weight=weight,
            idle=idle,
            picks=picks,
            unit=unit,
        )

    (part_3,) = finish((3,), 4)
    got_3 = fetch(part_3, dx=-2)
    part_1, part_2 = finish((1, 2), 2, idle=[part_3, w_up, w_down])
    got_1, got_2 = fetch(part_1, dx=-1), fetch(part_2, dx=1)
    (part_0,) = finish((0,), 4, idle=[got_3])
    joined = call(join_x, sds(64, QW), [part_0, got_1, got_2, got_3])
    halves = call(hand, [sds(512, 256)] * 2, [weight, joined], idle=(1,))
    weights = [out_weight, w_up, w_down] + [fetch(h, dx=2) for h in halves]
    attended = call(join_z, sds(64, GROUP * HD), [joined, fetch(joined, dz=1)])
    rows = [attended] + [fetch(attended, dy=d) for d in (1, -1, 2)]
    keep, send = call(
        project,
        [sds(128, 1024), sds(128, 1024)],
        rows + weights,
        scratch=[pltpu.VMEM((256, 1024), BF)],
        flops=2 * 256 * 1024 * 1024,
        nbytes=4 << 20,
    )
    got = lax.ppermute(send, "head", [(h, h ^ 1) for h in range(8)])
    halves = call(add_cores, [sds(32, 512)] * 8, [keep, got])
    summed = []
    for part in (halves[:4], halves[4:]):
        others = [lax.ppermute(o, "head", [(h, h ^ (2 * k)) for h in range(8)]) for k, o in zip((1, 2, 3), part[1:])]
        summed.append([part[0]] + others)
    two, one = call(add_z, [sds(32, 256)] * 2, summed[0])
    two, one = fetch(two, dx=-2), fetch(one, dx=-1)
    other, own = call(add_z, [sds(32, 256)] * 2, summed[1])
    pieces = [own, fetch(other, dx=1), one, two]
    return call(place, sds(128, 256), pieces)


def solution(mesh):
    return jax.shard_map(
        shards,
        mesh=mesh,
        in_specs=(
            P("ctx", "head"),
            P("ctx", "head"),
            P("ctx", "head"),
            P("ctx", "head"),
            P("ctx", "head"),
            P("ctx"),
            P("ctx"),
            P("head", "ctx"),
        ),
        out_specs=P("head", "ctx"),
        check_vma=False,
    )
```

```python
import functools
import math

import jax
import jax.numpy as jnp
from jax import lax
from jax.experimental import pallas as pl
from jax.experimental.pallas import tpu as pltpu
from jax.sharding import PartitionSpec as P

BF = jnp.bfloat16
F32 = jnp.float32
HD = 128
GROUP = 8
HALF = 1024
META = 128
QW = GROUP * HD + 128
LOG2_SCALE = math.log2(math.e) / math.sqrt(HD)
NEG = -1e30


def call(body, out_shape, args, scratch=(), smem=(), idle=(), raw=(), flops=0, nbytes=0, vmem=8 << 20):
    args, specs = list(args), []
    for i in range(len(args)):
        if i in smem:
            specs.append(pl.BlockSpec(memory_space=pltpu.SMEM))
        elif i in raw:
            specs.append(pl.BlockSpec(memory_space=pltpu.HBM))
            args[i] = pltpu.with_memory_space_constraint(args[i], pltpu.HBM)
        elif i in idle:
            specs.append(pl.BlockSpec(memory_space=pl.ANY))
        else:
            specs.append(pl.BlockSpec(memory_space=pltpu.VMEM))
    return pl.pallas_call(
        body,
        out_shape=out_shape,
        in_specs=specs,
        out_specs=jax.tree.map(lambda _: pl.BlockSpec(memory_space=pltpu.VMEM), out_shape),
        scratch_shapes=list(scratch),
        cost_estimate=pl.CostEstimate(flops=flops, bytes_accessed=nbytes, transcendentals=0),
        compiler_params=pltpu.CompilerParams(vmem_limit_bytes=vmem),
    )(*args)


def sds(*shape, dtype=BF):
    return jax.ShapeDtypeStruct(shape, dtype)


def pack(len_ref, q_hbm, k_hbm, v_hbm, sk_hbm, sv_hbm, pos_hbm, tile_ref, out_ref, k_ref, v_ref, pos_ref, sems):
    meta = 2 * HALF
    copies = [
        pltpu.make_async_copy(k_hbm, k_ref, sems.at[0]),
        pltpu.make_async_copy(v_hbm, v_ref, sems.at[1]),
        pltpu.make_async_copy(sk_hbm, out_ref.at[meta : meta + 32], sems.at[2]),
        pltpu.make_async_copy(sv_hbm, out_ref.at[meta + 32 : meta + 64], sems.at[3]),
        pltpu.make_async_copy(q_hbm, tile_ref.at[:, : GROUP * HD], sems.at[4]),
    ]
    pos_copy = pltpu.make_async_copy(pos_hbm, pos_ref, sems.at[5])
    pos_copy.start()
    for copy in copies:
        copy.start()
    pos_copy.wait()
    pos = jnp.broadcast_to(pos_ref[...], (32, 32))
    row = lax.broadcasted_iota(jnp.int32, (32, 32), 0)
    col = lax.broadcasted_iota(jnp.int32, (32, 32), 1)
    column = jnp.sum(jnp.where(row == col, pos, 0), axis=1, keepdims=True)
    lane = lax.broadcasted_iota(jnp.int32, (32, 128), 1)
    numbers = jnp.where(lane == 0, column // 32, jnp.where(lane == 1, column % 32, 0))
    tile_ref[:, GROUP * HD :] = numbers.astype(F32).astype(BF)
    for copy in copies:
        copy.wait()
    used = len_ref[0]
    first = jnp.broadcast_to(k_ref[0:1, :].astype(F32), (HD, HD))
    for half in range(2):
        base = half * (2 * HALF + META)
        for block in range(HALF // HD):
            start = half * HALF + block * HD
            seen = lax.broadcasted_iota(jnp.int32, (HD, HD), 0) + start < used
            keys = jnp.where(seen, k_ref[start : start + HD, :].astype(F32), first)
            out_ref[base + block * HD : base + (block + 1) * HD, :] = keys.astype(BF)
            values = jnp.where(seen, v_ref[start : start + HD, :].astype(F32), 0.0)
            out_ref[base + HALF + block * HD : base + HALF + (block + 1) * HD, :] = values.astype(BF)
    pos = jnp.concatenate([pos_ref[...], jnp.zeros((1, 96), jnp.int32)], axis=1)
    pos = jnp.broadcast_to(pos, (64, HD))
    row = lax.broadcasted_iota(jnp.int32, (64, HD), 0)
    lane = lax.broadcasted_iota(jnp.int32, (64, HD), 1)
    extent = jnp.where(lane == 0, used // 32, jnp.where(lane == 1, used % 32, 0))
    numbers = jnp.where(row == 0, pos // 32, jnp.where(row == 1, pos % 32, jnp.where(row == 2, extent, 0)))
    out_ref[meta + 64 : meta + 128, :] = numbers.astype(F32).astype(BF)


def pair(a_ref, b_ref, out_ref):
    out_ref[0:32, :] = a_ref[...]
    out_ref[32:64, :] = b_ref[...]


def attend(layout, span, n_carry, picks, unit, n_tiles, n_idle, has_weight, *refs):
    last, first = picks is not None, n_carry == 0
    refs = list(refs)
    take = lambda n: [refs.pop(0) for _ in range(n)]
    tiles, kvs, spans = take(n_tiles), take(len(layout)), take(3 if span else 0)
    accs_in, sts_in = take(n_carry), take(n_carry)
    w_in = take(int(has_weight))
    take(n_idle)
    if last:
        outs = take(len(picks))
    else:
        acc_out, st_out = take(2)
        for kv in kvs:
            refs.pop(0)[...] = kv[2 * HALF : 2 * HALF + META, :]
    for w in w_in:
        refs.pop(0)[...] = w[...]
    open_ref, score_a, score_b = refs
    rows = 64 * n_tiles

    def widen(shift, width):
        return shift if shift.shape[1] == 1 else jnp.concatenate([shift] * (width // HD), axis=1)

    def carried(parts, cols):
        if not last:
            return jnp.concatenate([ref[:, cols] for ref in parts], axis=0)
        return jnp.concatenate([parts[0][64 * i : 64 * (i + 1), cols] for i in picks], axis=0)

    blocks = []
    at = 0
    for i, (holder, pieces) in enumerate(layout):
        numbers = kvs[holder][2 * HALF + 64 : 2 * HALF + 80, :].astype(F32)
        used = numbers[2:3, 0:1] * 32.0 + numbers[2:3, 1:2]
        for start, cache_row in pieces:
            index = lax.broadcasted_iota(jnp.int32, (HALF, HD), 0) + cache_row
            open_ref[at : at + HALF, :] = jnp.where(index.astype(F32) < used, 1.0, 0.0).astype(BF)
            blocks += [(at + c, 256, kvs[i], start + c) for c in range(0, HALF, 256)]
            at += HALF
    if span:
        near = [s[...] for s in spans] + [kvs[0][2 * HALF : 2 * HALF + META, :]]
        span_keys = jnp.concatenate([s[0:32, :] for s in near], axis=0)
        span_values = jnp.concatenate([s[32:64, :] for s in near], axis=0)
        open_ref[at : at + HD, :] = jnp.ones((HD, HD), BF)
        near = [s[64:80, :].astype(F32) for s in near]
        key_pos = jnp.concatenate([s[0:1, 0:32] * 32.0 + s[1:2, 0:32] for s in near], axis=1)
        numbers = jnp.concatenate([t[:, GROUP * HD :] for t in tiles], axis=0).astype(F32)
        query_pos = numbers[:, 0:1] * 32.0 + numbers[:, 1:2]
        seen = key_pos <= query_pos
        blocks.append((at, HD, None, 0))
    if span:
        seen = jnp.concatenate([seen] * unit, axis=0)
    lane = lax.broadcasted_iota(jnp.int32, (rows, HD), 1)
    new_st = jnp.zeros((rows, HD), F32)
    peak = None
    for step in range(GROUP // unit + 1):
        mine, previous = (score_a, score_b) if step % 2 == 0 else (score_b, score_a)
        heads = range(step * unit, (step + 1) * unit)
        if step < GROUP // unit:
            query = jnp.concatenate([t[:, h * HD : (h + 1) * HD] for h in heads for t in tiles], axis=0)
            query = query.astype(F32) * LOG2_SCALE
            high = query.astype(BF)
            query = jnp.concatenate([high, (query - high.astype(F32)).astype(BF)], axis=1)
        top = None
        acc = None
        for c, width, kv, row in blocks:
            if step < GROUP // unit:
                keys = span_keys if kv is None else kv[row : row + width, :]
                keys = jnp.concatenate([keys, keys], axis=1)
                s = lax.dot_general(query, keys, (((1,), (1,)), ((), ())), preferred_element_type=F32)
                if kv is None:
                    s = jnp.where(seen, s, NEG)
                mine[:, c : c + width] = s
                for i in range(0, width, HD):
                    top = s[:, i : i + HD] if top is None else jnp.maximum(top, s[:, i : i + HD])
            if step > 0:
                p = jnp.exp2(previous[:, c : c + width] - widen(peak, width)).astype(BF)
                values = span_values if kv is None else kv[row + HALF : row + HALF + width, :]
                values = jnp.concatenate([values, open_ref[c : c + width, :]], axis=1)
                term = jnp.dot(p, values, preferred_element_type=F32)
                acc = term if acc is None else acc + term
        if step > 0:
            for u in range(unit):
                h = (step - 1) * unit + u
                part = slice(u * rows, (u + 1) * rows)
                cols = slice(h * HD, (h + 1) * HD)
                wide = slice(2 * h * HD, 2 * (h + 1) * HD)
                total, shift = acc[part, :], jnp.broadcast_to(peak[part, :], (rows, HD))
                if not first:
                    rescale = jnp.exp2(carried(sts_in, cols) - shift)
                    total = total + carried(accs_in, wide) * jnp.concatenate([rescale, rescale], axis=1)
                if last:
                    new_st = jnp.where(lane == h, shift, new_st)
                    new_st = jnp.where(lane == GROUP + h, total[:, HD:], new_st)
                    for i, out in enumerate(outs):
                        out[:, cols] = total[64 * i : 64 * (i + 1), :HD].astype(BF)
                else:
                    acc_out[:, wide] = total
                    st_out[:, cols] = shift
        if step < GROUP // unit:
            peak = jnp.max(top, axis=1, keepdims=True).astype(BF).astype(F32)
            if not first:
                before = [carried(sts_in, slice(h * HD, h * HD + (HD if last else 1))) for h in heads]
                peak = jnp.maximum(peak, jnp.concatenate(before, axis=0))
    if last:
        high = new_st.astype(BF).astype(F32)
        low = pltpu.roll(new_st - high, GROUP, 1)
        packed = jnp.where(lane < 2 * GROUP, high, jnp.where(lane < 3 * GROUP, low, 0.0)).astype(BF)
        for i, out in enumerate(outs):
            out[:, GROUP * HD :] = packed[64 * i : 64 * (i + 1), :]


def attend_call(tiles, kvs, layout, spans=(), accs=(), sts=(), weight=None, idle=(), picks=None, unit=1):
    n_keys = HALF * sum(len(p) for _, p in layout) + (HD if spans else 0)
    rows = 64 * len(tiles)
    handed = [] if weight is None else [weight]
    args = list(tiles) + list(kvs) + list(spans) + list(accs) + list(sts) + handed + list(idle)
    if picks is not None:
        out = [sds(64, QW) for _ in picks]
    else:
        out = [sds(rows, 2 * GROUP * HD, dtype=F32), sds(rows, GROUP * HD, dtype=F32)] + [sds(META, HD) for _ in kvs]
    out += [sds(*w.shape) for w in handed]
    return call(
        functools.partial(
            attend, layout, bool(spans), len(accs), picks, unit, len(tiles), len(idle), weight is not None
        ),
        out,
        args,
        scratch=[
            pltpu.VMEM((n_keys, HD), BF),
            pltpu.VMEM((rows * unit, n_keys), F32),
            pltpu.VMEM((rows * unit, n_keys), F32),
        ],
        idle=range(len(args) - len(idle), len(args)),
        flops=rows * GROUP * n_keys * HD * 8,
        nbytes=4 << 20,
        vmem=(rows * unit * n_keys * 8) + (8 << 20),
    )


def join(messages, final):
    stats = [m[:, GROUP * HD :].astype(F32) for m in messages]
    sums, peaks, weights = [], [], []
    for h in range(GROUP):
        each = [s[:, h : h + 1] for s in stats]
        peak = functools.reduce(jnp.maximum, each)
        scales = [jnp.exp2(p - peak) for p in each]
        weight = sum(
            (s[:, GROUP + h : GROUP + h + 1] + s[:, 2 * GROUP + h : 2 * GROUP + h + 1]) * c
            for s, c in zip(stats, scales)
        )
        total = sum(m[:, h * HD : (h + 1) * HD].astype(F32) * c for m, c in zip(messages, scales))
        sums.append(total / weight if final else total)
        peaks.append(peak)
        weights.append(weight)
    return sums, peaks, weights


def join_x(a_ref, b_ref, c_ref, d_ref, out_ref):
    messages = [r[...] for r in (a_ref, b_ref, c_ref, d_ref)]
    sums, peaks, weights = join(messages, False)
    lane = lax.broadcasted_iota(jnp.int32, (64, HD), 1)
    numbers = jnp.zeros((64, HD), F32)
    for h in range(GROUP):
        out_ref[:, h * HD : (h + 1) * HD] = sums[h].astype(BF)
        high = weights[h].astype(BF).astype(F32)
        numbers = jnp.where(lane == h, peaks[h], numbers)
        numbers = jnp.where(lane == GROUP + h, high, numbers)
        numbers = jnp.where(lane == 2 * GROUP + h, weights[h] - high, numbers)
    out_ref[:, GROUP * HD :] = numbers.astype(BF)


def hand(w_ref, _, *outs):
    depth = w_ref.shape[0] // len(outs)
    for i, out in enumerate(outs):
        out[...] = w_ref[i * depth : (i + 1) * depth, :]


def join_z(own_ref, other_ref, out_ref):
    other = jnp.concatenate([other_ref[32:64, :], other_ref[0:32, :]], axis=0)
    sums, _, _ = join([own_ref[...], other], True)
    for h in range(GROUP):
        out_ref[:, h * HD : (h + 1) * HD] = sums[h].astype(BF)


def project(depths, a0, a1, a2, a3, *refs):
    *ws, keep_ref, send_ref, rows_ref = refs
    index, core = lax.axis_index("ctx"), lax.rem(lax.axis_index("head"), 2)
    z, y = index // 16, lax.rem(index // 4, 4)
    for a, dy in zip((a0, a1, a2, a3), (0, 1, 3, 2)):
        there = lax.rem(y + dy, 4)
        other = lax.rem(there + core, 2)
        for part in range(2):
            z_there = z if part == 0 else 1 - z
            slot = pl.multiple_of((other * 4 + z_there * 2 + there // 2) * 32, 32)
            rows_ref[pl.ds(slot, 32), :] = a[32 * part : 32 * (part + 1), :]
    at = 0
    for i, count in enumerate(depths):
        depth = 1024 // count
        out = sum(
            jnp.dot(rows_ref[:, k * depth : (k + 1) * depth], ws[at + k][...], preferred_element_type=F32)
            for k in range(count)
        ).astype(BF)
        at += count
        keep_ref[:, i * 256 : (i + 1) * 256] = out[:128, :]
        send_ref[:, i * 256 : (i + 1) * 256] = out[128:, :]


def add_cores(keep_ref, got_ref, *outs):
    z_lo = lax.axis_index("head") // 2
    for k, out in enumerate(outs):
        slot = pl.multiple_of((z_lo ^ k) * 32, 32)
        out[...] = (keep_ref[pl.ds(slot, 32), :].astype(F32) + got_ref[pl.ds(slot, 32), :].astype(F32)).astype(BF)


def add_z(a_ref, b_ref, c_ref, d_ref, *rest):
    *_, o0, o1 = rest
    total = sum(r[...].astype(F32) for r in (a_ref, b_ref, c_ref, d_ref)).astype(BF)
    o0[...] = total[:, :256]
    o1[...] = total[:, 256:]


def place(a_ref, b_ref, c_ref, d_ref, out_ref):
    x = lax.rem(lax.axis_index("ctx"), 4)
    for dx, r in zip((0, 1, 3, 2), (a_ref, b_ref, c_ref, d_ref)):
        slot = pl.multiple_of(lax.rem(x + dx, 4) * 32, 32)
        out_ref[pl.ds(slot, 32), :] = r[...]


def ctx_shift(dz, dy, dx):
    pairs = []
    for c in range(32):
        z, y, x = c // 16, (c // 4) % 4, c % 4
        pairs.append((c, ((z + dz) % 2) * 16 + ((y + dy) % 4) * 4 + (x + dx) % 4))
    return pairs


def fetch(value, dz=0, dy=0, dx=0):
    return lax.ppermute(value, "ctx", ctx_shift(-dz, -dy, -dx))


def shards(queries, cache_keys, cache_values, span_keys, span_values, prefix_len, positions, out_weight):
    pos_row = positions.reshape(1, 32)
    tile, kv = call(
        pack,
        [sds(32, QW), sds(4 * HALF + META, HD)],
        [prefix_len, queries, cache_keys, cache_values, span_keys, span_values, pos_row],
        scratch=[
            pltpu.VMEM((2 * HALF, HD), BF),
            pltpu.VMEM((2 * HALF, HD), BF),
            pltpu.VMEM((1, 32), jnp.int32),
            pltpu.SemaphoreType.DMA((6,)),
        ],
        smem=(0,),
        raw=(1, 2, 3, 4, 5, 6),
    )
    kv_up = fetch(kv, dy=1)
    kv_down = fetch(kv, dy=-1)
    own = call(pair, sds(64, QW), [tile, fetch(tile, dz=1)])
    far = fetch(own, dx=2)
    tiles = [own, fetch(own, dx=1), fetch(own, dx=-1), far]

    cut = 2 * HALF + META
    whole = [(0, 0), (cut, HALF)]
    acc_a, st_a, span, weight = attend_call(tiles[:1], [kv], [(0, whole)], weight=out_weight, unit=4)
    w_up, w_down = fetch(weight, dx=1), fetch(weight, dx=-1)
    acc_b, st_b, _ = attend_call(tiles[1:], [kv], [(0, whole)], unit=4)
    far_a = fetch(kv_up[:cut], dy=1)
    far_b = fetch(kv_down[cut:], dy=-1)
    acc, st, *spans = attend_call(
        tiles, [kv_up, kv_down], [(0, whole), (1, whole)], accs=[acc_a, acc_b], sts=[st_a, st_b], unit=2
    )

    def finish(picks, unit, idle=(), weight=None):
        return attend_call(
            [tiles[i] for i in picks],
            [far_a, far_b],
            [(0, [(0, 0)]), (0, [(0, HALF)])],
            spans=[span] + spans,
            accs=[acc],
            sts=[st],
            weight=weight,
            idle=idle,
            picks=picks,
            unit=unit,
        )

    (part_3,) = finish((3,), 4)
    got_3 = fetch(part_3, dx=-2)
    part_1, part_2 = finish((1, 2), 2, idle=[part_3, w_up, w_down])
    got_1, got_2 = fetch(part_1, dx=-1), fetch(part_2, dx=1)
    (part_0,) = finish((0,), 4, idle=[got_3])
    joined = call(join_x, sds(64, QW), [part_0, got_1, got_2, got_3])
    halves = call(hand, [sds(512, 256)] * 2, [weight, joined], idle=(1,))
    weights = [out_weight, w_up, w_down] + [fetch(h, dx=2) for h in halves]
    attended = call(join_z, sds(64, GROUP * HD), [joined, fetch(joined, dz=1)])
    rows = [attended] + [fetch(attended, dy=d) for d in (1, -1, 2)]
    summed = []
    for blocks in ((weights[3:], weights[1:2]), (weights[2:3], weights[:1])):
        keep, send = call(
            functools.partial(project, [len(w) for w in blocks]),
            [sds(128, 512), sds(128, 512)],
            rows + [w for block in blocks for w in block],
            scratch=[pltpu.VMEM((256, 1024), BF)],
            flops=2 * 256 * 1024 * 512,
            nbytes=2 << 20,
        )
        got = lax.ppermute(send, "head", [(h, h ^ 1) for h in range(8)])
        part = call(add_cores, [sds(32, 512)] * 4, [keep, got])
        others = [lax.ppermute(o, "head", [(h, h ^ (2 * k)) for h in range(8)]) for k, o in zip((1, 2, 3), part[1:])]
        summed.append([part[0]] + others)
    two, one = call(add_z, [sds(32, 256)] * 2, summed[0])
    two, one = fetch(two, dx=-2), fetch(one, dx=-1)
    other, own = call(add_z, [sds(32, 256)] * 2, summed[1])
    pieces = [own, fetch(other, dx=1), one, two]
    return call(place, sds(128, 256), pieces)


def solution(mesh):
    return jax.shard_map(
        shards,
        mesh=mesh,
        in_specs=(
            P("ctx", "head"),
            P("ctx", "head"),
            P("ctx", "head"),
            P("ctx", "head"),
            P("ctx", "head"),
            P("ctx"),
            P("ctx"),
            P("head", "ctx"),
        ),
        out_specs=P("head", "ctx"),
        check_vma=False,
    )
```
